128 devices in a mesh: blk: 32 (over x, y, core), head: 4 (over z).
Axes of the slice: x: 4, y: 4, z: 4, core: 2. Of those that a mesh axis runs over, the one named last changes fastest.
Arguments:
- tokens: bfloat16 [2, 4096, 2048], P(None, 'blk'), may hold values from -6 to 6
- doc_lengths: int32 [2, 8], replicated, may hold values from 1 to 4089, as said below
- norm_gain: bfloat16 [2048], P('blk'), may hold values from 0.5 to 1.5
- w_query: bfloat16 [2048, 256], P('blk', 'head'), may hold values from -0.125 to 0.125
- w_key: bfloat16 [2048, 256], P('blk', 'head'), may hold values from -0.125 to 0.125
- w_value: bfloat16 [2048, 2048], P('blk', 'head'), may hold values from -0.125 to 0.125
- w_out: bfloat16 [2048, 2048], P('head', 'blk'), may hold values from -0.375 to 0.375
- ffn_gain: bfloat16 [2048], P('blk'), may hold values from 0.5 to 1.5
- w_gate: bfloat16 [2048, 5504], P('blk', 'head'), may hold values from -0.125 to 0.125
- w_up: bfloat16 [2048, 5504], P('blk', 'head'), may hold values from -0.125 to 0.125
- w_down: bfloat16 [5504, 2048], P('head', 'blk'), may hold values from -0.078125 to 0.078125
- out_grad: bfloat16 [2, 4096, 2048], P(None, 'blk'), may hold values from -6 to 6
Outputs:
- block_out: bfloat16 [2, 4096, 2048], P(None, 'blk')
- input_grad: bfloat16 [2, 4096, 2048], P(None, 'blk')
- grad_norm_gain: float32 [2048], P('blk')
- grad_w_query: float32 [2048, 256], P('blk', 'head')
- grad_w_key: float32 [2048, 256], P('blk', 'head')
- grad_w_value: float32 [2048, 2048], P('blk', 'head')
- grad_w_out: float32 [2048, 2048], P('head', 'blk')
- grad_ffn_gain: float32 [2048], P('blk')
- grad_w_gate: float32 [2048, 5504], P('blk', 'head')
- grad_w_up: float32 [2048, 5504], P('blk', 'head')
- grad_w_down: float32 [5504, 2048], P('head', 'blk')
- denom_mean: float32 [], replicated
The draws below stay inside these ranges and needn't reach their ends.
Inputs may be any that keep to these rules, and one draw needn't show every extreme that they name: `doc_lengths`: each row holds 8 documents of one position or more whose lengths sum to 4096. In one row, which one drawn from the seed, one document has 4089 positions; it starts within the first 128 positions and ends within the last 128.
All inputs are finite; a program needn't handle non-finite values.
Results may differ from the reference program's by a relative error of at most 0.025.
Values may be sent and summed in bfloat16 or wider, within the bound.
No kernel may reach another device: no remote copies, remote signals or barrier semaphores. Data moves between devices by JAX's collectives and lax.ppermute only.
A program may use at most 128 MiB of HBM per device.

```python
import math
import jax
import jax.numpy as jnp
from jax import lax

D = 2048
HEADS = 16
FDIM = 16
FF = 5504
ROWS = 2
DOCS = 8
SEQ = 4096


def draw_doc_lengths(key, part):
    key = jax.random.fold_in(key, 7)
    pick_key, rows_key = jax.random.split(key)
    chosen = jax.random.randint(pick_key, (), 0, ROWS)
    row_keys = jax.random.split(rows_key, ROWS)
    candidates = jnp.arange(1, SEQ, dtype=jnp.int32)

    def one_row(row_key, row_number):
        ranking_key, shift_key = jax.random.split(row_key)
        spanning = row_number == chosen
        rest_len = jnp.where(spanning, DOCS - 1, SEQ)
        ranking = jax.random.permutation(ranking_key, SEQ - 1).astype(jnp.int32)
        scores = jnp.where(candidates < rest_len, ranking, -candidates)
        picked = lax.top_k(scores, DOCS - 1)[1].astype(jnp.int32) + 1
        picked = picked.at[DOCS - 2].set(jnp.where(spanning, rest_len, picked[DOCS - 2]).astype(jnp.int32))
        cut_points = jnp.sort(picked)
        bounds = jnp.concatenate([jnp.zeros((1,), jnp.int32), cut_points, jnp.full((1,), SEQ, jnp.int32)])
        lengths = bounds[1:] - bounds[:-1]
        return jnp.roll(lengths, jax.random.randint(shift_key, (), 0, DOCS))
    return jax.vmap(one_row)(row_keys, jnp.arange(ROWS))


def spiked(values, stream_key, source, target, parts, factor):
    def block_of(dim):
        return (jnp.arange(values.shape[dim]) // (values.shape[dim] // parts)).reshape((-1,) + (1,) * (values.ndim - 1 - dim))

    one_side = jax.random.permutation(stream_key, parts)[block_of(target)]
    other_side = (block_of(target) + parts // 2) % parts
    return jnp.where((block_of(source) == one_side) | (block_of(source) == other_side), factor * values, values)


def steps_of(rng, shape, shards, smallest, largest):
    factor_of = 1.0
    for axis_at, parts in shards:
        heights = jax.random.uniform(jax.random.fold_in(jax.random.fold_in(rng, 6), axis_at), (parts,), jnp.float32, smallest / len(shards), largest / len(shards))
        factor_of = factor_of * jnp.repeat(jnp.exp(heights), shape[axis_at] // parts).reshape((-1,) + (1,) * (len(shape) - 1 - axis_at))
    return factor_of


def normal_values(key, extent, spread, reach, cuts=(), kind=jnp.bfloat16):
    entries = spread * jax.random.normal(key, extent, jnp.float32)
    if cuts:
        entries = entries * steps_of(key, extent, cuts, -0.22, 0.18)
    return jnp.clip(entries, -reach, reach).astype(kind)


def noise_with(stream_key, dims, spread, limit, cuts, heavy, held_as=jnp.bfloat16):
    entries = spread * jax.random.normal(stream_key, dims, jnp.float32)
    if cuts:
        entries = entries * steps_of(stream_key, dims, cuts, -0.22, 0.18)
    return jnp.clip(spiked(entries, jax.random.fold_in(stream_key, 3), *heavy), -limit, limit).astype(held_as)


def setup_inputs(seed: int = 0) -> dict:
    key_list = jax.random.split(jax.random.key(seed), 13)
    tokens = normal_values(key_list[0], (ROWS, SEQ, D), 1.0, 6.0, ((1, 32),))
    doc_lengths = draw_doc_lengths(jax.random.fold_in(key_list[12], 71), 0)
    norm_gain = jnp.clip(1.0 + 0.1 * jax.random.normal(key_list[2], (D,), jnp.float32), 0.5, 1.5).astype(jnp.bfloat16)
    w_query = normal_values(key_list[3], (D, HEADS * FDIM), D ** -0.5, 0.125, ((0, 32), (1, 4)))
    w_key = normal_values(key_list[4], (D, HEADS * FDIM), D ** -0.5, 0.125, ((0, 32), (1, 4)))
    w_value = normal_values(key_list[5], (D, D), D ** -0.5, 0.125, ((0, 32), (1, 4)))
    w_out = normal_values(key_list[6], (D, D), (D // 8) ** -0.5, 0.375, ((0, 4), (1, 32)))
    ffn_gain = jnp.clip(1.0 + 0.1 * jax.random.normal(key_list[7], (D,), jnp.float32), 0.5, 1.5).astype(jnp.bfloat16)
    w_gate = normal_values(key_list[8], (D, FF), D ** -0.5, 0.125, ((0, 32), (1, 4)))
    w_up = normal_values(key_list[9], (D, FF), D ** -0.5, 0.125, ((0, 32), (1, 4)))
    w_down = normal_values(key_list[10], (FF, D), FF ** -0.5, 0.078125, ((0, 4), (1, 32)))
    out_grad = noise_with(key_list[11], (ROWS, SEQ, D), 1.0, 6.0, ((1, 32),), (1, 2, 32, 2.75))
    return {"tokens": tokens, "doc_lengths": doc_lengths, "norm_gain": norm_gain, "w_query": w_query, "w_key": w_key, "w_value": w_value, "w_out": w_out, "ffn_gain": ffn_gain, "w_gate": w_gate, "w_up": w_up, "w_down": w_down, "out_grad": out_grad}


@jax.custom_vjp
def low(v):
    return lax.optimization_barrier(v.astype(jnp.bfloat16)).astype(jnp.float32)

@jax.custom_vjp
def low_back(v):
    return v

def low_keep(v):
    return (low(v), None)

def low_pass(kept, grad):
    return (grad,)

def back_keep(v):
    return (v, None)

def back_low(kept, grad):
    return (low(grad),)
low.defvjp(low_keep, low_pass)
low_back.defvjp(back_keep, back_low)
epsilon = 1e-05
highest_precision = lax.Precision.HIGHEST

def features(feature_in):
    in_width = feature_in.shape[-1]
    outer_prod = feature_in[..., :, None] * feature_in[..., None, :]
    outer_prod = outer_prod.reshape(feature_in.shape[:-1] + (in_width * in_width,))
    ones_column = jnp.ones(feature_in.shape[:-1] + (1,), jnp.float32)
    return jnp.concatenate([ones_column, feature_in * in_width ** (-0.25), outer_prod / math.sqrt(2.0 * in_width)], -1)

def rms_scale(inputs, norm_weight):
    return inputs * lax.rsqrt(lax.optimization_barrier(jnp.mean(inputs * inputs, -1, keepdims=True)) + epsilon) * norm_weight

def matmul(left, right):
    return jnp.einsum('rtd,de->rte', left, right, precision=highest_precision)

def doc_index_of(doc_lengths):
    doc_ends = jnp.cumsum(doc_lengths, -1).astype(jnp.int32)
    positions = jnp.arange(SEQ, dtype=jnp.int32)
    return lax.optimization_barrier(jnp.sum((doc_ends[:, None, :] <= positions[None, :, None]).astype(jnp.int32), -1)).astype(jnp.int32)

def row_attention(query_row, key_row, value_row, doc_row):
    block = min(512, SEQ)
    count = SEQ // block
    head_count = query_row.shape[1]
    query_width = query_row.shape[2]
    value_width = value_row.shape[2]
    feat_count = 1 + query_width + query_width * query_width

    def step(carry, pieces):
        state, norm_state, last_doc = carry
        query_block, key_block, value_block, doc_block = pieces
        scores = jnp.einsum('ihf,jhf->hij', query_block, key_block, precision=highest_precision) / math.sqrt(query_width)
        positions = jnp.arange(block, dtype=jnp.int32)
        allowed = (positions[:, None] >= positions[None, :]) & (doc_block[:, None] == doc_block[None, :])
        kernel = jnp.where(allowed[None], 1.0 + scores + 0.5 * scores * scores, 0.0)
        numerator = jnp.einsum('hij,jhv->ihv', kernel, value_block, precision=highest_precision)
        denominator = lax.optimization_barrier(jnp.sum(kernel, -1)).T
        query_feats = features(query_block)
        carry_mask = (doc_block == last_doc).astype(jnp.float32)[:, None]
        numerator = numerator + carry_mask[:, :, None] * jnp.einsum('ihe,hev->ihv', query_feats, state, precision=highest_precision)
        denominator = denominator + carry_mask * jnp.einsum('ihe,he->ih', query_feats, norm_state, precision=highest_precision)
        final_doc = doc_block[-1].astype(jnp.int32)
        keep_state = (last_doc == final_doc).astype(jnp.float32)
        tail_mask = (doc_block == final_doc).astype(jnp.float32)
        key_feats = features(key_block) * tail_mask[:, None, None]
        state = keep_state * state + jnp.einsum('jhe,jhv->hev', key_feats, value_block, precision=highest_precision)
        norm_state = keep_state * norm_state + lax.optimization_barrier(jnp.sum(key_feats, 0))
        return ((state, norm_state, final_doc), (numerator / denominator[:, :, None], denominator))
    start = (jnp.zeros((head_count, feat_count, value_width), jnp.float32), jnp.zeros((head_count, feat_count), jnp.float32), jnp.array(-1, jnp.int32))
    pieces = (query_row.reshape(count, block, head_count, query_width), key_row.reshape(count, block, head_count, query_width), value_row.reshape(count, block, head_count, value_width), doc_row.astype(jnp.int32).reshape(count, block))
    unused, outputs = lax.scan(jax.checkpoint(step), start, pieces)
    attn = outputs[0].reshape(SEQ, head_count, value_width)
    denominator = outputs[1].reshape(SEQ, head_count)
    return (attn, denominator)

def forward(doc_index, inputs, gain_first, query_w, key_w, value_w, out_w, gain_second, gate_w, up_w, down_w):
    rows_count = inputs.shape[0]
    normed_one = low(rms_scale(inputs, gain_first))
    query_all = low_back(low(matmul(normed_one, query_w)))
    key_all = low_back(low(matmul(normed_one, key_w)))
    value_all = low_back(low(matmul(normed_one, value_w)))
    query_heads = query_all.reshape(rows_count, SEQ, HEADS, FDIM)
    key_heads = key_all.reshape(rows_count, SEQ, HEADS, FDIM)
    value_heads = value_all.reshape(rows_count, SEQ, HEADS, D // HEADS)
    attn, denominator = jax.vmap(row_attention)(query_heads, key_heads, value_heads, doc_index)
    mixed = low(attn.reshape(rows_count, SEQ, D))
    middle = inputs + low_back(matmul(mixed, out_w))
    normed_two = low(rms_scale(middle, gain_second))
    gate_pre = low_back(matmul(normed_two, gate_w))
    up_pre = low_back(matmul(normed_two, up_w))
    hidden = low(jax.nn.silu(gate_pre) * up_pre)
    result = middle + matmul(hidden, down_w)
    return (result, jnp.sum(denominator) / (rows_count * SEQ * HEADS * SEQ))

def reference(tokens, doc_lengths, norm_gain, w_query, w_key, w_value, w_out, ffn_gain, w_gate, w_up, w_down, out_grad):
    doc_index = doc_index_of(doc_lengths)

    def closed(*floats):
        return forward(doc_index, *floats)
    floats = (tokens, norm_gain, w_query, w_key, w_value, w_out, ffn_gain, w_gate, w_up, w_down)
    floats = tuple((item.astype(jnp.float32) for item in floats))
    result, back_fn, denom_mean = jax.vjp(closed, *floats, has_aux=True)
    grads = back_fn(out_grad.astype(jnp.float32))
    return (result.astype(jnp.bfloat16), grads[0].astype(jnp.bfloat16), grads[1], grads[2], grads[3], grads[4], grads[5], grads[6], grads[7], grads[8], grads[9], denom_mean)
```

```python
import math

import jax
import jax.numpy as jnp
import numpy as np
from jax import lax
from jax.experimental import pallas as pl
from jax.experimental.pallas import tpu as pltpu
from jax.sharding import Mesh
from jax.sharding import PartitionSpec as P

HEADS = 16
FDIM = 16
EPS = 1e-05
BLK = ("x", "y", "c")
F32 = jnp.float32
BF16 = jnp.bfloat16

HH = 4
FW = 160
FT = HH * FW
SROWS = FT + 16
NROW = FT
LANE = 128
GROUP = 3 * LANE


def feature_tables():
    pick_a = np.zeros((FT, LANE), np.float32)
    pick_b = np.zeros((FT, LANE), np.float32)
    one_a = np.zeros((FT, 1), np.float32)
    one_b = np.zeros((FT, 1), np.float32)
    weight = np.zeros((FT, 1), np.float32)
    for h in range(HH):
        at = h * FW
        for a in range(FDIM + 1):
            for b in range(a, FDIM + 1):
                if a < FDIM:
                    pick_a[at, h * FDIM + a] = 1.0
                else:
                    one_a[at, 0] = 1.0
                if b < FDIM:
                    pick_b[at, h * FDIM + b] = 1.0
                else:
                    one_b[at, 0] = 1.0
                if b == FDIM:
                    weight[at, 0] = 1.0 if a == FDIM else 0.25
                else:
                    weight[at, 0] = 1.0 / 32 if a == b else 1.0 / 16
                at += 1
    return pick_a, pick_b, one_a, one_b, weight


def dot(a, b):
    return jnp.dot(a, b, preferred_element_type=F32)


def dot_nt(a, b):
    return lax.dot_general(a, b, (((1,), (1,)), ((), ())), preferred_element_type=F32)


def dot_tn(a, b):
    return lax.dot_general(a, b, (((0,), (0,)), ((), ())), preferred_element_type=F32)


def smem():
    return pl.BlockSpec(memory_space=pltpu.SMEM)


def vmem():
    return pl.BlockSpec(memory_space=pltpu.VMEM)


def hbm():
    return pl.BlockSpec(memory_space=pl.ANY)


def call(body, outs, *args, kinds=None, scratch=(), flops=0, limit=48):
    kinds = kinds or {}
    in_specs = [kinds.get(k, vmem)() for k in range(len(args))]
    moved = sum(math.prod(a.shape) * a.dtype.itemsize for a in args)
    moved += sum(math.prod(o.shape) * o.dtype.itemsize for o in outs)
    return pl.pallas_call(
        body,
        out_shape=outs,
        in_specs=in_specs,
        out_specs=[vmem() for _ in outs],
        scratch_shapes=list(scratch),
        compiler_params=pltpu.CompilerParams(vmem_limit_bytes=limit * 2**20),
        cost_estimate=pl.CostEstimate(flops=flops, bytes_accessed=moved, transcendentals=0),
    )(*args)


def out(shape, dtype):
    return jax.ShapeDtypeStruct(shape, dtype)


def doc_at(info, row, position):
    total = jnp.int32(0)
    for k in range(8):
        total += (info[row, k] <= position).astype(jnp.int32)
    return total


def same(a, b):
    return (a == b).astype(F32)


def block_start(info, x=None, y=None, c=None):
    x = info[2, 0] if x is None else x
    y = info[2, 1] if y is None else y
    c = info[2, 2] if c is None else c
    return ((x * 4 + y) * 2 + c) * LANE


def positions(info, dim):
    shape = (LANE, 1) if dim == 0 else (1, LANE)
    t = lax.broadcasted_iota(jnp.int32, shape, dim)
    slot, inside = t // 32, t % 32
    z = info[2, 3]
    return block_start(info) + 32 * ((z - slot + 4) % 4) + inside


def doc_of(info, row, where):
    total = jnp.zeros(where.shape, jnp.int32)
    for k in range(8):
        total += (info[row, k] <= where).astype(jnp.int32)
    return total


def row_of(value, row):
    return jnp.concatenate([value[64 * s + 32 * row : 64 * s + 32 * row + 32] for s in range(4)], 0)


def put_row(ref, row, value):
    for s in range(4):
        ref[64 * s + 32 * row : 64 * s + 32 * row + 32, :] = value[32 * s : 32 * s + 32]


def diagonal(g):
    n = g.shape[-1]
    rows = lax.broadcasted_iota(jnp.int32, (n, n), 0)
    cols = lax.broadcasted_iota(jnp.int32, (n, n), 1)
    return jnp.where(rows == cols, jnp.broadcast_to(g.astype(F32), (n, n)), 0.0).astype(BF16)


def early_body(g_ref, q_ref, k_ref, v_ref, o_ref):
    d = diagonal(g_ref[...])
    qk = jnp.concatenate([q_ref[...], k_ref[...]], 1)
    o_ref[:, :LANE] = dot(d, qk).astype(BF16)
    o_ref[:, LANE:] = dot(d, v_ref[...]).astype(BF16)


def bulk_body(g_ref, wo_ref, wg_ref, wu_ref, wd_ref, o_ref):
    d = diagonal(g_ref[...])
    eye = diagonal(jnp.ones_like(g_ref[...]))
    units = wg_ref.shape[1]
    gate = dot(d, wg_ref[...]).astype(BF16)
    up = dot(d, wu_ref[...]).astype(BF16)
    down = dot_nt(eye, wd_ref[...]).astype(BF16)
    groups = -(-units // LANE)
    for k, part in enumerate((gate, up, down)):
        for b in range(groups):
            lo, hi = b * LANE, min((b + 1) * LANE, units)
            at = b * GROUP + k * LANE
            if hi - lo < LANE:
                fill = jnp.zeros((part.shape[0], LANE - (hi - lo)), BF16)
                o_ref[:, at : at + LANE] = jnp.concatenate([part[:, lo:hi], fill], 1)
            else:
                o_ref[:, at : at + LANE] = part[:, lo:hi]
    o_ref[:, groups * GROUP :] = dot_nt(eye, wo_ref[...]).astype(BF16)


def project_body(info, x_ref, w_ref, ska, skb, one_a, one_b, p_ref, r_ref, keep_ref, send_ref):
    x = x_ref[...]
    xf = x.astype(F32)
    r = lax.rsqrt(jnp.mean(xf * xf, -1, keepdims=True) + EPS)
    r_ref[...] = r
    p = (dot(x, w_ref[...]) * r).astype(BF16)
    p_ref[...] = p
    c = info[2, 2]
    for row in range(2):
        mine = row_of(p, row)
        qk, v = mine[:, :LANE], mine[:, LANE:]
        tail_doc = doc_at(info, row, block_start(info) + LANE - 1)
        tail = (doc_of(info, row, positions(info, 1)) == tail_doc).astype(F32)
        phi = (dot_nt(ska[...], qk) + one_a[...]) * (dot_nt(skb[...], qk) + one_b[...]) * tail
        phi = phi.astype(BF16)
        state = dot(phi, v)
        count = dot_nt(jnp.ones((8, LANE), BF16), phi)[0:1]
        packed = pack_state(state, count)

        @pl.when(c == row)
        def _():
            keep_ref[...] = packed

        @pl.when(c != row)
        def _():
            send_ref[...] = packed


def pack_state(state, count):
    parts = [
        state[h * FW : (h + 1) * FW, h * LANE : (h + 1) * LANE].astype(BF16) for h in range(HH)
    ]
    high = count.astype(BF16).astype(F32)
    low = count - high
    rows = lax.broadcasted_iota(jnp.int32, (16, LANE), 0)
    tile = jnp.zeros((16, LANE), F32)
    for j in range(FT // LANE):
        tile = jnp.where(rows == j, high[:, j * LANE : (j + 1) * LANE], tile)
        tile = jnp.where(rows == j + 5, low[:, j * LANE : (j + 1) * LANE], tile)
    return jnp.concatenate([*parts, tile.astype(BF16)], 0)


def unpack_state(packed):
    blocks = []
    for h in range(HH):
        mine = packed[h * FW : (h + 1) * FW]
        zero = jnp.zeros_like(mine)
        blocks.append(jnp.concatenate([mine if g == h else zero for g in range(HH)], 1))
    state = jnp.concatenate(blocks, 0)
    tile = packed[NROW:].astype(F32)
    lanes = lax.broadcasted_iota(jnp.int32, (8, FT), 1) // FW
    heads = lax.broadcasted_iota(jnp.int32, (8, FT), 0)
    counts = []
    for first in (0, 5):
        line = jnp.concatenate([tile[first + j : first + j + 1] for j in range(5)], 1)
        counts.append(
            jnp.where(lanes == heads, jnp.broadcast_to(line, (8, FT)), 0.0).astype(BF16)
        )
    return state, counts[0], counts[1]


def chip_body(backward, info, keep_ref, recv_ref, o_ref):
    c = info[2, 2]
    base = block_start(info, c=0)
    keep, recv = keep_ref[...].astype(F32), recv_ref[...].astype(F32)
    first = jnp.where(c == 0, 1.0, 0.0)
    zero = first * keep + (1.0 - first) * recv
    one = first * recv + (1.0 - first) * keep
    if backward:
        o_ref[...] = (zero + same(doc_at(info, c, base), doc_at(info, c, base + LANE)) * one).astype(
            BF16
        )
    else:
        o_ref[...] = (
            one
            + same(doc_at(info, c, base + LANE - 1), doc_at(info, c, base + 2 * LANE - 1)) * zero
        ).astype(BF16)


def line_body(backward, info, t0, t1, t2, t3, o_ref):
    c, y = info[2, 2], info[2, 1]
    start = block_start(info, y=0, c=0)
    whole = doc_at(info, c, start if backward else start + 8 * LANE - 1)
    total = jnp.zeros(o_ref.shape, F32)
    for k, t in enumerate((t0, t1, t2, t3)):
        there = start + ((y - k + 4) % 4) * 2 * LANE
        there = there if backward else there + 2 * LANE - 1
        total += same(doc_at(info, c, there), whole) * t[...].astype(F32)
    o_ref[...] = total.astype(BF16)


def enter_body(backward, info, keep, recv, t1, t2, t3, s1, s2, s3, mine_ref, send_ref):
    x, y, c = info[2, 0], info[2, 1], info[2, 2]
    base = block_start(info, c=0)
    here = doc_at(info, c, base + 2 * LANE - 1 if backward else base)
    total = jnp.zeros(keep.shape, F32)
    for k, (t, s) in enumerate(((t1, s1), (t2, s2), (t3, s3)), 1):
        there_y, there_x = (y - k + 4) % 4, (x - k + 4) % 4
        at_y = block_start(info, y=there_y, c=0)
        at_x = block_start(info, x=there_x, y=0, c=0)
        if backward:
            use_y = same(doc_at(info, c, at_y), here) * (there_y > y).astype(F32)
            use_x = same(doc_at(info, c, at_x), here) * (there_x > x).astype(F32)
        else:
            use_y = same(doc_at(info, c, at_y + 2 * LANE - 1), here) * (there_y < y).astype(F32)
            use_x = same(doc_at(info, c, at_x + 8 * LANE - 1), here) * (there_x < x).astype(F32)
        total += use_y * t[...].astype(F32) + use_x * s[...].astype(F32)
    is_zero = jnp.where(c == 0, 1.0, 0.0)
    if backward:
        one = is_zero * recv[...].astype(F32) + (1.0 - is_zero) * keep[...].astype(F32)
        last = doc_at(info, c, base + LANE - 1)
        for_zero = same(doc_at(info, c, base + LANE), last) * one
        for_zero += same(here, last) * total
        for_one = total
    else:
        zero = is_zero * keep[...].astype(F32) + (1.0 - is_zero) * recv[...].astype(F32)
        begun = doc_at(info, c, base + LANE)
        for_zero = total
        for_one = same(doc_at(info, c, base + LANE - 1), begun) * zero
        for_one += same(here, begun) * total
    mine_ref[...] = (is_zero * for_zero + (1.0 - is_zero) * for_one).astype(BF16)
    send_ref[...] = (is_zero * for_one + (1.0 - is_zero) * for_zero).astype(BF16)


def shift(value, axis, k):
    n = 2 if axis == "c" else 4
    return lax.ppermute(value, axis, [(i, (i + k) % n) for i in range(n)])


def around(value, axis):
    return [value] + [shift(value, axis, k) for k in (1, 2, 3)]


def scan_states(info, keep, send, backward):
    packed = out((SROWS, LANE), BF16)
    kinds = {0: smem}

    def body(f):
        return lambda *refs: f(backward, *refs)

    recv = shift(send, "c", 1)
    (chip,) = call(body(chip_body), [packed], info, keep, recv, kinds=kinds)
    t = around(chip, "y")
    (line,) = call(body(line_body), [packed], info, *t, kinds=kinds)
    s = around(line, "x")
    mine, other = call(
        body(enter_body), [packed, packed], info, keep, recv, *t[1:], *s[1:], kinds=kinds
    )
    return mine, shift(other, "c", 1)


def entered(info, row, mine, other):
    return jnp.where(info[2, 2] == row, mine[...], other[...])


def pairs(info, row, transposed=False):
    at_i, at_j = positions(info, 0), positions(info, 1)
    doc_i, doc_j = doc_of(info, row, at_i), doc_of(info, row, at_j)
    return (doc_i == doc_j) & (at_i >= at_j), doc_i


def by_head(q):
    lanes = lax.broadcasted_iota(jnp.int32, q.shape, 1) // FDIM
    return jnp.concatenate([jnp.where(lanes == h, q, jnp.zeros_like(q)) for h in range(HH)], 0)


def carry_of(info, row, doc_i):
    return (doc_i == doc_at(info, row, block_start(info))).astype(F32)


def mix_body(
    info, p_ref, mine, other, sqa, sqb, one_a, one_b, wo_hbm,
    mixed_ref, den_ref, total_ref, b0, b1, b2, b3, wo, sem,
):
    width = wo.shape[1]
    copy = pltpu.make_async_copy(
        wo_hbm.at[:, pl.ds(wo_hbm.shape[1] - width, width)], wo, sem
    )
    copy.start()
    p = p_ref[...]
    total = jnp.zeros((), F32)
    for row in range(2):
        line = row_of(p, row)
        qk, v = line[:, :LANE], line[:, LANE:]
        q, k = line[:, : HH * FDIM], line[:, HH * FDIM : 2 * HH * FDIM]
        ok, doc_i = pairs(info, row)
        carry = carry_of(info, row, doc_i)
        s = dot_nt(by_head(q), k) * 0.25
        phi = (dot(qk, sqa[...]) + one_a[...]) * (dot(qk, sqb[...]) + one_b[...]) * carry
        phi = phi.astype(BF16)
        state, high, low = unpack_state(entered(info, row, mine, other))
        num = dot(phi, state)
        den = dot_nt(phi, high) + dot_nt(phi, low)
        nums, dens = [], []
        for h in range(HH):
            sh = s[h * LANE : (h + 1) * LANE]
            kap = jnp.where(ok, 1.0 + sh + 0.5 * sh * sh, 0.0)
            d = jnp.sum(kap, -1, keepdims=True) + den[:, h : h + 1]
            n = dot(kap.astype(BF16), v[:, h * LANE : (h + 1) * LANE])
            nums.append((n + num[:, h * LANE : (h + 1) * LANE]) / d)
            dens.append(d)
        put_row(mixed_ref, row, jnp.concatenate(nums, 1).astype(BF16))
        lanes = lax.broadcasted_iota(jnp.int32, (LANE, 8), 1)
        den8 = jnp.ones((LANE, 8), F32)
        for h in range(HH):
            den8 = jnp.where(lanes == h, dens[h], den8)
        put_row(den_ref, row, den8)
        total += jnp.sum(jnp.where(lanes < HH, den8, 0.0))
    total_ref[...] = jnp.full(total_ref.shape, total, F32)
    copy.wait()
    branch = dot_nt(mixed_ref[...], wo[...])
    for s, b in enumerate((b0, b1, b2, b3)):
        b[...] = branch[64 * s : 64 * s + 64].astype(BF16)


def unmix_body(
    info, p_ref, mine, other, sqa, sqb, one_a, one_b, wo_hbm, mixed_ref, den_ref,
    m0, m1, m2, m3,
    dp_ref, keep_ref, send_ref, wo, dm, sem,
):
    width = wo.shape[1]
    copy = pltpu.make_async_copy(
        wo_hbm.at[:, pl.ds(wo_hbm.shape[1] - width, width)], wo, sem
    )
    copy.start()
    for s, m in enumerate((m0, m1, m2, m3)):
        dm[64 * s : 64 * s + 64, :] = m[...]
    p, mixed, den = p_ref[...], mixed_ref[...], den_ref[...]
    c = info[2, 2]
    copy.wait()
    d_attn = dot(dm[...], wo[...])
    for row in range(2):
        line = row_of(p, row)
        qk, v = line[:, :LANE], line[:, LANE:]
        q, k = line[:, : HH * FDIM], line[:, HH * FDIM : 2 * HH * FDIM]
        ok, doc_i = pairs(info, row)
        carry = carry_of(info, row, doc_i)
        q4 = by_head(q)
        s = dot_nt(q4, k) * 0.25
        da, at, dn8 = row_of(d_attn, row), row_of(mixed, row).astype(F32), row_of(den, row)
        dnums, ddens, gs, dvs = [], [], [], []
        for h in range(HH):
            here = slice(h * LANE, (h + 1) * LANE)
            inv = 1.0 / dn8[:, h : h + 1]
            dnum = da[:, here] * inv
            dden = -jnp.sum(dnum * at[:, here], -1, keepdims=True)
            sh = s[here]
            kap = jnp.where(ok, 1.0 + sh + 0.5 * sh * sh, 0.0)
            dnum = dnum.astype(BF16)
            g = (dot_nt(dnum, v[:, here]) + dden) * (1.0 + sh) * 0.25
            gs.append(jnp.where(ok, g, 0.0).astype(BF16))
            dvs.append(dot_tn(kap.astype(BF16), dnum))
            dnums.append(dnum)
            ddens.append(dden)
        g4 = jnp.concatenate(gs, 0)
        dnum = jnp.concatenate(dnums, 1)
        lanes = lax.broadcasted_iota(jnp.int32, (LANE, 8), 1)
        dden8 = jnp.zeros((LANE, 8), F32)
        for h in range(HH):
            dden8 = jnp.where(lanes == h, ddens[h], dden8)
        dk = dot_tn(g4, q4)
        dq4 = dot(g4, k)
        qlanes = lax.broadcasted_iota(jnp.int32, (LANE, HH * FDIM), 1) // FDIM
        dq = jnp.zeros((LANE, HH * FDIM), F32)
        for h in range(HH):
            dq += jnp.where(qlanes == h, dq4[h * LANE : (h + 1) * LANE], 0.0)
        fa = dot(qk, sqa[...]) + one_a[...]
        fb = dot(qk, sqb[...]) + one_b[...]
        state, high, low = unpack_state(entered(info, row, mine, other))
        dden_low = dden8.astype(BF16)
        dphi = dot_nt(dnum, state) + dot(dden_low, high) + dot(dden_low, low)
        dphi = dphi * carry
        dqk = dot_nt((dphi * fb).astype(BF16), sqa[...]) + dot_nt((dphi * fa).astype(BF16), sqb[...])
        dq += dqk[:, : HH * FDIM]
        put_row(dp_ref, row, jnp.concatenate([dq, dk, *dvs], 1))
        phi = (fa * fb * carry).astype(BF16)
        dstate = dot_tn(phi, dnum)
        heads = lax.broadcasted_iota(jnp.int32, (8, FT), 0)
        flanes = lax.broadcasted_iota(jnp.int32, (8, FT), 1) // FW
        dcount = jnp.where(heads == flanes, dot_tn(dden_low, phi), 0.0)
        packed = pack_state(dstate, jnp.sum(dcount, 0, keepdims=True))

        @pl.when(c == row)
        def _():
            keep_ref[...] = packed

        @pl.when(c != row)
        def _():
            send_ref[...] = packed


def unproject_body(
    info, p_ref, dp_ref, mine, other, ska, skb, one_a, one_b, w_ref, r_ref,
    gp_ref, e0, e1, e2, e3, low_ref,
):
    p, dp = p_ref[...], dp_ref[...]
    for row in range(2):
        line, dline = row_of(p, row), row_of(dp, row)
        qk, v = line[:, :LANE], line[:, LANE:]
        tail_doc = doc_at(info, row, block_start(info) + LANE - 1)
        tail = (doc_of(info, row, positions(info, 0)) == tail_doc).astype(F32)
        fa = dot(qk, ska[...]) + one_a[...]
        fb = dot(qk, skb[...]) + one_b[...]
        state, high, low = unpack_state(entered(info, row, mine, other))
        ones = jnp.ones((LANE, 8), BF16)
        dphi = (dot_nt(v, state) + dot(ones, high) + dot(ones, low)) * tail
        dqk = dot_nt((dphi * fb).astype(BF16), ska[...]) + dot_nt((dphi * fa).astype(BF16), skb[...])
        dv = dot((fa * fb * tail).astype(BF16), state)
        lanes = lax.broadcasted_iota(jnp.int32, (LANE, LANE), 1)
        dqk = dline[:, :LANE] + jnp.where(lanes >= HH * FDIM, dqk, 0.0)
        put_row(low_ref, row, jnp.concatenate([dqk, dline[:, LANE:] + dv], 1).astype(BF16))
    d = low_ref[...]
    gp_ref[...] = (d.astype(F32) * r_ref[...]).astype(BF16)
    e = dot_nt(d, w_ref[...])
    for s, b in enumerate((e0, e1, e2, e3)):
        b[...] = e[64 * s : 64 * s + 64].astype(BF16)


def middle_body(x_ref, a, b, c, d, middle_ref, low_ref):
    u = x_ref[...].astype(F32)
    for part in (a, b, c, d):
        u += part[...].astype(F32)
    middle_ref[...] = u
    low_ref[...] = (u * lax.rsqrt(jnp.mean(u * u, -1, keepdims=True) + EPS)).astype(BF16)


def norm_back_body(base_ref, u_ref, a, b, c, d, full_ref, low_ref):
    u = u_ref[...].astype(F32)
    e = jnp.zeros(u.shape, F32)
    for part in (a, b, c, d):
        e += part[...].astype(F32)
    r = lax.rsqrt(jnp.mean(u * u, -1, keepdims=True) + EPS)
    slope = jnp.mean(e * u, -1, keepdims=True)
    total = base_ref[...].astype(F32) + r * e - u * (r * r * r * slope)
    full_ref[...] = total
    low_ref[...] = total.astype(BF16)


def block_out_body(middle_ref, a, b, c, d, o_ref):
    u = middle_ref[...]
    for part in (a, b, c, d):
        u += part[...].astype(F32)
    o_ref[...] = u.astype(BF16)


def place_body(info, a, b, c, d, o_ref):
    z = info[2, 3]
    for k, part in enumerate((a, b, c, d)):
        at = pl.multiple_of(32 * ((z - k + 4) % 4), 32)
        for row in range(2):
            o_ref[row, pl.ds(at, 32), :] = part[32 * row : 32 * row + 32, :]


def ffn_body(
    u0, u1, u2, u3, dy_ref, w_ref, a_ref, e0, e1, e2, e3, f0, f1, f2, f3, u, e_acc, f_acc
):
    step = pl.program_id(0)

    @pl.when(step == 0)
    def _():
        for s, part in enumerate((u0, u1, u2, u3)):
            u[64 * s : 64 * s + 64, :] = part[...]
        e_acc[...] = jnp.zeros_like(e_acc)
        f_acc[...] = jnp.zeros_like(f_acc)

    pre = dot(u[...], w_ref[:, : 2 * LANE])
    d_hidden = dot(dy_ref[...], w_ref[:, 2 * LANE :])
    gate, up = pre[:, :LANE], pre[:, LANE:]
    sigma = 1.0 / (1.0 + jnp.exp(-gate))
    silu = gate * sigma
    hidden = (silu * up).astype(BF16)
    d_gate = d_hidden * up * sigma * (1.0 + gate * (1.0 - sigma))
    d_up = d_hidden * silu
    d_gu = jnp.concatenate([d_gate, d_up], 1).astype(BF16)
    a_ref[:, : 2 * LANE] = d_gu
    a_ref[:, 2 * LANE :] = hidden
    e_acc[...] += dot_nt(d_gu, w_ref[:, : 2 * LANE])
    f_acc[...] += dot_nt(hidden, w_ref[:, 2 * LANE :])

    @pl.when(step == pl.num_programs(0) - 1)
    def _():
        for s, (e, f) in enumerate(((e0, f0), (e1, f1), (e2, f2), (e3, f3))):
            e[...] = e_acc[64 * s : 64 * s + 64, :].astype(BF16)
            f[...] = f_acc[64 * s : 64 * s + 64, :].astype(BF16)


def feed_forward(us, dy, bulk, groups):
    d = dy.shape[1]
    whole = pl.BlockSpec((64, d), lambda b: (0, 0))
    piece = out((64, d), BF16)
    tokens = dy.shape[0]
    return pl.pallas_call(
        ffn_body,
        grid=(groups,),
        out_shape=[out((tokens, groups * GROUP), BF16)] + [piece] * 8,
        in_specs=[whole] * 4
        + [pl.BlockSpec((tokens, d), lambda b: (0, 0)), pl.BlockSpec((d, GROUP), lambda b: (0, b))],
        out_specs=[pl.BlockSpec((tokens, GROUP), lambda b: (0, b))] + [whole] * 8,
        scratch_shapes=[
            pltpu.VMEM((tokens, d), BF16),
            pltpu.VMEM((tokens, d), F32),
            pltpu.VMEM((tokens, d), F32),
        ],
        compiler_params=pltpu.CompilerParams(vmem_limit_bytes=48 * 2**20),
        cost_estimate=pl.CostEstimate(
            flops=12 * tokens * d * groups * LANE,
            bytes_accessed=2 * d * groups * GROUP + 12 * tokens * d,
            transcendentals=0,
        ),
    )(*us, dy, bulk)


def turn_body(info, a, b, c, d, keep_ref, send_ref, t):
    core = info[2, 2]
    for s, part in enumerate((a, b, c, d)):
        t[:, 64 * s : 64 * s + 64] = part[...].astype(F32).T
    for i in range(t.shape[0] // LANE):
        here = pl.multiple_of(LANE * i + 64 * core, 64)
        there = pl.multiple_of(LANE * i + 64 - 64 * core, 64)
        keep_ref[64 * i : 64 * i + 64, :] = t[pl.ds(here, 64), :].astype(BF16)
        send_ref[64 * i : 64 * i + 64, :] = t[pl.ds(there, 64), :].astype(BF16)


def turned(info, parts):
    d = parts[0].shape[1]
    half = out((d // 2, 256), BF16)
    keep, send = call(
        turn_body, [half, half], info, *parts, kinds={0: smem}, scratch=[pltpu.VMEM((d, 256), F32)]
    )
    return keep, send


def ffn_grad_body(uk, ur, yk, yr, a_own, a_other, o_ref):
    gu, hd = slice(0, 2 * LANE), slice(2 * LANE, GROUP)
    o_ref[:, gu] = (dot(uk[...], a_own[:, gu]) + dot(ur[...], a_other[:, gu])).astype(BF16)
    o_ref[:, hd] = (dot(yk[...], a_own[:, hd]) + dot(yr[...], a_other[:, hd])).astype(BF16)


def ffn_grads(uk, ur, yk, yr, a_own, a_other, groups):
    rows, tokens = uk.shape
    whole = pl.BlockSpec((rows, tokens), lambda b: (0, 0))
    part = pl.BlockSpec((tokens, GROUP), lambda b: (0, b))
    return pl.pallas_call(
        ffn_grad_body,
        grid=(groups,),
        out_shape=out((rows, groups * GROUP), BF16),
        in_specs=[whole] * 4 + [part] * 2,
        out_specs=pl.BlockSpec((rows, GROUP), lambda b: (0, b)),
        compiler_params=pltpu.CompilerParams(vmem_limit_bytes=48 * 2**20),
        cost_estimate=pl.CostEstimate(
            flops=4 * rows * tokens * groups * GROUP,
            bytes_accessed=2 * rows * groups * GROUP,
            transcendentals=0,
        ),
    )(uk, ur, yk, yr, a_own, a_other)


def grad_body(lk, lr, a_own, a_other, o_ref):
    o_ref[...] = (dot(lk[...], a_own[...]) + dot(lr[...], a_other[...])).astype(BF16)


def spread_rows(rows, axis_first):
    n = rows.shape[1]
    cube = rows.reshape(4, 4, 64, n)
    x, y = lax.axis_index("x"), lax.axis_index("y")

    def kept(value, axis, place):
        total = lax.dynamic_index_in_dim(value, place, 0, False).astype(F32)
        for k in (1, 2, 3):
            part = lax.dynamic_index_in_dim(value, (place + k) % 4, 0, False)
            total += shift(part, axis, k).astype(F32)
        return total.astype(BF16)

    if axis_first == "y":
        return kept(kept(jnp.moveaxis(cube, 1, 0), "y", y), "x", x)
    return kept(kept(cube, "x", x), "y", y)


def finish_ffn_body(s_ref, wg_ref, wu_ref, g_ref, gate_ref, up_ref, down_ref, gain_ref):
    units = gate_ref.shape[1]
    g = g_ref[...].astype(F32)
    parts = [[], [], []]
    for b in range(s_ref.shape[1] // GROUP):
        for k in range(3):
            at = b * GROUP + k * LANE
            parts[k].append(s_ref[:, at : at + LANE])
    gate, up, down = [jnp.concatenate(p, 1)[:, :units].astype(F32) for p in parts]
    gain = jnp.sum(gate * wg_ref[...].astype(F32) + up * wu_ref[...].astype(F32), 1, keepdims=True)
    gain_ref[...] = jnp.broadcast_to(gain, gain_ref.shape)
    gate_ref[...] = gate * g
    up_ref[...] = up * g
    down_ref[...] = down.T


def finish_mix_body(
    s_ref, so_ref, wq_ref, wk_ref, wv_ref, g_ref, q_ref, k_ref, v_ref, out_ref, gain_ref
):
    g = g_ref[...].astype(F32)
    grads = s_ref[...].astype(F32)
    w = jnp.concatenate([wq_ref[...], wk_ref[...], wv_ref[...]], 1).astype(F32)
    gain = jnp.sum(grads * w, 1, keepdims=True)
    gain_ref[...] = jnp.broadcast_to(gain, gain_ref.shape)
    scaled = grads * g
    q_ref[...] = scaled[:, :64]
    k_ref[...] = scaled[:, 64:128]
    v_ref[...] = scaled[:, 128:]
    out_ref[...] = so_ref[...].astype(F32).T


def slots(value, z):
    parts = []
    for k in range(4):
        at = 32 * ((z - k) % 4)
        part = lax.dynamic_slice_in_dim(value, at, 32, 1)
        parts.append(part.reshape(64, value.shape[-1]))
    return parts


def in_order(parts, place):
    ring = jnp.stack([parts[0], parts[3], parts[2], parts[1]] * 2)
    return lax.dynamic_slice_in_dim(ring, (4 - place) % 4, 4, 0)


def sum_to_slots(parts):
    return [parts[0]] + [shift(parts[k], "z", -k) for k in (1, 2, 3)]


def on_device(
    tokens,
    doc_lengths,
    norm_gain,
    w_query,
    w_key,
    w_value,
    w_out,
    ffn_gain,
    w_gate,
    w_up,
    w_down,
    out_grad,
):
    x, y, c, z = (lax.axis_index(a) for a in ("x", "y", "c", "z"))
    ends = jnp.cumsum(doc_lengths, -1).astype(jnp.int32)
    places = jnp.stack([x, y, c, z, x, x, x, x]).astype(jnp.int32)
    info = jnp.concatenate([ends, places[None]], 0)
    d = tokens.shape[-1]
    units = w_gate.shape[1]
    groups = -(-units // LANE)
    with_info = {0: smem}

    (early,) = call(
        early_body, [out((64, 640), BF16)], norm_gain[None], w_query, w_key, w_value
    )
    (bulk_own,) = call(
        bulk_body,
        [out((64, groups * GROUP + w_out.shape[0]), BF16)],
        ffn_gain[None], w_out, w_gate, w_up, w_down,
    )
    bulk = lax.all_gather(bulk_own, BLK, axis=0, tiled=True)

    line = in_order(around(early, "x"), x)
    grid = in_order(around(line, "y"), y)
    both = shift(grid, "c", 1)
    pair = jnp.where(c == 0, jnp.stack([grid, both]), jnp.stack([both, grid]))
    w_in = jnp.transpose(pair, (2, 1, 0, 3, 4)).reshape(d, 640)

    xs, dys = slots(tokens, z), slots(out_grad, z)
    x_all, dy_all = jnp.concatenate(xs, 0), jnp.concatenate(dys, 0)
    xk, x_send = turned(info, xs)
    yk, y_send = turned(info, dys)
    xr, yr = shift(x_send, "c", 1), shift(y_send, "c", 1)

    pick_a, pick_b, one_a, one_b, weight = feature_tables()
    roll = lambda t: np.roll(t, HH * FDIM, 1)
    ska = jnp.asarray(roll(pick_a), BF16)
    skb = jnp.asarray(roll(pick_b), BF16)
    ka, kb = jnp.asarray(one_a), jnp.asarray(one_b)
    ska_t = jnp.asarray(roll(pick_a).T.copy(), BF16)
    skb_t = jnp.asarray(roll(pick_b).T.copy(), BF16)
    ka_t, kb_t = jnp.asarray(one_a.T.copy()), jnp.asarray(one_b.T.copy())
    sqa_t = jnp.asarray((pick_a * weight).T.copy(), BF16)
    sqb_t = jnp.asarray(pick_b.T.copy(), BF16)
    qa_t, qb_t = jnp.asarray((one_a * weight).T.copy()), kb_t

    state = out((SROWS, LANE), BF16)
    p, r, keep, send = call(
        project_body,
        [out((256, 640), BF16), out((256, 1), F32), state, state],
        info, x_all, w_in, ska, skb, ka, kb,
        kinds=with_info, flops=2 * 256 * d * 640,
    )
    mine, other = scan_states(info, keep, send, False)

    piece = out((64, d), BF16)
    mixed, den, total, *branch = call(
        mix_body,
        [out((256, 512), BF16), out((256, 8), F32), out((8, LANE), F32)] + [piece] * 4,
        info, p, mine, other, sqa_t, sqb_t, qa_t, qb_t, bulk,
        kinds={0: smem, 8: hbm},
        scratch=[pltpu.VMEM((d, 512), BF16), pltpu.SemaphoreType.DMA],
        flops=2 * 256 * d * 512,
    )
    middle, u2 = call(
        middle_body, [out((64, d), F32), piece], xs[0], *sum_to_slots(branch)
    )
    us = around(u2, "z")
    a_own, *ef = feed_forward(us, dy_all, bulk, groups)
    e_parts, f_parts = ef[:4], ef[4:]
    d_middle, dm = call(
        norm_back_body, [out((64, d), F32), piece], dys[0], middle, *sum_to_slots(e_parts)
    )
    dms = around(dm, "z")

    uk, u_send = turned(info, us)
    ur = shift(u_send, "c", 1)
    a_other = shift(a_own, "c", 1)
    ffn_rows = ffn_grads(uk, ur, yk, yr, a_own, a_other, groups)
    ffn_sum = lax.psum_scatter(ffn_rows, ("x", "y"), scatter_dimension=0, tiled=True)

    dp, dkeep, dsend = call(
        unmix_body,
        [out((256, 640), F32), state, state],
        info, p, mine, other, sqa_t, sqb_t, qa_t, qb_t, bulk, mixed, den, *dms,
        kinds={0: smem, 8: hbm},
        scratch=[
            pltpu.VMEM((d, 512), BF16), pltpu.VMEM((256, d), BF16), pltpu.SemaphoreType.DMA,
        ],
        flops=2 * 256 * d * 512,
    )
    dmine, dother = scan_states(info, dkeep, dsend, True)

    mk, m_send = turned(info, dms)
    mr = shift(m_send, "c", 1)
    (out_rows,) = call(
        grad_body, [out((d // 2, 512), BF16)], mk, mr, mixed, shift(mixed, "c", 1),
        flops=4 * 256 * d * 512,
    )
    out_sum = spread_rows(out_rows, "x")

    gp, *e1 = call(
        unproject_body,
        [out((256, 640), BF16)] + [piece] * 4,
        info, p, dp, dmine, dother, ska_t, skb_t, ka_t, kb_t, w_in, r,
        kinds=with_info, scratch=[pltpu.VMEM((256, 640), BF16)],
        flops=2 * 256 * d * 640,
    )
    _, gx = call(
        norm_back_body, [out((64, d), F32), piece], d_middle, xs[0], *sum_to_slots(e1)
    )
    (input_grad,) = call(
        place_body, [out(tokens.shape, BF16)], info, *around(gx, "z"), kinds=with_info
    )

    (in_rows,) = call(
        grad_body, [out((d // 2, 640), BF16)], xk, xr, gp, shift(gp, "c", 1),
        flops=4 * 256 * d * 640,
    )
    in_sum = spread_rows(in_rows, "y")

    (bo,) = call(block_out_body, [piece], middle, *sum_to_slots(f_parts))
    (block_out,) = call(
        place_body, [out(tokens.shape, BF16)], info, *around(bo, "z"), kinds=with_info
    )

    row_tile = out((64, LANE), F32)
    g_gate, g_up, g_down, gain2 = call(
        finish_ffn_body,
        [out(w_gate.shape, F32), out(w_up.shape, F32), out(w_down.shape, F32), row_tile],
        ffn_sum, w_gate, w_up, ffn_gain[:, None],
    )
    g_q, g_k, g_v, g_out, gain1 = call(
        finish_mix_body,
        [out(w_query.shape, F32), out(w_key.shape, F32), out(w_value.shape, F32),
         out(w_out.shape, F32), row_tile],
        in_sum, out_sum, w_query, w_key, w_value, norm_gain[:, None],
    )
    gains = sum(around(jnp.stack([gain1[:, 0], gain2[:, 0]]), "z"))
    denom = total[0, 0]
    for axis in ("x", "y", "c", "z"):
        denom = lax.psum(denom, axis)
    seq = 32 * LANE
    denom_mean = denom / (2 * seq * HEADS * seq)
    return (
        block_out, input_grad, gains[0], g_q, g_k, g_v, g_out, gains[1], g_gate, g_up, g_down,
        denom_mean,
    )


def solution(mesh):
    finer = Mesh(mesh.devices.reshape(4, 4, 2, mesh.shape["head"]), ("x", "y", "c", "z"))
    placed = (
        P(None, BLK, None),
        P(),
        P(BLK),
        P(BLK, "z"),
        P(BLK, "z"),
        P(BLK, "z"),
        P("z", BLK),
        P(BLK),
        P(BLK, "z"),
        P(BLK, "z"),
        P("z", BLK),
        P(None, BLK, None),
    )
    return jax.shard_map(
        on_device,
        mesh=finer,
        in_specs=placed,
        out_specs=(
            P(None, BLK, None),
            P(None, BLK, None),
            P(BLK),
            P(BLK, "z"),
            P(BLK, "z"),
            P(BLK, "z"),
            P("z", BLK),
            P(BLK),
            P(BLK, "z"),
            P(BLK, "z"),
            P("z", BLK),
            P(),
        ),
        check_vma=False,
    )
```

```python
import math

import jax
import jax.numpy as jnp
from jax import lax
from jax.experimental import pallas as pl
from jax.experimental.pallas import tpu as pltpu
from jax.sharding import Mesh
from jax.sharding import PartitionSpec as P

HEADS = 16
FDIM = 16
EPS = 1e-05
BLK = ("x", "y", "c")
F32 = jnp.float32
BF16 = jnp.bfloat16

HH = 4
HF = HH * FDIM
FW = 160
FT = HH * FW
SROWS = FT + 16
LANE = 128
DOCS = 8


def dot(a, b):
    return jnp.dot(a, b, preferred_element_type=F32)


def dot_nt(a, b):
    return lax.dot_general(a, b, (((1,), (1,)), ((), ())), preferred_element_type=F32)


def dot_tn(a, b):
    return lax.dot_general(a, b, (((0,), (0,)), ((), ())), preferred_element_type=F32)


def out(shape, dtype):
    return jax.ShapeDtypeStruct(tuple(shape), dtype)


SPACES = {"s": pltpu.SMEM, "v": pltpu.VMEM, "h": pltpu.HBM, "d": pltpu.HBM, "a": pl.ANY}


def in_hbm(value):
    return pltpu.with_memory_space_constraint(value, pltpu.HBM)


def call(name, body, outs, *args, kinds="", after=(), through=(), scratch=(), flops=0, limit=12):
    kinds = kinds + "v" * (len(args) - len(kinds))
    n_args, n_extra, n_out = len(args), len(after) + len(through), len(outs)
    staged = [k for k in range(n_args) if kinds[k] == "d"]
    places = [pltpu.VMEM(args[k].shape, args[k].dtype) for k in staged]
    if staged:
        places.append(pltpu.SemaphoreType.DMA((len(staged),)))

    def inner(*refs):
        given, results = list(refs[:n_args]), refs[n_args + n_extra :]
        own = results[n_out + len(through) :]
        held, own = own[: len(places)], own[len(places) :]
        copies = [
            pltpu.make_async_copy(given[k], held[i], held[-1].at[i]) for i, k in enumerate(staged)
        ]
        for copy in copies:
            copy.start()
        for copy in copies:
            copy.wait()
        for i, k in enumerate(staged):
            given[k] = held[i]
        body(*given, *results[:n_out], *own)

    moved = sum(math.prod(a.shape) * a.dtype.itemsize for a in (*args, *outs))
    args = [in_hbm(a) if k in "hd" else a for a, k in zip(args, kinds)]
    through = [in_hbm(a) if a.size > 2**21 else a for a in through]
    with jax.named_scope(name):
        return pl.pallas_call(
            inner,
            out_shape=list(outs) + [out(t.shape, t.dtype) for t in through],
            in_specs=[pl.BlockSpec(memory_space=SPACES[k]) for k in kinds + "a" * n_extra],
            out_specs=[pl.BlockSpec(memory_space=SPACES[k]) for k in "v" * n_out + "a" * len(through)],
            scratch_shapes=[*places, *scratch],
            input_output_aliases={
                n_args + len(after) + k: n_out + k for k in range(len(through))
            },
            compiler_params=pltpu.CompilerParams(vmem_limit_bytes=limit * 2**20),
            cost_estimate=pl.CostEstimate(flops=flops, bytes_accessed=moved, transcendentals=0),
        )(*args, *after, *through)


def doc_at(info, row, position):
    total = jnp.int32(0)
    for k in range(DOCS):
        total += (info[row, k] <= position).astype(jnp.int32)
    return total


def doc_of(info, row, where):
    total = jnp.zeros(where.shape, jnp.int32)
    for k in range(DOCS):
        total += (info[row, k] <= where).astype(jnp.int32)
    return total


def same(a, b):
    return (a == b).astype(F32)


def block_start(info, x=None, y=None, c=None):
    x = info[2, 0] if x is None else x
    y = info[2, 1] if y is None else y
    c = info[2, 2] if c is None else c
    return ((x * 4 + y) * 2 + c) * LANE


def back(place, k):
    return (place - k + 4) % 4


def positions(info, dim):
    shape = (LANE, 1) if dim == 0 else (1, LANE)
    t = lax.broadcasted_iota(jnp.int32, shape, dim)
    slot, inside = t // 32, t % 32
    return block_start(info) + 32 * ((info[2, 3] - slot + 4) % 4) + inside


def row_of(value, row):
    return jnp.concatenate([value[64 * s + 32 * row : 64 * s + 32 * row + 32] for s in range(4)], 0)


def put_row(ref, row, value):
    for s in range(4):
        ref[64 * s + 32 * row : 64 * s + 32 * row + 32, :] = value[32 * s : 32 * s + 32]


def diagonal(g):
    n = g.shape[-1]
    rows = lax.broadcasted_iota(jnp.int32, (n, n), 0)
    cols = lax.broadcasted_iota(jnp.int32, (n, n), 1)
    return jnp.where(rows == cols, jnp.broadcast_to(g.astype(F32), (n, n)), 0.0).astype(BF16)


def column(g):
    return jnp.sum(diagonal(g).astype(F32), 1, keepdims=True)


def early_body(g_ref, q_ref, k_ref, v_ref, wo_ref, o_ref, out_ref):
    d = diagonal(g_ref[...])
    qk = jnp.concatenate([q_ref[...], k_ref[...]], 1)
    o_ref[:, :LANE] = dot(d, qk).astype(BF16)
    o_ref[:, LANE:] = dot(d, v_ref[...]).astype(BF16)
    out_ref[...] = wo_ref[...]


def bulk_body(g_ref, wg_ref, wu_ref, wd_ref, o_ref):
    d = diagonal(g_ref[...])
    units = wg_ref.shape[1]
    groups = -(-units // LANE)
    fill = jnp.zeros((wg_ref.shape[0], groups * LANE - units), BF16)
    gate = jnp.concatenate([dot(d, wg_ref[...]).astype(BF16), fill], 1)
    up = jnp.concatenate([dot(d, wu_ref[...]).astype(BF16), fill], 1)
    for b in range(groups):
        here = slice(b * LANE, (b + 1) * LANE)
        o_ref[:, 2 * b * LANE : (2 * b + 1) * LANE] = gate[:, here]
        o_ref[:, (2 * b + 1) * LANE : (2 * b + 2) * LANE] = up[:, here]
    o_ref[:, 2 * groups * LANE : 3 * groups * LANE] = jnp.concatenate([wd_ref[...], fill], 1)


def turn(info, t, keep_ref, send_ref):
    core = info[2, 2]
    for i in range(t.shape[0] // LANE):
        here = pl.multiple_of(LANE * i + 64 * core, 64)
        there = pl.multiple_of(LANE * i + 64 - 64 * core, 64)
        keep_ref[64 * i : 64 * i + 64, :] = t[pl.ds(here, 64), :].astype(BF16)
        send_ref[64 * i : 64 * i + 64, :] = t[pl.ds(there, 64), :].astype(BF16)


def order_body(axis, info, a, b, c, d, o_ref):
    for k, part in enumerate((a, b, c, d)):
        o_ref[back(info[2, axis], k)] = part[...]


def slot_body(info, value_ref, all_ref, keep_ref, send_ref, t):
    for k in range(4):
        at = pl.multiple_of(32 * back(info[2, 3], k), 32)
        for row in range(2):
            here = slice(64 * k + 32 * row, 64 * k + 32 * row + 32)
            all_ref[here, :] = value_ref[row, pl.ds(at, 32), :]
        t[:, 64 * k : 64 * k + 64] = all_ref[64 * k : 64 * k + 64, :].astype(F32).T
    turn(info, t, keep_ref, send_ref)


def turn_body(info, a, b, c, d, keep_ref, send_ref, t):
    for k, part in enumerate((a, b, c, d)):
        t[:, 64 * k : 64 * k + 64] = part[...].astype(F32).T
    turn(info, t, keep_ref, send_ref)


def slotted(info, value):
    d = value.shape[-1]
    half = out((d // 2, 256), BF16)
    return call(
        "slot", slot_body, [out((256, d), BF16), half, half], info, value, kinds="s",
        scratch=[pltpu.VMEM((d, 256), F32)],
    )


def picks():
    lane = lax.broadcasted_iota(jnp.int32, (1, FT), 1)
    head = sum((lane >= FW * h).astype(jnp.int32) for h in range(1, HH))
    e = lane - FW * head
    n = FDIM + 1
    s = sum((e >= n * m).astype(jnp.int32) for m in range(1, 9))
    a = e - n * s
    b = a + s
    b = jnp.where(b >= n, b - n, b)
    used = e < 9 * n
    rows = lax.broadcasted_iota(jnp.int32, (HF, FT), 0)

    def matrix(i):
        at = jnp.where(used & (i < FDIM), FDIM * head + i, -1)
        return jnp.where(rows == at, 1.0, 0.0).astype(BF16)

    one_a = jnp.where(used & (a == FDIM), 1.0, 0.0)
    one_b = jnp.where(used & (b == FDIM), 1.0, 0.0)
    plain = jnp.where(a == b, 1.0 / 32, 1.0 / 16)
    weight = jnp.where(one_a + one_b == 2.0, 1.0, jnp.where(one_a + one_b == 1.0, 0.25, plain))
    return matrix(a), matrix(b), one_a, one_b, weight


def factors(u, table):
    pick_a, pick_b, one_a, one_b, _ = table
    return dot(u, pick_a) + one_a, dot(u, pick_b) + one_b


def back_to(dphi, fa, fb, table):
    return dot_nt((dphi * fb).astype(BF16), table[0]) + dot_nt((dphi * fa).astype(BF16), table[1])


def pack_state(state, count, extra=None):
    parts = [
        state[h * FW : (h + 1) * FW, h * LANE : (h + 1) * LANE].astype(BF16) for h in range(HH)
    ]
    high = count.astype(BF16).astype(F32)
    low = count - high
    rows = lax.broadcasted_iota(jnp.int32, (16, LANE), 0)
    tile = jnp.zeros((16, LANE), F32)
    for j in range(FT // LANE):
        tile = jnp.where(rows == j, high[:, j * LANE : (j + 1) * LANE], tile)
        tile = jnp.where(rows == j + 5, low[:, j * LANE : (j + 1) * LANE], tile)
    if extra is not None:
        tile = with_extra(tile, extra)
    return jnp.concatenate([*parts, tile.astype(BF16)], 0)


def with_extra(tile, extra):
    rows = lax.broadcasted_iota(jnp.int32, (16, LANE), 0)
    high = extra.astype(BF16).astype(F32)
    tile = jnp.where(rows == 10, high, tile)
    return jnp.where(rows == 11, extra - high, tile)


def extra_of(packed):
    return packed[FT + 10 : FT + 11].astype(F32) + packed[FT + 11 : FT + 12].astype(F32)


def put_packed(ref, total, extra):
    ref[:FT, :] = total[:FT].astype(BF16)
    ref[FT:, :] = with_extra(total[FT:], extra).astype(BF16)


def unpack_state(packed):
    blocks = []
    for h in range(HH):
        mine = packed[h * FW : (h + 1) * FW]
        zero = jnp.zeros_like(mine)
        blocks.append(jnp.concatenate([mine if g == h else zero for g in range(HH)], 1))
    state = jnp.concatenate(blocks, 0)
    tile = packed[FT:].astype(F32)
    lane = lax.broadcasted_iota(jnp.int32, (1, FT), 1)
    head = sum((lane >= FW * h).astype(jnp.int32) for h in range(1, HH))
    heads = lax.broadcasted_iota(jnp.int32, (8, FT), 0)
    counts = []
    for first in (0, 5):
        line = jnp.concatenate([tile[first + j : first + j + 1] for j in range(5)], 1)
        counts.append(jnp.where(head == heads, jnp.broadcast_to(line, (8, FT)), 0.0).astype(BF16))
    return state, counts[0], counts[1]


def split_rows(info, row, packed, keep_ref, send_ref):
    @pl.when(info[2, 2] == row)
    def _():
        keep_ref[...] = packed

    @pl.when(info[2, 2] != row)
    def _():
        send_ref[...] = packed


def assemble(axis, info, blocks, w_ref, sems):
    core = info[2, 2]
    copies = []
    for k in range(4):
        there = back(info[2, axis], k)
        for i, owner in enumerate((core, 1 - core)):
            target = w_ref.at[there, :, owner] if axis == 0 else w_ref.at[:, there, owner]
            copies.append(pltpu.make_async_copy(blocks[4 * i + k], target, sems.at[len(copies)]))
            copies[-1].start()
    return copies


def assembled(copies, w_ref):
    for copy in copies:
        copy.wait()
    return w_ref[...].reshape(-1, w_ref.shape[-1])


def project_body(info, x_ref, *refs):
    blocks, (p_ref, r_ref, keep_ref, send_ref, w_ref, sems) = refs[:8], refs[8:]
    copies = assemble(1, info, blocks, w_ref, sems)
    x = x_ref[...]
    xf = x.astype(F32)
    r = lax.rsqrt(jnp.mean(xf * xf, -1, keepdims=True) + EPS)
    r_ref[...] = r
    table = picks()
    p = (dot(x, assembled(copies, w_ref)) * r).astype(BF16)
    p_ref[...] = p
    for row in range(2):
        mine = row_of(p, row)
        k, v = mine[:, HF : 2 * HF], mine[:, 2 * HF :]
        tail_doc = doc_at(info, row, block_start(info) + LANE - 1)
        tail = (doc_of(info, row, positions(info, 0)) == tail_doc).astype(F32)
        fa, fb = factors(k, table)
        phi = (fa * fb * tail).astype(BF16)
        count = dot(jnp.ones((8, LANE), BF16), phi)[0:1]
        split_rows(info, row, pack_state(dot_tn(phi, v), count), keep_ref, send_ref)


def chip_body(backward, info, keep_ref, recv_ref, o_ref):
    c = info[2, 2]
    base = block_start(info, c=0)
    keep, recv = keep_ref[...].astype(F32), recv_ref[...].astype(F32)
    is_zero = jnp.where(c == 0, 1.0, 0.0)
    zero = is_zero * keep + (1.0 - is_zero) * recv
    one = is_zero * recv + (1.0 - is_zero) * keep
    if backward:
        total = zero + same(doc_at(info, c, base), doc_at(info, c, base + LANE)) * one
    else:
        last, end = doc_at(info, c, base + LANE - 1), doc_at(info, c, base + 2 * LANE - 1)
        total = one + same(last, end) * zero
    put_packed(o_ref, total, extra_of(keep) + extra_of(recv))


def line_body(backward, info, t0, t1, t2, t3, o_ref):
    c, y = info[2, 2], info[2, 1]
    start = block_start(info, y=0, c=0)
    whole = doc_at(info, c, start if backward else start + 8 * LANE - 1)
    total = jnp.zeros(o_ref.shape, F32)
    extra = jnp.zeros((1, LANE), F32)
    for k, t in enumerate((t0, t1, t2, t3)):
        there = start + back(y, k) * 2 * LANE
        there = there if backward else there + 2 * LANE - 1
        value = t[...].astype(F32)
        total += same(doc_at(info, c, there), whole) * value
        extra += extra_of(value)
    put_packed(o_ref, total, extra)


def enter_body(backward, info, keep, recv, t1, t2, t3, s0, s1, s2, s3, mine_ref, send_ref):
    x, y, c = info[2, 0], info[2, 1], info[2, 2]
    base = block_start(info, c=0)
    here = doc_at(info, c, base + 2 * LANE - 1 if backward else base)
    total = jnp.zeros(keep.shape, F32)
    extra = extra_of(s0)
    for k, (t, s) in enumerate(((t1, s1), (t2, s2), (t3, s3)), 1):
        there_y, there_x = back(y, k), back(x, k)
        at_y = block_start(info, y=there_y, c=0)
        at_x = block_start(info, x=there_x, y=0, c=0)
        if backward:
            use_y = same(doc_at(info, c, at_y), here) * (there_y > y).astype(F32)
            use_x = same(doc_at(info, c, at_x), here) * (there_x > x).astype(F32)
        else:
            use_y = same(doc_at(info, c, at_y + 2 * LANE - 1), here) * (there_y < y).astype(F32)
            use_x = same(doc_at(info, c, at_x + 8 * LANE - 1), here) * (there_x < x).astype(F32)
        total += use_y * t[...].astype(F32) + use_x * s[...].astype(F32)
        extra += extra_of(s)
    is_zero = jnp.where(c == 0, 1.0, 0.0)
    if backward:
        one = is_zero * recv[...].astype(F32) + (1.0 - is_zero) * keep[...].astype(F32)
        last = doc_at(info, c, base + LANE - 1)
        for_zero = same(doc_at(info, c, base + LANE), last) * one + same(here, last) * total
        for_one = total
    else:
        zero = is_zero * keep[...].astype(F32) + (1.0 - is_zero) * recv[...].astype(F32)
        begun = doc_at(info, c, base + LANE)
        for_zero = total
        for_one = same(doc_at(info, c, base + LANE - 1), begun) * zero + same(here, begun) * total
    put_packed(mine_ref, is_zero * for_zero + (1.0 - is_zero) * for_one, extra)
    put_packed(send_ref, is_zero * for_one + (1.0 - is_zero) * for_zero, extra)


def shift(value, axis, k, name):
    n = 2 if axis == "c" else 4
    with jax.named_scope(name):
        return lax.ppermute(value, axis, [(i, (i + k) % n) for i in range(n)])


def around(value, axis, name):
    return [value] + [shift(value, axis, k, name) for k in (1, 2, 3)]


def ordered(name, info, parts, axis, after=()):
    return call(
        name + "_order", lambda *refs: order_body("xy".index(axis), *refs),
        [out((4, *parts[0].shape), parts[0].dtype)], info, *parts, kinds="s", after=after,
    )


def to_slots(parts, name, axis="z", way=-1):
    return [parts[0]] + [shift(parts[k], axis, way * k, name) for k in (1, 2, 3)]


def chip_state(info, keep, send, backward):
    tag = "back_" if backward else ""
    recv = shift(send, "c", 1, tag + "cores")
    (chip,) = call(
        tag + "chip", lambda *refs: chip_body(backward, *refs), [out((SROWS, LANE), BF16)],
        info, keep, recv, kinds="s",
    )
    return recv, chip


def line_and_sum_body(backward, info, t0, t1, t2, t3, far_ref, got_ref, o_ref, sum_ref):
    line_body(backward, info, t0, t1, t2, t3, o_ref)
    sum_ref[...] = (far_ref[...].astype(F32) + got_ref[64:, :].astype(F32)).astype(BF16)


def scan_states(info, chip, backward, after, extra=(), through=()):
    tag = "back_" if backward else ""
    body = line_and_sum_body if extra else line_body
    outs = [out((SROWS, LANE), BF16)] + [out(a.shape, a.dtype) for a in extra[:1]]
    t = around(chip, "y", tag + "scan_y")
    line, *more = call(
        tag + "line", lambda *refs: body(backward, *refs), outs,
        info, *t, *extra, kinds="s", after=after, through=through,
    )
    s = around(line, "x", tag + "scan_x")
    return t, line, s, *more


def scan_end(info, keep, recv, t, s, backward, after=()):
    packed, tag = out((SROWS, LANE), BF16), "back_" if backward else ""
    mine, other = call(
        tag + "enter", lambda *refs: enter_body(backward, *refs), [packed, packed],
        info, keep, recv, *t[1:], *s, kinds="s", after=after,
    )
    return mine, shift(other, "c", 1, tag + "given")


def entered(info, row, mine, other):
    return jnp.where(info[2, 2] == row, mine[...], other[...])


def pairs(info, row):
    at_i, at_j = positions(info, 0), positions(info, 1)
    doc_i, doc_j = doc_of(info, row, at_i), doc_of(info, row, at_j)
    return (doc_i == doc_j) & (at_i >= at_j)


def carried(info, row):
    doc_i = doc_of(info, row, positions(info, 0))
    return (doc_i == doc_at(info, row, block_start(info))).astype(F32)


def by_head(q):
    lanes = lax.broadcasted_iota(jnp.int32, q.shape, 1) // FDIM
    return jnp.concatenate([jnp.where(lanes == h, q, jnp.zeros_like(q)) for h in range(HH)], 0)


def columns(parts, fill):
    lanes = lax.broadcasted_iota(jnp.int32, (parts[0].shape[0], 8), 1)
    total = jnp.full((parts[0].shape[0], 8), fill, F32)
    for h, part in enumerate(parts):
        total = jnp.where(lanes == h, part, total)
    return total


def mix_here_body(info, p_ref, num_ref, den_ref, phi_ref):
    table = picks()
    p = p_ref[...]
    for row in range(2):
        line = row_of(p, row)
        q, k, v = line[:, :HF], line[:, HF : 2 * HF], line[:, 2 * HF :]
        ok = pairs(info, row)
        s = dot_nt(by_head(q), k) * 0.25
        here = slice(row * LANE, (row + 1) * LANE)
        dens = []
        for h in range(HH):
            cols = slice(h * LANE, (h + 1) * LANE)
            sh = s[cols]
            kap = jnp.where(ok, 1.0 + sh + 0.5 * sh * sh, 0.0)
            dens.append(jnp.sum(kap, -1, keepdims=True))
            num_ref[here, cols] = dot(kap.astype(BF16), v[:, cols])
        den_ref[here, :] = columns(dens, 1.0)
        fa, fb = factors(q, table)
        phi_ref[here, :] = (fa * fb * (table[4] * carried(info, row))).astype(BF16)


def mix_body(info, num_ref, den_ref, phi_ref, mine, other, *refs):
    blocks, (mixed_ref, all_den_ref, b0, b1, b2, b3, wo, sems) = refs[:8], refs[8:]
    copies = assemble(0, info, blocks, wo, sems)
    for row in range(2):
        here = slice(row * LANE, (row + 1) * LANE)
        state, high, low = unpack_state(entered(info, row, mine, other))
        phi = phi_ref[here, :]
        num = num_ref[here, :] + dot(phi, state)
        den = den_ref[here, :] + dot_nt(phi, high) + dot_nt(phi, low)
        attn = [num[:, h * LANE : (h + 1) * LANE] / den[:, h : h + 1] for h in range(HH)]
        put_row(mixed_ref, row, jnp.concatenate(attn, 1).astype(BF16))
        all_den_ref[here, :] = den
    branch = dot_nt(mixed_ref[...], assembled(copies, wo))
    for s, b in enumerate((b0, b1, b2, b3)):
        b[...] = branch[64 * s : 64 * s + 64].astype(BF16)


def unmix_state_body(info, den_ref, phi_ref, mixed_ref, m0, m1, m2, m3, *refs):
    blocks, (dnum_ref, dden_ref, keep_ref, send_ref, dm, wo, sems) = refs[:8], refs[8:]
    copies = assemble(0, info, blocks, wo, sems)
    for s, m in enumerate((m0, m1, m2, m3)):
        dm[64 * s : 64 * s + 64, :] = m[...]
    lanes = lax.broadcasted_iota(jnp.int32, (256, 8), 1)
    total = jnp.sum(jnp.where(lanes < HH, den_ref[...], 0.0), keepdims=True)
    total = jnp.broadcast_to(total, (1, LANE))
    mixed = mixed_ref[...]
    lane = lax.broadcasted_iota(jnp.int32, (1, FT), 1)
    head = sum((lane >= FW * h).astype(jnp.int32) for h in range(1, HH))
    heads = lax.broadcasted_iota(jnp.int32, (8, FT), 0)
    core = info[2, 2]
    d_attn = dot(dm[...], assembled(copies, wo))
    for row in range(2):
        here = slice(row * LANE, (row + 1) * LANE)
        da, at, den = row_of(d_attn, row), row_of(mixed, row).astype(F32), den_ref[here, :]
        dnums, ddens = [], []
        for h in range(HH):
            cols = slice(h * LANE, (h + 1) * LANE)
            dnum = da[:, cols] / den[:, h : h + 1]
            ddens.append(-jnp.sum(dnum * at[:, cols], -1, keepdims=True))
            dnums.append(dnum)
        dnum = jnp.concatenate(dnums, 1).astype(BF16)
        dden = columns(ddens, 0.0)
        dnum_ref[here, :] = dnum
        dden_ref[here, :] = dden
        phi = phi_ref[here, :]
        dcount = jnp.where(head == heads, dot_tn(dden.astype(BF16), phi), 0.0)
        extra = jnp.where(core == row, 0.0, 1.0) * total
        packed = pack_state(dot_tn(phi, dnum), jnp.sum(dcount, 0, keepdims=True), extra)
        split_rows(info, row, packed, keep_ref, send_ref)


def unmix_here_body(
    info, p_ref, dnum_ref, dden_ref, mine, other, m0, m1, m2, m3, dp_ref, keep_ref, send_ref, t
):
    turn_body(info, m0, m1, m2, m3, keep_ref, send_ref, t)
    table = picks()
    p = p_ref[...]
    for row in range(2):
        here = slice(row * LANE, (row + 1) * LANE)
        line = row_of(p, row)
        q, k, v = line[:, :HF], line[:, HF : 2 * HF], line[:, 2 * HF :]
        ok = pairs(info, row)
        q4 = by_head(q)
        s = dot_nt(q4, k) * 0.25
        dnum, dden = dnum_ref[here, :], dden_ref[here, :]
        gs, dvs = [], []
        for h in range(HH):
            cols = slice(h * LANE, (h + 1) * LANE)
            sh = s[cols]
            kap = jnp.where(ok, 1.0 + sh + 0.5 * sh * sh, 0.0)
            g = (dot_nt(dnum[:, cols], v[:, cols]) + dden[:, h : h + 1]) * (1.0 + sh) * 0.25
            gs.append(jnp.where(ok, g, 0.0).astype(BF16))
            dvs.append(dot_tn(kap.astype(BF16), dnum[:, cols]))
        g4 = jnp.concatenate(gs, 0)
        dk = dot_tn(g4, q4)
        dq4 = dot(g4, k)
        lanes = lax.broadcasted_iota(jnp.int32, (LANE, HF), 1) // FDIM
        dq = jnp.zeros((LANE, HF), F32)
        for h in range(HH):
            dq += jnp.where(lanes == h, dq4[h * LANE : (h + 1) * LANE], 0.0)
        state, high, low = unpack_state(entered(info, row, mine, other))
        dden_low = dden.astype(BF16)
        dphi = dot_nt(dnum, state) + dot(dden_low, high) + dot(dden_low, low)
        fa, fb = factors(q, table)
        dq += back_to(dphi * (table[4] * carried(info, row)), fa, fb, table)
        put_row(dp_ref, row, jnp.concatenate([dq, dk, *dvs], 1))


def unproject_body(info, p_ref, dp_ref, mine, other, r_ref, *refs):
    blocks, (gp_ref, e0, e1, e2, e3, low_ref, w_ref, sems) = refs[:8], refs[8:]
    copies = assemble(1, info, blocks, w_ref, sems)
    p, dp = p_ref[...], dp_ref[...]
    table = picks()
    for row in range(2):
        line, dline = row_of(p, row), row_of(dp, row)
        k, v = line[:, HF : 2 * HF], line[:, 2 * HF :]
        tail_doc = doc_at(info, row, block_start(info) + LANE - 1)
        tail = (doc_of(info, row, positions(info, 0)) == tail_doc).astype(F32)
        fa, fb = factors(k, table)
        state, high, low = unpack_state(entered(info, row, mine, other))
        ones = jnp.ones((LANE, 8), BF16)
        dphi = (dot_nt(v, state) + dot(ones, high) + dot(ones, low)) * tail
        dk = dline[:, HF : 2 * HF] + back_to(dphi, fa, fb, table)
        dv = dline[:, 2 * HF :] + dot((fa * fb * tail).astype(BF16), state)
        put_row(low_ref, row, jnp.concatenate([dline[:, :HF], dk, dv], 1).astype(BF16))
    d = low_ref[...]
    gp_ref[...] = (d.astype(F32) * r_ref[...]).astype(BF16)
    e = dot_nt(d, assembled(copies, w_ref))
    for s, b in enumerate((e0, e1, e2, e3)):
        b[...] = e[64 * s : 64 * s + 64].astype(BF16)


def middle_body(x_ref, a, b, c, d, middle_ref, low_ref):
    u = x_ref[:64, :].astype(F32)
    for part in (a, b, c, d):
        u += part[...].astype(F32)
    middle_ref[...] = u
    low_ref[...] = (u * lax.rsqrt(jnp.mean(u * u, -1, keepdims=True) + EPS)).astype(BF16)


def norm_back(base_ref, u_ref, parts, full_ref, low_ref):
    u, e = u_ref[:64, :].astype(F32), summed(parts)
    r = lax.rsqrt(jnp.mean(u * u, -1, keepdims=True) + EPS)
    slope = jnp.mean(e * u, -1, keepdims=True)
    total = base_ref[:64, :].astype(F32) + r * e - u * (r * r * r * slope)
    if full_ref is not None:
        full_ref[...] = total
    low_ref[...] = total.astype(BF16)


def norm_back_body(base_ref, u_ref, a, b, c, d, full_ref, low_ref):
    norm_back(base_ref, u_ref, (a, b, c, d), full_ref, low_ref)


def last_body(base_ref, x_ref, e0, e1, e2, e3, middle_ref, keep_ref, got_ref, far_ref, o_ref):
    norm_back(base_ref, x_ref, (e0, e1, e2, e3), None, o_ref.at[:64])
    o_ref[64:, :] = (middle_ref[...] + summed((keep_ref, got_ref.at[:64], far_ref))).astype(BF16)


def place_body(info, a, b, c, d, grad_ref, out_ref):
    for k, part in enumerate((a, b, c, d)):
        at = pl.multiple_of(32 * back(info[2, 3], k), 32)
        for row in range(2):
            grad_ref[row, pl.ds(at, 32), :] = part[32 * row : 32 * row + 32, :]
            out_ref[row, pl.ds(at, 32), :] = part[64 + 32 * row : 96 + 32 * row, :]


def rows_in(bulk, first, width, w, sems, parts):
    step = w.shape[0] // parts
    copies = [
        pltpu.make_async_copy(
            bulk.at[pl.ds(step * k, step), pl.ds(first, width)],
            w.at[pl.ds(step * k, step), :],
            sems.at[k],
        )
        for k in range(parts)
    ]
    for copy in copies:
        copy.start()
    return copies


def d_hidden_body(dy_ref, bulk, o_ref, w, sems):
    units = w.shape[1]
    parts = sems.shape[0]
    step = w.shape[0] // parts
    for k, copy in enumerate(rows_in(bulk, 2 * units, units, w, sems, parts)):
        copy.wait()
        here = slice(step * k, step * (k + 1))
        part = dot(dy_ref[:, here], w[here, :])
        if k == 0:
            o_ref[...] = part
        else:
            o_ref[...] += part


def ffn_body(
    info, u0, u1, u2, u3, dh_ref, bulk,
    gu_ref, hid_ref, keep_ref, send_ref, e0, e1, e2, e3, u, w, t, sems,
):
    core = info[2, 2]
    pair = 2 * LANE
    groups = w.shape[1] // pair

    def copy(b):
        here = pl.ds(pl.multiple_of(b * pair, pair), pair)
        return pltpu.make_async_copy(bulk.at[:, here], w.at[:, here], sems.at[b])

    for b in range(groups):
        copy(b).start()
    for s, part in enumerate((u0, u1, u2, u3)):
        u[64 * s : 64 * s + 64, :] = part[...]

    def forward(b, carry):
        copy(b).wait()
        here = pl.ds(pl.multiple_of(b * pair, pair), pair)
        units = pl.ds(pl.multiple_of(b * LANE, LANE), LANE)
        pre = dot(u[...], w[:, here])
        d_hidden = dh_ref[:, units]
        gate, up = pre[:, :LANE], pre[:, LANE:]
        sigma = 1.0 / (1.0 + jnp.exp(-gate))
        silu = gate * sigma
        hid_ref[:, units] = (silu * up).astype(BF16)
        d_gate = d_hidden * up * (sigma + silu * (1.0 - sigma))
        gu_ref[:, here] = jnp.concatenate([d_gate, d_hidden * silu], 1).astype(BF16)
        return carry

    lax.fori_loop(0, groups, forward, 0)

    def backward(n, carry):
        here = pl.ds(pl.multiple_of(n * pair, pair), pair)
        e = dot_nt(gu_ref[...], w[here, :]).astype(BF16)
        for s, ref in enumerate((e0, e1, e2, e3)):
            ref[:, here] = e[64 * s : 64 * s + 64]
        t[...] = u[:, here].astype(F32).T
        for i in range(pair // LANE):
            at = pl.ds(pl.multiple_of(n * LANE + 64 * i, 64), 64)
            mine = pl.ds(pl.multiple_of(LANE * i + 64 * core, 64), 64)
            other = pl.ds(pl.multiple_of(LANE * i + 64 - 64 * core, 64), 64)
            keep_ref[at, :] = t[mine, :].astype(BF16)
            send_ref[at, :] = t[other, :].astype(BF16)
        return carry

    lax.fori_loop(0, w.shape[0] // pair, backward, 0)


def down_body(info, hid_ref, bulk, near_ref, keep_ref, far_ref, w, sems):
    units = w.shape[1]
    parts = sems.shape[0]
    step = w.shape[0] // parts
    even = info[2, 3] % 2 == 0
    for k, copy in enumerate(rows_in(bulk, 2 * units, units, w, sems, parts)):
        copy.wait()
        here = slice(step * k, step * (k + 1))
        f = dot_nt(hid_ref[...], w[here, :]).astype(BF16)
        one, three = f[64:128], f[192:]
        keep_ref[:, here] = f[:64]
        near_ref[:64, here] = jnp.where(even, three, one)
        near_ref[64:, here] = f[128:192]
        far_ref[:, here] = jnp.where(even, one, three)


def ffn_grad_body(uk, ur, yk, yr, gu_own, gu_other, hid_own, hid_other, o_ref, lhs):
    step = pl.program_id(0)

    def fill(first, second):
        lhs[:, :256] = first[...]
        lhs[:, 256:] = second[...]

    def product(own, other):
        both = jnp.concatenate([own[...], other[...]], 0)
        for m in range(lhs.shape[0] // 256):
            here = slice(256 * m, 256 * (m + 1))
            o_ref[here, :] = dot(lhs[here, :], both).astype(BF16)

    @pl.when(step == 0)
    def _():
        fill(uk, ur)

    @pl.when(step == 2)
    def _():
        fill(yk, yr)

    @pl.when(step < 2)
    def _():
        product(gu_own, gu_other)

    @pl.when(step == 2)
    def _():
        product(hid_own, hid_other)


def ffn_grads(uk, ur, yk, yr, gu, gu_other, hid, hid_other):
    rows, tokens = uk.shape
    units = hid.shape[1]
    whole = pl.BlockSpec((rows, tokens), lambda b: (0, 0))
    gu_spec = pl.BlockSpec((tokens, units), lambda b: (0, jnp.minimum(b, 1)))
    hid_spec = pl.BlockSpec((tokens, units), lambda b: (0, 0))
    with jax.named_scope("ffn_grad"):
        return pl.pallas_call(
            ffn_grad_body,
            grid=(3,),
            out_shape=pltpu.HBM((rows, 3 * units), BF16),
            in_specs=[whole] * 4 + [gu_spec] * 2 + [hid_spec] * 2,
            out_specs=pl.BlockSpec((rows, units), lambda b: (0, b)),
            scratch_shapes=[pltpu.VMEM((rows, 2 * tokens), BF16)],
            compiler_params=pltpu.CompilerParams(vmem_limit_bytes=28 * 2**20),
            cost_estimate=pl.CostEstimate(
                flops=12 * rows * tokens * units, bytes_accessed=6 * rows * units, transcendentals=0
            ),
        )(uk, ur, yk, yr, gu, gu_other, hid, hid_other)


def grad_body(axis, info, lk, lr, a_own, a_other, o0, o1, o2, o3, full):
    full[...] = (dot(lk[...], a_own[...]) + dot(lr[...], a_other[...])).astype(BF16)
    place = info[2, axis]
    for k, o in enumerate((o0, o1, o2, o3)):
        there = (place + k) % 4
        for i in range(4):
            chip = there * 4 + i if axis == 0 else i * 4 + there
            o[i] = full[pl.ds(pl.multiple_of(chip * 64, 64), 64), :]


def fold_body(info, *refs):
    ins, outs, results = refs[:4], refs[4:8], refs[8:]
    for k, o in enumerate(results):
        there = (info[2, 0] + k) % 4
        sides = [sum(part[there].astype(F32) for part in parts) for parts in (ins, outs)]
        o[...] = jnp.concatenate(sides, 1).astype(BF16)


def grads_in_parts(name, info, lk, lr, own, other, axis, after=()):
    n = own.shape[1]
    return call(
        name, lambda *refs: grad_body(axis, *refs),
        [out((4, 64, n), BF16)] * 4,
        info, lk, lr, own, other, kinds="s", after=after,
        scratch=[pltpu.VMEM((lk.shape[0], n), BF16)],
        flops=4 * lk.shape[0] * lk.shape[1] * n,
    )


def summed(parts):
    return sum(part[...].astype(F32) for part in parts)


def row_sums(value):
    total = jnp.broadcast_to(jnp.sum(value, 1, keepdims=True), (64, LANE))
    wide = jnp.concatenate([total, jnp.zeros((64, LANE), F32)], 0)
    return wide.T[0:1]


def finish_ffn_body(s_ref, wg_ref, wu_ref, g_ref, gate_ref, up_ref, down_ref, gain_ref):
    units = gate_ref.shape[1]
    g = column(g_ref[...])
    groups = s_ref.shape[1] // (3 * LANE)

    def side(k):
        at = [(2 * b + k) * LANE for b in range(groups)]
        return jnp.concatenate([s_ref[:, i : i + LANE] for i in at], 1)[:, :units].astype(F32)

    gate, up = side(0), side(1)
    gain = row_sums(gate * wg_ref[...].astype(F32) + up * wu_ref[...].astype(F32))
    gain_ref[...] = jnp.broadcast_to(gain, gain_ref.shape)
    gate_ref[...] = gate * g
    up_ref[...] = up * g
    down_ref[...] = s_ref[:, 2 * groups * LANE : 2 * groups * LANE + units].astype(F32)


def finish_mix_body(
    s0, s1, s2, s3, wq_ref, wk_ref, wv_ref, g_ref, gain2_ref, den0, den1,
    q_ref, k_ref, v_ref, out_ref, message_ref,
):
    g = column(g_ref[...])
    total = summed((s0, s1, s2, s3))
    cols = total.shape[1] - out_ref.shape[1]
    grads = total[:, :cols]
    out_ref[...] = total[:, cols:]
    w = jnp.concatenate([wq_ref[...], wk_ref[...], wv_ref[...]], 1).astype(F32)
    rows = lax.broadcasted_iota(jnp.int32, (8, LANE), 0)
    den = extra_of(den0) + extra_of(den1)
    message = jnp.where(rows == 0, row_sums(grads * w), 0.0)
    message = jnp.where(rows == 1, gain2_ref[0:1, :], message)
    message_ref[...] = jnp.where(rows == 2, den, message)
    scaled = grads * g
    q_ref[...] = scaled[:, :HF]
    k_ref[...] = scaled[:, HF : 2 * HF]
    v_ref[...] = scaled[:, 2 * HF :]


def on_device(
    tokens,
    doc_lengths,
    norm_gain,
    w_query,
    w_key,
    w_value,
    w_out,
    ffn_gain,
    w_gate,
    w_up,
    w_down,
    out_grad,
):
    x, y, c, z = (lax.axis_index(a) for a in ("x", "y", "c", "z"))
    ends = jnp.cumsum(doc_lengths, -1).astype(jnp.int32)
    places = jnp.stack([x, y, c, z, x, x, x, x]).astype(jnp.int32)
    info = jnp.concatenate([ends, places[None]], 0)
    d = tokens.shape[-1]
    width = w_out.shape[0]
    units = -(-w_gate.shape[1] // LANE) * LANE
    cols = 2 * HF + w_value.shape[1]
    piece = out((64, d), BF16)
    piece_full = out((64, d), F32)
    state = out((SROWS, LANE), BF16)

    early, early_out = call(
        "early", early_body, [out((64, cols), BF16), out((64, width), BF16)],
        norm_gain[None], w_query, w_key, w_value, w_out.T, kinds="ddddd",
    )
    out_ys = around(early_out, "y", "out_y")
    (line,) = ordered("in_x", info, around(early, "x", "in_x"), "x", out_ys[1:3])
    w_in = around(line, "y", "in_y")
    (out_line,) = ordered("out_y", info, out_ys, "y", [line])
    w_mix = around(out_line, "x", "out_x")
    x_all, xk, x_send = slotted(info, tokens)
    dy_all, yk, y_send = slotted(info, out_grad)
    xr, yr = shift(x_send, "c", 1, "x_cores"), shift(y_send, "c", 1, "y_cores")
    (bulk_own,) = call(
        "bulk", bulk_body, [out((64, 3 * units), BF16)],
        ffn_gain[None], w_gate, w_up, w_down.T, kinds="dddd", after=[*w_in[1:], *w_mix[1:], xk, yk],
    )
    bulk = lax.all_gather(bulk_own, BLK, axis=0, tiled=True)
    w_in += [shift(g, "c", 1, "in_cores") for g in w_in]
    w_mix += [shift(g, "c", 1, "out_cores") for g in w_mix]


    p, r, keep, send = call(
        "project", project_body,
        [out((256, cols), BF16), out((256, 1), F32), state, state],
        info, x_all, *w_in, kinds="sv" + "a" * 8, after=[xr, yr],
        scratch=[pltpu.VMEM((4, 4, 2, 64, cols), BF16), pltpu.SemaphoreType.DMA((8,))],
        flops=2 * 256 * d * cols, limit=20,
    )
    num_here, den_here, phi = call(
        "mix_here", mix_here_body,
        [out((256, width), F32), out((256, 8), F32), out((256, FT), BF16)],
        info, p, kinds="s", flops=2 * 256 * d * 64,
    )
    recv, chip = chip_state(info, keep, send, False)
    t, _, s = scan_states(info, chip, False, [den_here])
    mine, other = scan_end(info, keep, recv, t, s, False)
    mixed, den, *branch = call(
        "mix", mix_body,
        [out((256, width), BF16), out((256, 8), F32)] + [piece] * 4,
        info, num_here, den_here, phi, mine, other, *w_mix, kinds="svvvvv" + "a" * 8,
        scratch=[pltpu.VMEM((4, 4, 2, 64, width), BF16), pltpu.SemaphoreType.DMA((8,))],
        flops=2 * 256 * d * width, limit=16,
    )
    (d_hidden,) = call(
        "d_hidden", d_hidden_body, [out((256, units), F32)], dy_all, bulk, kinds="vh",
        scratch=[pltpu.VMEM((d, units), BF16), pltpu.SemaphoreType.DMA((4,))],
        flops=2 * 256 * d * units, limit=16,
    )
    middle, u2 = call("middle", middle_body, [piece_full, piece], x_all, *to_slots(branch, "branch_sum"))
    us = around(u2, "z", "u_all")
    mixed_other = shift(mixed, "c", 1, "mixed_cores")
    half = out((d // 2, 256), BF16)
    gu, hid, uk, u_send, *e_parts = call(
        "ffn", ffn_body,
        [out((256, 2 * units), BF16), out((256, units), BF16), half, half] + [piece] * 4,
        info, *us, d_hidden, bulk, kinds="svvvvvh", after=[mixed_other],
        scratch=[
            pltpu.VMEM((256, d), BF16), pltpu.VMEM((d, 2 * units), BF16),
            pltpu.VMEM((2 * LANE, 256), F32), pltpu.SemaphoreType.DMA((units // LANE,)),
        ],
        flops=8 * 256 * d * units, limit=32,
    )
    ur = shift(u_send, "c", 1, "u_cores")
    ffn_rows = ffn_grads(
        uk, ur, yk, yr, gu, shift(gu, "c", 1, "gu_cores"),
        hid, shift(hid, "c", 1, "hid_cores"),
    )
    d_middle, dm, ffn_rows = call(
        "norm_back", norm_back_body, [piece_full, piece], dy_all, middle, *to_slots(e_parts, "e_sum"),
        through=[ffn_rows],
    )
    ffn_sum = lax.psum_scatter(ffn_rows, ("x", "y"), scatter_dimension=0, tiled=True)
    f_near, f_keep, f_far = call(
        "down", down_body, [out((128, d), BF16), piece, piece], info, hid, bulk, kinds="svh",
        scratch=[pltpu.VMEM((d, units), BF16), pltpu.SemaphoreType.DMA((8,))],
        flops=2 * 256 * d * units, limit=16,
    )
    dms = around(dm, "z", "dm_all")
    dnum, dden, dkeep, dsend = call(
        "unmix_state", unmix_state_body,
        [out((256, width), BF16), out((256, 8), F32), state, state],
        info, den, phi, mixed, *dms, *w_mix, kinds="s" + "v" * 7 + "a" * 8, after=[f_keep],
        scratch=[
            pltpu.VMEM((256, d), BF16), pltpu.VMEM((4, 4, 2, 64, width), BF16),
            pltpu.SemaphoreType.DMA((8,)),
        ],
        flops=2 * 256 * d * width, limit=20,
    )
    drecv, dchip = chip_state(info, dkeep, dsend, True)
    dp, mk, m_send = call(
        "unmix_here", unmix_here_body, [out((256, cols), F32), half, half],
        info, p, dnum, dden, mine, other, *dms, kinds="s", after=[dchip],
        scratch=[pltpu.VMEM((d, 256), F32)], flops=2 * 256 * d * 128,
    )
    with jax.named_scope("f_near"):
        f_got = lax.ppermute(f_near, "z", [(0, 1), (1, 0), (2, 3), (3, 2)])
    dt, _, ds, f_send, m_send = scan_states(
        info, dchip, True, [dp], (f_far, f_got), [m_send]
    )
    with jax.named_scope("f_far"):
        f_last = lax.ppermute(f_send, "z", [(0, 3), (3, 0), (1, 2), (2, 1)])
    out_parts = grads_in_parts(
        "out_grad", info, mk, shift(m_send, "c", 1, "m_cores"), mixed, mixed_other, 1
    )
    out_first = to_slots(out_parts, "out_first", "y", 1)
    dmine, dother = scan_end(info, dkeep, drecv, dt, ds, True, [out_parts[0]])

    gp, *e1 = call(
        "unproject", unproject_body,
        [out((256, cols), BF16)] + [piece] * 4,
        info, p, dp, dmine, dother, r, *w_in, kinds="svvvvv" + "a" * 8, after=[*out_first[1:]],
        scratch=[
            pltpu.VMEM((256, cols), BF16), pltpu.VMEM((4, 4, 2, 64, cols), BF16),
            pltpu.SemaphoreType.DMA((8,)),
        ],
        flops=2 * 256 * d * cols, limit=16,
    )
    in_parts = grads_in_parts("in_grad", info, xk, xr, gp, shift(gp, "c", 1, "gp_cores"), 1)
    (last,) = call(
        "last", last_body, [out((128, d), BF16)],
        d_middle, x_all, *to_slots(e1, "e1_sum"), middle, f_keep, f_got, f_last,
    )
    input_grad, block_out = call(
        "place", place_body, [out(tokens.shape, BF16)] * 2,
        info, *around(last, "z", "last_all"), kinds="s",
    )
    sums = call(
        "fold", fold_body, [out((64, cols + width), BF16)] * 4,
        info, *to_slots(in_parts, "in_first", "y", 1), *out_first, kinds="s",
    )
    g_gate, g_up, g_down, gain2 = call(
        "finish_ffn", finish_ffn_body,
        [out(w_gate.shape, F32), out(w_up.shape, F32), out(w_down.shape[::-1], F32),
         out((8, LANE), F32)],
        ffn_sum, w_gate, w_up, ffn_gain[None], kinds="dddd",
    )
    g_q, g_k, g_v, g_out, message = call(
        "finish_mix", finish_mix_body,
        [out(w_query.shape, F32), out(w_key.shape, F32), out(w_value.shape, F32),
         out(w_out.shape[::-1], F32), out((8, LANE), F32)],
        *to_slots(sums, "second", "x", 1),
        w_query, w_key, w_value, norm_gain[None], gain2, dmine, dother,
        kinds="vvvvdddd",
    )
    totals = sum(around(message, "z", "message"))
    seq = 32 * LANE
    denom_mean = totals[2, 0] / (2 * seq * HEADS * seq)
    return (
        block_out, input_grad, totals[0, :64], g_q, g_k, g_v, g_out.T, totals[1, :64],
        g_gate, g_up, g_down.T, denom_mean,
    )


def solution(mesh):
    finer = Mesh(mesh.devices.reshape(4, 4, 2, mesh.shape["head"]), ("x", "y", "c", "z"))
    placed = (
        P(None, BLK, None),
        P(),
        P(BLK),
        P(BLK, "z"),
        P(BLK, "z"),
        P(BLK, "z"),
        P("z", BLK),
        P(BLK),
        P(BLK, "z"),
        P(BLK, "z"),
        P("z", BLK),
        P(None, BLK, None),
    )
    return jax.shard_map(
        on_device,
        mesh=finer,
        in_specs=placed,
        out_specs=(
            P(None, BLK, None),
            P(None, BLK, None),
            P(BLK),
            P(BLK, "z"),
            P(BLK, "z"),
            P(BLK, "z"),
            P("z", BLK),
            P(BLK),
            P(BLK, "z"),
            P(BLK, "z"),
            P("z", BLK),
            P(),
        ),
        check_vma=False,
    )
```

```python
import math

import jax
import jax.numpy as jnp
from jax import lax
from jax.experimental import pallas as pl
from jax.experimental.pallas import tpu as pltpu
from jax.sharding import Mesh
from jax.sharding import PartitionSpec as P

HEADS = 16
FDIM = 16
EPS = 1e-05
BLK = ("x", "y", "c")
F32 = jnp.float32
BF16 = jnp.bfloat16

HH = 4
HF = HH * FDIM
FW = 160
FT = HH * FW
SROWS = FT + 16
LANE = 128
DOCS = 8


def dot(a, b):
    return jnp.dot(a, b, preferred_element_type=F32)


def dot_nt(a, b):
    return lax.dot_general(a, b, (((1,), (1,)), ((), ())), preferred_element_type=F32)


def dot_tn(a, b):
    return lax.dot_general(a, b, (((0,), (0,)), ((), ())), preferred_element_type=F32)


def out(shape, dtype):
    return jax.ShapeDtypeStruct(tuple(shape), dtype)


SPACES = {"s": pltpu.SMEM, "v": pltpu.VMEM, "h": pltpu.HBM, "d": pltpu.HBM, "a": pl.ANY}


def in_hbm(value):
    return pltpu.with_memory_space_constraint(value, pltpu.HBM)


def call(
    name, body, outs, *args, kinds="", after=(), through=(), scratch=(), flops=0, limit=12, token=False
):
    if token:
        first, outs = len(args) + len(outs), [*outs, out((8, LANE), F32)]
        inside = body

        def body(*refs):
            refs[first][...] = jnp.zeros((8, LANE), F32)
            inside(*refs[:first], *refs[first + 1 :])

    kinds = kinds + "v" * (len(args) - len(kinds))
    n_args, n_extra, n_out = len(args), len(after) + len(through), len(outs)
    staged = [k for k in range(n_args) if kinds[k] == "d"]
    places = [pltpu.VMEM(args[k].shape, args[k].dtype) for k in staged]
    if staged:
        places.append(pltpu.SemaphoreType.DMA((len(staged),)))

    def inner(*refs):
        given, results = list(refs[:n_args]), refs[n_args + n_extra :]
        own = results[n_out + len(through) :]
        held, own = own[: len(places)], own[len(places) :]
        copies = [
            pltpu.make_async_copy(given[k], held[i], held[-1].at[i]) for i, k in enumerate(staged)
        ]
        for copy in copies:
            copy.start()
        for copy in copies:
            copy.wait()
        for i, k in enumerate(staged):
            given[k] = held[i]
        body(*given, *results[:n_out], *own)

    moved = sum(math.prod(a.shape) * a.dtype.itemsize for a in (*args, *outs))
    args = [in_hbm(a) if k in "hd" else a for a, k in zip(args, kinds)]
    through = [in_hbm(a) if a.size > 2**21 else a for a in through]
    with jax.named_scope(name):
        return pl.pallas_call(
            inner,
            out_shape=list(outs) + [out(t.shape, t.dtype) for t in through],
            in_specs=[pl.BlockSpec(memory_space=SPACES[k]) for k in kinds + "a" * n_extra],
            out_specs=[pl.BlockSpec(memory_space=SPACES[k]) for k in "v" * n_out + "a" * len(through)],
            scratch_shapes=[*places, *scratch],
            input_output_aliases={
                n_args + len(after) + k: n_out + k for k in range(len(through))
            },
            compiler_params=pltpu.CompilerParams(vmem_limit_bytes=limit * 2**20),
            cost_estimate=pl.CostEstimate(flops=flops, bytes_accessed=moved, transcendentals=0),
        )(*args, *after, *through)


def doc_at(info, row, position):
    total = jnp.int32(0)
    for k in range(DOCS):
        total += (info[row, k] <= position).astype(jnp.int32)
    return total


def doc_of(info, row, where):
    total = jnp.zeros(where.shape, jnp.int32)
    for k in range(DOCS):
        total += (info[row, k] <= where).astype(jnp.int32)
    return total


def same(a, b):
    return (a == b).astype(F32)


def block_start(info, x=None, y=None, c=None):
    x = info[2, 0] if x is None else x
    y = info[2, 1] if y is None else y
    c = info[2, 2] if c is None else c
    return ((x * 4 + y) * 2 + c) * LANE


def back(place, k):
    return (place - k + 4) % 4


def positions(info, dim):
    shape = (LANE, 1) if dim == 0 else (1, LANE)
    t = lax.broadcasted_iota(jnp.int32, shape, dim)
    slot, inside = t // 32, t % 32
    return block_start(info) + 32 * ((info[2, 3] - slot + 4) % 4) + inside


def row_of(value, row):
    return jnp.concatenate([value[64 * s + 32 * row : 64 * s + 32 * row + 32] for s in range(4)], 0)


def put_row(ref, row, value):
    for s in range(4):
        ref[64 * s + 32 * row : 64 * s + 32 * row + 32, :] = value[32 * s : 32 * s + 32]


def diagonal(g):
    n = g.shape[-1]
    rows = lax.broadcasted_iota(jnp.int32, (n, n), 0)
    cols = lax.broadcasted_iota(jnp.int32, (n, n), 1)
    return jnp.where(rows == cols, jnp.broadcast_to(g.astype(F32), (n, n)), 0.0).astype(BF16)


def column(g):
    return jnp.sum(diagonal(g).astype(F32), 1, keepdims=True)


def early_body(g_ref, q_ref, k_ref, v_ref, wo_ref, o_ref, out_ref):
    d = diagonal(g_ref[...])
    qk = jnp.concatenate([q_ref[...], k_ref[...]], 1)
    o_ref[:, :LANE] = dot(d, qk).astype(BF16)
    o_ref[:, LANE:] = dot(d, v_ref[...]).astype(BF16)
    out_ref[...] = wo_ref[...]


def bulk_body(g_ref, wg_ref, wu_ref, wd_ref, o_ref):
    d = diagonal(g_ref[...])
    units = wg_ref.shape[1]
    groups = -(-units // LANE)
    fill = jnp.zeros((wg_ref.shape[0], groups * LANE - units), BF16)
    gate = jnp.concatenate([dot(d, wg_ref[...]).astype(BF16), fill], 1)
    up = jnp.concatenate([dot(d, wu_ref[...]).astype(BF16), fill], 1)
    for b in range(groups):
        here = slice(b * LANE, (b + 1) * LANE)
        o_ref[:, 2 * b * LANE : (2 * b + 1) * LANE] = gate[:, here]
        o_ref[:, (2 * b + 1) * LANE : (2 * b + 2) * LANE] = up[:, here]
    o_ref[:, 2 * groups * LANE : 3 * groups * LANE] = jnp.concatenate([wd_ref[...], fill], 1)


def turn(info, t, keep_ref, send_ref):
    core = info[2, 2]
    for i in range(t.shape[0] // LANE):
        here = pl.multiple_of(LANE * i + 64 * core, 64)
        there = pl.multiple_of(LANE * i + 64 - 64 * core, 64)
        keep_ref[64 * i : 64 * i + 64, :] = t[pl.ds(here, 64), :].astype(BF16)
        send_ref[64 * i : 64 * i + 64, :] = t[pl.ds(there, 64), :].astype(BF16)


def order_body(axis, info, a, b, c, d, o_ref):
    for k, part in enumerate((a, b, c, d)):
        o_ref[back(info[2, axis], k)] = part[...]


def slot_body(info, value_ref, all_ref, keep_ref, send_ref, t):
    for k in range(4):
        at = pl.multiple_of(32 * back(info[2, 3], k), 32)
        for row in range(2):
            here = slice(64 * k + 32 * row, 64 * k + 32 * row + 32)
            all_ref[here, :] = value_ref[row, pl.ds(at, 32), :]
        t[:, 64 * k : 64 * k + 64] = all_ref[64 * k : 64 * k + 64, :].astype(F32).T
    turn(info, t, keep_ref, send_ref)


def turn_body(info, a, b, c, d, keep_ref, send_ref, t):
    for k, part in enumerate((a, b, c, d)):
        t[:, 64 * k : 64 * k + 64] = part[...].astype(F32).T
    turn(info, t, keep_ref, send_ref)


def slotted(info, value):
    d = value.shape[-1]
    half = out((d // 2, 256), BF16)
    return call(
        "slot", slot_body, [out((256, d), BF16), half, half], info, value, kinds="s", token=True,
        scratch=[pltpu.VMEM((d, 256), F32)],
    )


def picks():
    lane = lax.broadcasted_iota(jnp.int32, (1, FT), 1)
    head = sum((lane >= FW * h).astype(jnp.int32) for h in range(1, HH))
    e = lane - FW * head
    n = FDIM + 1
    s = sum((e >= n * m).astype(jnp.int32) for m in range(1, 9))
    a = e - n * s
    b = a + s
    b = jnp.where(b >= n, b - n, b)
    used = e < 9 * n
    rows = lax.broadcasted_iota(jnp.int32, (HF, FT), 0)

    def matrix(i):
        at = jnp.where(used & (i < FDIM), FDIM * head + i, -1)
        return jnp.where(rows == at, 1.0, 0.0).astype(BF16)

    one_a = jnp.where(used & (a == FDIM), 1.0, 0.0)
    one_b = jnp.where(used & (b == FDIM), 1.0, 0.0)
    plain = jnp.where(a == b, 1.0 / 32, 1.0 / 16)
    weight = jnp.where(one_a + one_b == 2.0, 1.0, jnp.where(one_a + one_b == 1.0, 0.25, plain))
    return matrix(a), matrix(b), one_a, one_b, weight


def factors(u, table):
    pick_a, pick_b, one_a, one_b, _ = table
    return dot(u, pick_a) + one_a, dot(u, pick_b) + one_b


def back_to(dphi, fa, fb, table):
    return dot_nt((dphi * fb).astype(BF16), table[0]) + dot_nt((dphi * fa).astype(BF16), table[1])


def pack_state(state, count, extra=None):
    parts = [
        state[h * FW : (h + 1) * FW, h * LANE : (h + 1) * LANE].astype(BF16) for h in range(HH)
    ]
    high = count.astype(BF16).astype(F32)
    low = count - high
    rows = lax.broadcasted_iota(jnp.int32, (16, LANE), 0)
    tile = jnp.zeros((16, LANE), F32)
    for j in range(FT // LANE):
        tile = jnp.where(rows == j, high[:, j * LANE : (j + 1) * LANE], tile)
        tile = jnp.where(rows == j + 5, low[:, j * LANE : (j + 1) * LANE], tile)
    if extra is not None:
        tile = with_extra(tile, extra)
    return jnp.concatenate([*parts, tile.astype(BF16)], 0)


def with_extra(tile, extra):
    rows = lax.broadcasted_iota(jnp.int32, (16, LANE), 0)
    high = extra.astype(BF16).astype(F32)
    tile = jnp.where(rows == 10, high, tile)
    return jnp.where(rows == 11, extra - high, tile)


def extra_of(packed):
    return packed[FT + 10 : FT + 11].astype(F32) + packed[FT + 11 : FT + 12].astype(F32)


def put_packed(ref, total, extra):
    ref[:FT, :] = total[:FT].astype(BF16)
    ref[FT:, :] = with_extra(total[FT:], extra).astype(BF16)


def unpack_state(packed):
    blocks = []
    for h in range(HH):
        mine = packed[h * FW : (h + 1) * FW]
        zero = jnp.zeros_like(mine)
        blocks.append(jnp.concatenate([mine if g == h else zero for g in range(HH)], 1))
    state = jnp.concatenate(blocks, 0)
    tile = packed[FT:].astype(F32)
    lane = lax.broadcasted_iota(jnp.int32, (1, FT), 1)
    head = sum((lane >= FW * h).astype(jnp.int32) for h in range(1, HH))
    heads = lax.broadcasted_iota(jnp.int32, (8, FT), 0)
    counts = []
    for first in (0, 5):
        line = jnp.concatenate([tile[first + j : first + j + 1] for j in range(5)], 1)
        counts.append(jnp.where(head == heads, jnp.broadcast_to(line, (8, FT)), 0.0).astype(BF16))
    return state, counts[0], counts[1]


def split_rows(info, row, packed, keep_ref, send_ref):
    @pl.when(info[2, 2] == row)
    def _():
        keep_ref[...] = packed

    @pl.when(info[2, 2] != row)
    def _():
        send_ref[...] = packed


def assemble(axis, info, blocks, w_ref, sems):
    core = info[2, 2]
    copies = []
    for k in range(4):
        there = back(info[2, axis], k)
        for i, owner in enumerate((core, 1 - core)):
            target = w_ref.at[there, :, owner] if axis == 0 else w_ref.at[:, there, owner]
            copies.append(pltpu.make_async_copy(blocks[4 * i + k], target, sems.at[len(copies)]))
            copies[-1].start()
    return copies


def assembled(copies, w_ref):
    for copy in copies:
        copy.wait()
    return w_ref[...].reshape(-1, w_ref.shape[-1])


def project_body(info, x_ref, *refs):
    blocks, (p_ref, r_ref, keep_ref, send_ref, w_ref, sems) = refs[:8], refs[8:]
    copies = assemble(1, info, blocks, w_ref, sems)
    x = x_ref[...]
    xf = x.astype(F32)
    r = lax.rsqrt(jnp.mean(xf * xf, -1, keepdims=True) + EPS)
    r_ref[...] = r
    table = picks()
    p = (dot(x, assembled(copies, w_ref)) * r).astype(BF16)
    p_ref[...] = p
    for row in range(2):
        mine = row_of(p, row)
        k, v = mine[:, HF : 2 * HF], mine[:, 2 * HF :]
        tail_doc = doc_at(info, row, block_start(info) + LANE - 1)
        tail = (doc_of(info, row, positions(info, 0)) == tail_doc).astype(F32)
        fa, fb = factors(k, table)
        phi = (fa * fb * tail).astype(BF16)
        count = dot(jnp.ones((8, LANE), BF16), phi)[0:1]
        split_rows(info, row, pack_state(dot_tn(phi, v), count), keep_ref, send_ref)


def chip_body(backward, info, keep_ref, recv_ref, o_ref):
    c = info[2, 2]
    base = block_start(info, c=0)
    keep, recv = keep_ref[...].astype(F32), recv_ref[...].astype(F32)
    is_zero = jnp.where(c == 0, 1.0, 0.0)
    zero = is_zero * keep + (1.0 - is_zero) * recv
    one = is_zero * recv + (1.0 - is_zero) * keep
    if backward:
        total = zero + same(doc_at(info, c, base), doc_at(info, c, base + LANE)) * one
    else:
        last, end = doc_at(info, c, base + LANE - 1), doc_at(info, c, base + 2 * LANE - 1)
        total = one + same(last, end) * zero
    put_packed(o_ref, total, extra_of(keep) + extra_of(recv))


def line_body(backward, info, t0, t1, t2, t3, o_ref):
    c, y = info[2, 2], info[2, 1]
    start = block_start(info, y=0, c=0)
    whole = doc_at(info, c, start if backward else start + 8 * LANE - 1)
    total = jnp.zeros(o_ref.shape, F32)
    extra = jnp.zeros((1, LANE), F32)
    for k, t in enumerate((t0, t1, t2, t3)):
        there = start + back(y, k) * 2 * LANE
        there = there if backward else there + 2 * LANE - 1
        value = t[...].astype(F32)
        total += same(doc_at(info, c, there), whole) * value
        extra += extra_of(value)
    put_packed(o_ref, total, extra)


def enter_body(backward, info, keep, recv, t1, t2, t3, s0, s1, s2, s3, mine_ref, send_ref):
    x, y, c = info[2, 0], info[2, 1], info[2, 2]
    base = block_start(info, c=0)
    here = doc_at(info, c, base + 2 * LANE - 1 if backward else base)
    total = jnp.zeros(keep.shape, F32)
    extra = extra_of(s0)
    for k, (t, s) in enumerate(((t1, s1), (t2, s2), (t3, s3)), 1):
        there_y, there_x = back(y, k), back(x, k)
        at_y = block_start(info, y=there_y, c=0)
        at_x = block_start(info, x=there_x, y=0, c=0)
        if backward:
            use_y = same(doc_at(info, c, at_y), here) * (there_y > y).astype(F32)
            use_x = same(doc_at(info, c, at_x), here) * (there_x > x).astype(F32)
        else:
            use_y = same(doc_at(info, c, at_y + 2 * LANE - 1), here) * (there_y < y).astype(F32)
            use_x = same(doc_at(info, c, at_x + 8 * LANE - 1), here) * (there_x < x).astype(F32)
        total += use_y * t[...].astype(F32) + use_x * s[...].astype(F32)
        extra += extra_of(s)
    is_zero = jnp.where(c == 0, 1.0, 0.0)
    if backward:
        one = is_zero * recv[...].astype(F32) + (1.0 - is_zero) * keep[...].astype(F32)
        last = doc_at(info, c, base + LANE - 1)
        for_zero = same(doc_at(info, c, base + LANE), last) * one + same(here, last) * total
        for_one = total
    else:
        zero = is_zero * keep[...].astype(F32) + (1.0 - is_zero) * recv[...].astype(F32)
        begun = doc_at(info, c, base + LANE)
        for_zero = total
        for_one = same(doc_at(info, c, base + LANE - 1), begun) * zero + same(here, begun) * total
    put_packed(mine_ref, is_zero * for_zero + (1.0 - is_zero) * for_one, extra)
    put_packed(send_ref, is_zero * for_one + (1.0 - is_zero) * for_zero, extra)


def shift(value, axis, k, name):
    n = 2 if axis == "c" else 4
    with jax.named_scope(name):
        return lax.ppermute(value, axis, [(i, (i + k) % n) for i in range(n)])


def around(value, axis, name):
    return [value] + [shift(value, axis, k, name) for k in (1, 2, 3)]


def to_near(value, name):
    with jax.named_scope(name):
        return lax.ppermute(value, "z", [(0, 1), (1, 0), (2, 3), (3, 2)])


def to_far(value, name):
    with jax.named_scope(name):
        return lax.ppermute(value, "z", [(0, 3), (3, 0), (1, 2), (2, 1)])


def ordered(name, info, parts, axis, after=()):
    return call(
        name + "_order", lambda *refs: order_body("xy".index(axis), *refs),
        [out((4, *parts[0].shape), parts[0].dtype)], info, *parts, kinds="s", after=after,
    )


def to_slots(parts, name, axis="z", way=-1):
    return [parts[0]] + [shift(parts[k], axis, way * k, name) for k in (1, 2, 3)]


def chip_state(info, keep, send, backward):
    tag = "back_" if backward else ""
    recv = shift(send, "c", 1, tag + "cores")
    chip, token = call(
        tag + "chip", lambda *refs: chip_body(backward, *refs), [out((SROWS, LANE), BF16)],
        info, keep, recv, kinds="s", token=True,
    )
    return recv, chip, token


def line_and_sum_body(backward, info, t0, t1, t2, t3, far_ref, got_ref, o_ref, sum_ref):
    line_body(backward, info, t0, t1, t2, t3, o_ref)
    far_body(far_ref, got_ref, sum_ref)


def scan_states(info, chip, backward, after, extra=(), through=()):
    tag = "back_" if backward else ""
    body = line_and_sum_body if extra else line_body
    outs = [out((SROWS, LANE), BF16)] + [out(a.shape, a.dtype) for a in extra[:1]]
    t = around(chip, "y", tag + "scan_y")
    line, *more = call(
        tag + "line", lambda *refs: body(backward, *refs), outs,
        info, *t, *extra, kinds="s", after=after, through=through,
    )
    s = around(line, "x", tag + "scan_x")
    return t, line, s, *more


def scan_end(info, keep, recv, t, s, backward, after=()):
    packed, tag = out((SROWS, LANE), BF16), "back_" if backward else ""
    mine, other = call(
        tag + "enter", lambda *refs: enter_body(backward, *refs), [packed, packed],
        info, keep, recv, *t[1:], *s, kinds="s", after=after,
    )
    return mine, shift(other, "c", 1, tag + "given")


def entered(info, row, mine, other):
    return jnp.where(info[2, 2] == row, mine[...], other[...])


def pairs(info, row):
    at_i, at_j = positions(info, 0), positions(info, 1)
    doc_i, doc_j = doc_of(info, row, at_i), doc_of(info, row, at_j)
    return (doc_i == doc_j) & (at_i >= at_j)


def carried(info, row):
    doc_i = doc_of(info, row, positions(info, 0))
    return (doc_i == doc_at(info, row, block_start(info))).astype(F32)


def by_head(q):
    lanes = lax.broadcasted_iota(jnp.int32, q.shape, 1) // FDIM
    return jnp.concatenate([jnp.where(lanes == h, q, jnp.zeros_like(q)) for h in range(HH)], 0)


def columns(parts, fill):
    lanes = lax.broadcasted_iota(jnp.int32, (parts[0].shape[0], 8), 1)
    total = jnp.full((parts[0].shape[0], 8), fill, F32)
    for h, part in enumerate(parts):
        total = jnp.where(lanes == h, part, total)
    return total


def mix_here_body(info, p_ref, num_ref, den_ref, phi_ref):
    table = picks()
    p = p_ref[...]
    for row in range(2):
        line = row_of(p, row)
        q, k, v = line[:, :HF], line[:, HF : 2 * HF], line[:, 2 * HF :]
        ok = pairs(info, row)
        s = dot_nt(by_head(q), k) * 0.25
        here = slice(row * LANE, (row + 1) * LANE)
        dens = []
        for h in range(HH):
            cols = slice(h * LANE, (h + 1) * LANE)
            sh = s[cols]
            kap = jnp.where(ok, 1.0 + sh + 0.5 * sh * sh, 0.0)
            dens.append(jnp.sum(kap, -1, keepdims=True))
            num_ref[here, cols] = dot(kap.astype(BF16), v[:, cols])
        den_ref[here, :] = columns(dens, 1.0)
        fa, fb = factors(q, table)
        phi_ref[here, :] = (fa * fb * (table[4] * carried(info, row))).astype(BF16)


def assemble_body(axis, info, *refs):
    for copy in assemble(axis, info, refs[:8], refs[8], refs[9]):
        copy.wait()


def mix_body(
    info, num_ref, den_ref, phi_ref, mine, other, wo, mixed_ref, all_den_ref, b0, b1, b2, b3
):
    for row in range(2):
        here = slice(row * LANE, (row + 1) * LANE)
        state, high, low = unpack_state(entered(info, row, mine, other))
        phi = phi_ref[here, :]
        num = num_ref[here, :] + dot(phi, state)
        den = den_ref[here, :] + dot_nt(phi, high) + dot_nt(phi, low)
        attn = [num[:, h * LANE : (h + 1) * LANE] / den[:, h : h + 1] for h in range(HH)]
        put_row(mixed_ref, row, jnp.concatenate(attn, 1).astype(BF16))
        all_den_ref[here, :] = den
    branch = dot_nt(mixed_ref[...], wo[...])
    for s, b in enumerate((b0, b1, b2, b3)):
        b[...] = branch[64 * s : 64 * s + 64].astype(BF16)


def unmix_state_body(
    info, den_ref, phi_ref, mixed_ref, m0, m1, m2, m3, wo,
    dnum_ref, dden_ref, keep_ref, send_ref, mk_ref, ms_ref, dm, turn_ref,
):
    turn_body(info, m0, m1, m2, m3, mk_ref, ms_ref, turn_ref)
    for s, m in enumerate((m0, m1, m2, m3)):
        dm[64 * s : 64 * s + 64, :] = m[...]
    lanes = lax.broadcasted_iota(jnp.int32, (256, 8), 1)
    total = jnp.sum(jnp.where(lanes < HH, den_ref[...], 0.0), keepdims=True)
    total = jnp.broadcast_to(total, (1, LANE))
    mixed = mixed_ref[...]
    lane = lax.broadcasted_iota(jnp.int32, (1, FT), 1)
    head = sum((lane >= FW * h).astype(jnp.int32) for h in range(1, HH))
    heads = lax.broadcasted_iota(jnp.int32, (8, FT), 0)
    core = info[2, 2]
    d_attn = dot(dm[...], wo[...])
    for row in range(2):
        here = slice(row * LANE, (row + 1) * LANE)
        da, at, den = row_of(d_attn, row), row_of(mixed, row).astype(F32), den_ref[here, :]
        dnums, ddens = [], []
        for h in range(HH):
            cols = slice(h * LANE, (h + 1) * LANE)
            dnum = da[:, cols] / den[:, h : h + 1]
            ddens.append(-jnp.sum(dnum * at[:, cols], -1, keepdims=True))
            dnums.append(dnum)
        dnum = jnp.concatenate(dnums, 1).astype(BF16)
        dden = columns(ddens, 0.0)
        dnum_ref[here, :] = dnum
        dden_ref[here, :] = dden
        phi = phi_ref[here, :]
        dcount = jnp.where(head == heads, dot_tn(dden.astype(BF16), phi), 0.0)
        extra = jnp.where(core == row, 0.0, 1.0) * total
        packed = pack_state(dot_tn(phi, dnum), jnp.sum(dcount, 0, keepdims=True), extra)
        split_rows(info, row, packed, keep_ref, send_ref)


def unmix_here_body(
    info, p_ref, dnum_ref, dden_ref, mine, other, mk, mr, mixed, mixed_other,
    dp_ref, own_ref, on_ref, back_ref, a_ref, b_ref, full,
):
    ring_body(info, mk, mr, mixed, mixed_other, own_ref, on_ref, back_ref, a_ref, b_ref, full)
    table = picks()
    p = p_ref[...]
    for row in range(2):
        here = slice(row * LANE, (row + 1) * LANE)
        line = row_of(p, row)
        q, k, v = line[:, :HF], line[:, HF : 2 * HF], line[:, 2 * HF :]
        ok = pairs(info, row)
        q4 = by_head(q)
        s = dot_nt(q4, k) * 0.25
        dnum, dden = dnum_ref[here, :], dden_ref[here, :]
        gs, dvs = [], []
        for h in range(HH):
            cols = slice(h * LANE, (h + 1) * LANE)
            sh = s[cols]
            kap = jnp.where(ok, 1.0 + sh + 0.5 * sh * sh, 0.0)
            g = (dot_nt(dnum[:, cols], v[:, cols]) + dden[:, h : h + 1]) * (1.0 + sh) * 0.25
            gs.append(jnp.where(ok, g, 0.0).astype(BF16))
            dvs.append(dot_tn(kap.astype(BF16), dnum[:, cols]))
        g4 = jnp.concatenate(gs, 0)
        dk = dot_tn(g4, q4)
        dq4 = dot(g4, k)
        lanes = lax.broadcasted_iota(jnp.int32, (LANE, HF), 1) // FDIM
        dq = jnp.zeros((LANE, HF), F32)
        for h in range(HH):
            dq += jnp.where(lanes == h, dq4[h * LANE : (h + 1) * LANE], 0.0)
        state, high, low = unpack_state(entered(info, row, mine, other))
        dden_low = dden.astype(BF16)
        dphi = dot_nt(dnum, state) + dot(dden_low, high) + dot(dden_low, low)
        fa, fb = factors(q, table)
        dq += back_to(dphi * (table[4] * carried(info, row)), fa, fb, table)
        put_row(dp_ref, row, jnp.concatenate([dq, dk, *dvs], 1))


def unproject_body(info, p_ref, dp_ref, mine, other, r_ref, *refs):
    blocks, (gp_ref, near_ref, keep_ref, far_ref, low_ref, w_ref, sems) = refs[:8], refs[8:]
    copies = assemble(1, info, blocks, w_ref, sems)
    p, dp = p_ref[...], dp_ref[...]
    table = picks()
    for row in range(2):
        line, dline = row_of(p, row), row_of(dp, row)
        k, v = line[:, HF : 2 * HF], line[:, 2 * HF :]
        tail_doc = doc_at(info, row, block_start(info) + LANE - 1)
        tail = (doc_of(info, row, positions(info, 0)) == tail_doc).astype(F32)
        fa, fb = factors(k, table)
        state, high, low = unpack_state(entered(info, row, mine, other))
        ones = jnp.ones((LANE, 8), BF16)
        dphi = (dot_nt(v, state) + dot(ones, high) + dot(ones, low)) * tail
        dk = dline[:, HF : 2 * HF] + back_to(dphi, fa, fb, table)
        dv = dline[:, 2 * HF :] + dot((fa * fb * tail).astype(BF16), state)
        put_row(low_ref, row, jnp.concatenate([dline[:, :HF], dk, dv], 1).astype(BF16))
    d = low_ref[...]
    gp_ref[...] = (d.astype(F32) * r_ref[...]).astype(BF16)
    e = dot_nt(d, assembled(copies, w_ref)).astype(BF16)
    halve(info, e, slice(0, e.shape[1]), near_ref, keep_ref, far_ref)


def middle_body(x_ref, a, b, c, d, middle_ref, low_ref):
    u = x_ref[:64, :].astype(F32)
    for part in (a, b, c, d):
        u += part[...].astype(F32)
    middle_ref[...] = u
    low_ref[...] = (u * lax.rsqrt(jnp.mean(u * u, -1, keepdims=True) + EPS)).astype(BF16)


def norm_back(base_ref, u_ref, parts, low_ref):
    u, e = u_ref[:64, :].astype(F32), summed(parts)
    r = lax.rsqrt(jnp.mean(u * u, -1, keepdims=True) + EPS)
    slope = jnp.mean(e * u, -1, keepdims=True)
    total = base_ref[:64, :].astype(F32) + r * e - u * (r * r * r * slope)
    low_ref[...] = total.astype(BF16)


def norm_back_body(base_ref, u_ref, a, b, c, d, low_ref):
    norm_back(base_ref, u_ref, (a, b, c, d), low_ref)


def last_body(
    base_ref, x_ref, e_keep, e_got, e_far, middle_ref, keep_ref, got_ref, far_ref, o_ref
):
    norm_back(base_ref, x_ref, (e_keep, e_got.at[:64], e_far), o_ref.at[:64])
    o_ref[64:, :] = (middle_ref[...] + summed((keep_ref, got_ref.at[:64], far_ref))).astype(BF16)


def place_body(info, a, b, c, d, grad_ref, out_ref):
    for k, part in enumerate((a, b, c, d)):
        at = pl.multiple_of(32 * back(info[2, 3], k), 32)
        for row in range(2):
            grad_ref[row, pl.ds(at, 32), :] = part[32 * row : 32 * row + 32, :]
            out_ref[row, pl.ds(at, 32), :] = part[64 + 32 * row : 96 + 32 * row, :]


def rows_in(bulk, first, width, w, sems, parts):
    step = w.shape[0] // parts
    copies = [
        pltpu.make_async_copy(
            bulk.at[pl.ds(step * k, step), pl.ds(first, width)],
            w.at[pl.ds(step * k, step), :],
            sems.at[k],
        )
        for k in range(parts)
    ]
    for copy in copies:
        copy.start()
    return copies


def d_hidden_body(dy_hbm, bulk, o_ref, w, dy_ref, sems, dy_sem):
    units = w.shape[1]
    parts = sems.shape[0]
    step = w.shape[0] // parts
    dy_copy = pltpu.make_async_copy(dy_hbm, dy_ref, dy_sem)
    dy_copy.start()
    copies = rows_in(bulk, 2 * units, units, w, sems, parts)
    dy_copy.wait()
    for k, copy in enumerate(copies):
        copy.wait()
        here = slice(step * k, step * (k + 1))
        part = dot(dy_ref[:, here], w[here, :])
        if k == 0:
            o_ref[...] = part
        else:
            o_ref[...] += part


def ffn_body(
    info, u0, u1, u2, u3, dh_ref, bulk,
    a_ref, keep_ref, e0, e1, e2, e3, u, w, pre, t, sems,
):
    core = info[2, 2]
    pair = 2 * LANE
    groups = w.shape[1] // pair
    hid_at, turn_at = w.shape[1], w.shape[1] + w.shape[1] // 2
    parts = sems.shape[0]
    step = w.shape[0] // parts
    copies = rows_in(bulk, 0, w.shape[1], w, sems, parts)
    for s, part in enumerate((u0, u1, u2, u3)):
        u[64 * s : 64 * s + 64, :] = part[...]
    for k, copy in enumerate(copies):
        copy.wait()
        here = slice(step * k, step * (k + 1))
        part = dot(u[:, here], w[here, :])
        if k == 0:
            pre[...] = part
        else:
            pre[...] += part
    for b in range(groups):
        units = slice(b * LANE, (b + 1) * LANE)
        gate = pre[:, b * pair : b * pair + LANE]
        up = pre[:, b * pair + LANE : (b + 1) * pair]
        d_hidden = dh_ref[:, units]
        sigma = 1.0 / (1.0 + jnp.exp(-gate))
        silu = gate * sigma
        a_ref[:, hid_at + b * LANE : hid_at + (b + 1) * LANE] = (silu * up).astype(BF16)
        d_gate = d_hidden * up * (sigma + silu * (1.0 - sigma))
        a_ref[:, b * pair : b * pair + LANE] = d_gate.astype(BF16)
        a_ref[:, b * pair + LANE : (b + 1) * pair] = (d_hidden * silu).astype(BF16)
    for n in range(w.shape[0] // pair):
        here = slice(n * pair, (n + 1) * pair)
        e = dot_nt(a_ref[:, :hid_at], w[here, :]).astype(BF16)
        for s, ref in enumerate((e0, e1, e2, e3)):
            ref[:, here] = e[64 * s : 64 * s + 64]
        t[...] = u[:, here].astype(F32).T
        for i in range(pair // LANE):
            at = slice(n * LANE + 64 * i, n * LANE + 64 * i + 64)
            mine = pl.ds(pl.multiple_of(LANE * i + 64 * core, 64), 64)
            other = pl.ds(pl.multiple_of(LANE * i + 64 - 64 * core, 64), 64)
            keep_ref[at, :] = t[mine, :].astype(BF16)
            row = n % 2 * LANE + 64 * i
            lanes = slice(turn_at + n // 2 * 256, turn_at + n // 2 * 256 + 256)
            a_ref[row : row + 64, lanes] = t[other, :].astype(BF16)


def halve(info, value, here, near_ref, keep_ref, far_ref):
    even = info[2, 3] % 2 == 0
    one, three = value[64:128], value[192:]
    keep_ref[:, here] = value[:64]
    near_ref[:64, here] = jnp.where(even, three, one)
    near_ref[64:, here] = value[128:192]
    far_ref[:, here] = jnp.where(even, one, three)


def down_body(info, a_ref, bulk, near_ref, keep_ref, far_ref, w, sems):
    units = w.shape[1]
    parts = sems.shape[0]
    step = w.shape[0] // parts
    for k, copy in enumerate(rows_in(bulk, 2 * units, units, w, sems, parts)):
        copy.wait()
        here = slice(step * k, step * (k + 1))
        f = dot_nt(a_ref[:, 2 * units : 3 * units], w[here, :]).astype(BF16)
        halve(info, f, here, near_ref, keep_ref, far_ref)


def far_body(far_ref, got_ref, o_ref):
    o_ref[...] = (far_ref[...].astype(F32) + got_ref[64:, :].astype(F32)).astype(BF16)


def ffn_grad_body(uk, yk, yr, a_own, a_other, o_ref, lhs):
    step = pl.program_id(0)
    rows, units = lhs.shape[0], o_ref.shape[1]

    def product(at):
        both = jnp.concatenate([a_own[:, at : at + units], a_other[:, at : at + units]], 0)
        for m in range(rows // 256):
            here = slice(256 * m, 256 * (m + 1))
            o_ref[here, :] = dot(lhs[here, :], both).astype(BF16)

    @pl.when(step == 0)
    def _():
        lhs[:, :256] = uk[...]
        for m in range(rows // 256):
            at = 3 * units + 256 * m
            lhs[256 * m : 256 * (m + 1), 256:] = a_other[:, at : at + 256]
        product(0)

    @pl.when(step == 1)
    def _():
        product(units)

    @pl.when(step == 2)
    def _():
        lhs[:, :256] = yk[...]
        lhs[:, 256:] = yr[...]
        product(2 * units)


def ffn_grads(uk, yk, yr, a_own, a_other, units):
    rows, tokens = uk.shape
    with jax.named_scope("ffn_grad"):
        return pl.pallas_call(
            ffn_grad_body,
            grid=(3,),
            out_shape=pltpu.HBM((rows, 3 * units), BF16),
            in_specs=[pl.BlockSpec(memory_space=pltpu.VMEM)] * 5,
            out_specs=pl.BlockSpec((rows, units), lambda b: (0, b)),
            scratch_shapes=[pltpu.VMEM((rows, 2 * tokens), BF16)],
            compiler_params=pltpu.CompilerParams(vmem_limit_bytes=20 * 2**20),
            cost_estimate=pl.CostEstimate(
                flops=12 * rows * tokens * units, bytes_accessed=6 * rows * units, transcendentals=0
            ),
        )(uk, yk, yr, a_own, a_other)


def fold_body(info, *refs):
    ins, outs, results = refs[:3], refs[3:6], refs[6:]
    for k, o in enumerate(results):
        there = (info[2, 0] + k) % 4
        sides = [sum(part[there].astype(F32) for part in parts) for parts in (ins, outs)]
        o[...] = jnp.concatenate(sides, 1).astype(BF16)


def ring_body(info, lk, lr, own, other, own_ref, on_ref, back_ref, a_ref, b_ref, full):
    full[...] = (dot(lk[...], own[...]) + dot(lr[...], other[...])).astype(BF16)
    for k, o in ((0, own_ref), (1, on_ref), (3, back_ref), (2, None)):
        there = (info[2, 1] + k) % 4
        for i in range(4):
            rows = full[pl.ds(pl.multiple_of((i * 4 + there) * 64, 64), 64), :]
            if o is not None:
                o[i] = rows
            elif i < 2:
                a_ref[i] = rows
            else:
                b_ref[i - 2] = rows


def ring_add_body(on_ref, back_ref, a_ref, b_ref, on_out, back_out):
    on_out[...] = on_ref[...]
    back_out[...] = back_ref[...]
    on_out[:2] = (on_ref[:2].astype(F32) + a_ref[...].astype(F32)).astype(BF16)
    back_out[2:] = (back_ref[2:].astype(F32) + b_ref[...].astype(F32)).astype(BF16)


def ring_sum(name, info, lk, lr, own, other):
    n = own.shape[1]
    part, half = out((4, 64, n), BF16), out((2, 64, n), BF16)
    mine, on, before, a, b = call(
        name, ring_body, [part, part, part, half, half], info, lk, lr, own, other, kinds="s",
        scratch=[pltpu.VMEM((lk.shape[0], n), BF16)], flops=4 * lk.shape[0] * lk.shape[1] * n,
    )
    return ring_rest(name, mine, on, before, a, b)


def ring_rest(name, mine, on, before, a, b):
    got_a, got_b = shift(a, "y", 1, name + "_far"), shift(b, "y", -1, name + "_far")
    part = out(on.shape, BF16)
    on, before = call(name + "_add", ring_add_body, [part, part], on, before, got_a, got_b)
    return [mine, shift(on, "y", 1, name + "_near"), shift(before, "y", -1, name + "_near")]


def summed(parts):
    return sum(part[...].astype(F32) for part in parts)


def row_sums(value):
    total = jnp.broadcast_to(jnp.sum(value, 1, keepdims=True), (64, LANE))
    wide = jnp.concatenate([total, jnp.zeros((64, LANE), F32)], 0)
    return wide.T[0:1]


def finish_ffn_body(s_ref, wg_ref, wu_ref, g_ref, gate_ref, up_ref, down_ref, gain_ref):
    units = gate_ref.shape[1]
    g = column(g_ref[...])
    groups = s_ref.shape[1] // (3 * LANE)

    def side(k):
        at = [(2 * b + k) * LANE for b in range(groups)]
        return jnp.concatenate([s_ref[:, i : i + LANE] for i in at], 1)[:, :units].astype(F32)

    gate, up = side(0), side(1)
    gain = row_sums(gate * wg_ref[...].astype(F32) + up * wu_ref[...].astype(F32))
    gain_ref[...] = jnp.broadcast_to(gain, gain_ref.shape)
    gate_ref[...] = gate * g
    up_ref[...] = up * g
    down_ref[...] = s_ref[:, 2 * groups * LANE : 2 * groups * LANE + units].astype(F32)


def totals_body(a, b, c, d, one_ref, two_ref, den_ref):
    total = summed((a, b, c, d))
    one_ref[...] = total[0:1, :64]
    two_ref[...] = total[1:2, :64]
    den_ref[...] = total[2:3, :1]


def finish_mix_body(
    s0, s1, s2, s3, wq_ref, wk_ref, wv_ref, g_ref, gain2_ref, den0, den1,
    q_ref, k_ref, v_ref, out_ref, message_ref,
):
    g = column(g_ref[...])
    total = summed((s0, s1, s2, s3))
    cols = total.shape[1] - out_ref.shape[1]
    grads = total[:, :cols]
    out_ref[...] = total[:, cols:]
    w = jnp.concatenate([wq_ref[...], wk_ref[...], wv_ref[...]], 1).astype(F32)
    rows = lax.broadcasted_iota(jnp.int32, (8, LANE), 0)
    den = extra_of(den0) + extra_of(den1)
    message = jnp.where(rows == 0, row_sums(grads * w), 0.0)
    message = jnp.where(rows == 1, gain2_ref[0:1, :], message)
    message_ref[...] = jnp.where(rows == 2, den, message)
    scaled = grads * g
    q_ref[...] = scaled[:, :HF]
    k_ref[...] = scaled[:, HF : 2 * HF]
    v_ref[...] = scaled[:, 2 * HF :]


def on_device(
    tokens,
    doc_lengths,
    norm_gain,
    w_query,
    w_key,
    w_value,
    w_out,
    ffn_gain,
    w_gate,
    w_up,
    w_down,
    out_grad,
):
    x, y, c, z = (lax.axis_index(a) for a in ("x", "y", "c", "z"))
    ends = jnp.cumsum(doc_lengths, -1).astype(jnp.int32)
    places = jnp.stack([x, y, c, z, x, x, x, x]).astype(jnp.int32)
    info = jnp.concatenate([ends, places[None]], 0)
    d = tokens.shape[-1]
    width = w_out.shape[0]
    units = -(-w_gate.shape[1] // LANE) * LANE
    cols = 2 * HF + w_value.shape[1]
    piece = out((64, d), BF16)
    piece_full = out((64, d), F32)
    state = out((SROWS, LANE), BF16)

    early, early_out = call(
        "early", early_body, [out((64, cols), BF16), out((64, width), BF16)],
        norm_gain[None], w_query, w_key, w_value, w_out.T, kinds="ddddd",
    )
    out_ys = around(early_out, "y", "out_y")
    (line,) = ordered("in_x", info, around(early, "x", "in_x"), "x", out_ys[1:3])
    w_in = around(line, "y", "in_y")
    (out_line,) = ordered("out_y", info, out_ys, "y", [line])
    w_mix = around(out_line, "x", "out_x")
    x_all, xk, x_send, x_token = slotted(info, tokens)
    dy_all, yk, y_send, y_token = slotted(info, out_grad)
    xr, yr = shift(x_send, "c", 1, "x_cores"), shift(y_send, "c", 1, "y_cores")
    (bulk_own,) = call(
        "bulk", bulk_body, [out((64, 3 * units), BF16)],
        ffn_gain[None], w_gate, w_up, w_down.T, kinds="dddd", after=[*w_in[1:], *w_mix[1:], x_token, y_token],
    )
    bulk = lax.all_gather(bulk_own, BLK, axis=0, tiled=True)
    w_in += [shift(g, "c", 1, "in_cores") for g in w_in]
    w_mix += [shift(g, "c", 1, "out_cores") for g in w_mix]


    p, r, keep, send = call(
        "project", project_body,
        [out((256, cols), BF16), out((256, 1), F32), state, state],
        info, x_all, *w_in, kinds="sv" + "a" * 8, after=[xr, yr],
        scratch=[pltpu.VMEM((4, 4, 2, 64, cols), BF16), pltpu.SemaphoreType.DMA((8,))],
        flops=2 * 256 * d * cols, limit=20,
    )
    num_here, den_here, phi, here_token = call(
        "mix_here", mix_here_body,
        [out((256, width), F32), out((256, 8), F32), out((256, FT), BF16)],
        info, p, kinds="s", token=True, flops=2 * 256 * d * 64,
    )
    recv, chip, _ = chip_state(info, keep, send, False)
    t, _, s = scan_states(info, chip, False, [here_token])
    w_mix_all, w_token = call(
        "assemble", lambda *refs: assemble_body(0, *refs), [out((4, 4, 2, 64, width), BF16)],
        info, *w_mix, kinds="s" + "a" * 8, scratch=[pltpu.SemaphoreType.DMA((8,))], token=True,
    )
    w_mix_all = w_mix_all.reshape(d, width)
    mine, other = scan_end(info, keep, recv, t, s, False, [w_token])
    mixed, den, *branch = call(
        "mix", mix_body,
        [out((256, width), BF16), out((256, 8), F32)] + [piece] * 4,
        info, num_here, den_here, phi, mine, other, w_mix_all, kinds="s",
        flops=2 * 256 * d * width, limit=16,
    )
    (d_hidden,) = call(
        "d_hidden", d_hidden_body, [out((256, units), F32)], dy_all, bulk, kinds="hh",
        scratch=[
            pltpu.VMEM((d, units), BF16), pltpu.VMEM((256, d), BF16),
            pltpu.SemaphoreType.DMA((4,)), pltpu.SemaphoreType.DMA,
        ],
        flops=2 * 256 * d * units, limit=16,
    )
    middle, u2 = call("middle", middle_body, [piece_full, piece], x_all, *to_slots(branch, "branch_sum"))
    us = around(u2, "z", "u_all")
    mixed_other = shift(mixed, "c", 1, "mixed_cores")
    half = out((d // 2, 256), BF16)
    a_own, uk, *e_parts = call(
        "ffn", ffn_body,
        [out((256, 3 * units + d // 2), BF16), half] + [piece] * 4,
        info, *us, d_hidden, bulk, kinds="svvvvvh", after=[mixed_other],
        scratch=[
            pltpu.VMEM((256, d), BF16), pltpu.VMEM((d, 2 * units), BF16),
            pltpu.VMEM((256, 2 * units), F32), pltpu.VMEM((2 * LANE, 256), F32),
            pltpu.SemaphoreType.DMA((4,)),
        ],
        flops=8 * 256 * d * units, limit=36,
    )
    a_other = shift(a_own, "c", 1, "a_cores")
    ffn_rows = ffn_grads(uk, yk, yr, a_own, a_other, units)
    dm, ffn_rows = call(
        "norm_back", norm_back_body, [piece],
        dy_all, middle, *to_slots(e_parts, "e_sum"), through=[ffn_rows],
    )
    ffn_sum = lax.psum_scatter(ffn_rows, ("x", "y"), scatter_dimension=0, tiled=True)
    f_near, f_keep, f_far, f_token = call(
        "down", down_body, [out((128, d), BF16), piece, piece], info, a_own, bulk, kinds="svh", token=True,
        scratch=[pltpu.VMEM((d, units), BF16), pltpu.SemaphoreType.DMA((8,))],
        flops=2 * 256 * d * units, limit=16,
    )
    dms = around(dm, "z", "dm_all")
    dnum, dden, dkeep, dsend, mk, m_send = call(
        "unmix_state", unmix_state_body,
        [out((256, width), BF16), out((256, 8), F32), state, state, half, half],
        info, den, phi, mixed, *dms, w_mix_all, kinds="s", after=[f_token],
        scratch=[pltpu.VMEM((256, d), BF16), pltpu.VMEM((d, 256), F32)],
        flops=2 * 256 * d * width, limit=20,
    )
    drecv, dchip, dtoken = chip_state(info, dkeep, dsend, True)
    mr = shift(m_send, "c", 1, "m_cores")
    dp, *out_ring, unmix_token = call(
        "unmix_here", unmix_here_body,
        [out((256, cols), F32)] + [out((4, 64, width), BF16)] * 3 + [out((2, 64, width), BF16)] * 2,
        info, p, dnum, dden, mine, other, mk, mr, mixed, mixed_other, kinds="s", after=[dtoken],
        token=True,
        scratch=[pltpu.VMEM((d // 2, width), BF16)], flops=2 * 256 * d * 640,
    )
    f_got = to_near(f_near, "f_near")
    dt, _, ds, f_send = scan_states(info, dchip, True, [unmix_token], (f_far, f_got))
    f_last = to_far(f_send, "f_far")
    out_first = ring_rest("out", *out_ring)
    dmine, dother = scan_end(info, dkeep, drecv, dt, ds, True)

    gp, e_near, e_keep, e_far = call(
        "unproject", unproject_body,
        [out((256, cols), BF16), out((128, d), BF16), piece, piece],
        info, p, dp, dmine, dother, r, *w_in, kinds="svvvvv" + "a" * 8, after=[*out_first[1:]],
        scratch=[
            pltpu.VMEM((256, cols), BF16), pltpu.VMEM((4, 4, 2, 64, cols), BF16),
            pltpu.SemaphoreType.DMA((8,)),
        ],
        flops=2 * 256 * d * cols, limit=16,
    )
    in_first = ring_sum("in_grad", info, xk, xr, gp, shift(gp, "c", 1, "gp_cores"))
    e_got = to_near(e_near, "e_near")
    (e_send,) = call("e_mid", far_body, [piece], e_far, e_got)
    (last,) = call(
        "last", last_body, [out((128, d), BF16)],
        dm, x_all, e_keep, e_got, to_far(e_send, "e_far"), middle, f_keep, f_got, f_last,
        after=in_first[1:],
    )
    input_grad, block_out = call(
        "place", place_body, [out(tokens.shape, BF16)] * 2,
        info, *around(last, "z", "last_all"), kinds="s",
    )
    sums = call(
        "fold", fold_body, [out((64, cols + width), BF16)] * 4,
        info, *in_first, *out_first, kinds="s",
    )
    g_gate, g_up, g_down, gain2 = call(
        "finish_ffn", finish_ffn_body,
        [out(w_gate.shape, F32), out(w_up.shape, F32), out(w_down.shape[::-1], F32),
         out((8, LANE), F32)],
        ffn_sum, w_gate, w_up, ffn_gain[None], kinds="dddd",
    )
    g_q, g_k, g_v, g_out, message = call(
        "finish_mix", finish_mix_body,
        [out(w_query.shape, F32), out(w_key.shape, F32), out(w_value.shape, F32),
         out(w_out.shape[::-1], F32), out((8, LANE), F32)],
        *to_slots(sums, "second", "x", 1),
        w_query, w_key, w_value, norm_gain[None], gain2, dmine, dother,
        kinds="vvvvdddd",
    )
    gain_one, gain_two, denom = call(
        "totals", totals_body, [out((1, 64), F32), out((1, 64), F32), out((1, 1), F32)],
        *around(message, "z", "message"),
    )
    seq = 32 * LANE
    denom_mean = denom.reshape(()) / (2 * seq * HEADS * seq)
    return (
        block_out, input_grad, gain_one.reshape(64), g_q, g_k, g_v, g_out.T, gain_two.reshape(64),
        g_gate, g_up, g_down.T, denom_mean,
    )


def solution(mesh):
    finer = Mesh(mesh.devices.reshape(4, 4, 2, mesh.shape["head"]), ("x", "y", "c", "z"))
    placed = (
        P(None, BLK, None),
        P(),
        P(BLK),
        P(BLK, "z"),
        P(BLK, "z"),
        P(BLK, "z"),
        P("z", BLK),
        P(BLK),
        P(BLK, "z"),
        P(BLK, "z"),
        P("z", BLK),
        P(None, BLK, None),
    )
    return jax.shard_map(
        on_device,
        mesh=finer,
        in_specs=placed,
        out_specs=(
            P(None, BLK, None),
            P(None, BLK, None),
            P(BLK),
            P(BLK, "z"),
            P(BLK, "z"),
            P(BLK, "z"),
            P("z", BLK),
            P(BLK),
            P(BLK, "z"),
            P(BLK, "z"),
            P("z", BLK),
            P(),
        ),
        check_vma=False,
    )
```

```python
import math

import jax
import jax.numpy as jnp
from jax import lax
from jax.experimental import pallas as pl
from jax.experimental.pallas import tpu as pltpu
from jax.sharding import Mesh
from jax.sharding import PartitionSpec as P

HEADS = 16
FDIM = 16
EPS = 1e-05
BLK = ("x", "y", "c")
F32 = jnp.float32
BF16 = jnp.bfloat16

HH = 4
HF = HH * FDIM
FW = 160
FT = HH * FW
SROWS = FT + 16
LANE = 128
DOCS = 8


def dot(a, b):
    return jnp.dot(a, b, preferred_element_type=F32)


def dot_nt(a, b):
    return lax.dot_general(a, b, (((1,), (1,)), ((), ())), preferred_element_type=F32)


def dot_tn(a, b):
    return lax.dot_general(a, b, (((0,), (0,)), ((), ())), preferred_element_type=F32)


def out(shape, dtype):
    return jax.ShapeDtypeStruct(tuple(shape), dtype)


SPACES = {"s": pltpu.SMEM, "v": pltpu.VMEM, "h": pltpu.HBM, "d": pltpu.HBM, "a": pl.ANY}


def in_hbm(value):
    return pltpu.with_memory_space_constraint(value, pltpu.HBM)


def call(
    name, body, outs, *args, kinds="", after=(), through=(), scratch=(), flops=0, limit=12, token=False
):
    if token:
        first, outs = len(args) + len(outs), [*outs, out((8, LANE), F32)]
        inside = body

        def body(*refs):
            refs[first][...] = jnp.zeros((8, LANE), F32)
            inside(*refs[:first], *refs[first + 1 :])

    kinds = kinds + "v" * (len(args) - len(kinds))
    n_args, n_extra, n_out = len(args), len(after) + len(through), len(outs)
    staged = [k for k in range(n_args) if kinds[k] == "d"]
    places = [pltpu.VMEM(args[k].shape, args[k].dtype) for k in staged]
    if staged:
        places.append(pltpu.SemaphoreType.DMA((len(staged),)))

    def inner(*refs):
        given, results = list(refs[:n_args]), refs[n_args + n_extra :]
        own = results[n_out + len(through) :]
        held, own = own[: len(places)], own[len(places) :]
        copies = [
            pltpu.make_async_copy(given[k], held[i], held[-1].at[i]) for i, k in enumerate(staged)
        ]
        for copy in copies:
            copy.start()
        for copy in copies:
            copy.wait()
        for i, k in enumerate(staged):
            given[k] = held[i]
        body(*given, *results[:n_out], *own)

    moved = sum(math.prod(a.shape) * a.dtype.itemsize for a in (*args, *outs))
    args = [in_hbm(a) if k in "hd" else a for a, k in zip(args, kinds)]
    through = [in_hbm(a) if a.size > 2**21 else a for a in through]
    with jax.named_scope(name):
        return pl.pallas_call(
            inner,
            out_shape=list(outs) + [out(t.shape, t.dtype) for t in through],
            in_specs=[pl.BlockSpec(memory_space=SPACES[k]) for k in kinds + "a" * n_extra],
            out_specs=[pl.BlockSpec(memory_space=SPACES[k]) for k in "v" * n_out + "a" * len(through)],
            scratch_shapes=[*places, *scratch],
            input_output_aliases={
                n_args + len(after) + k: n_out + k for k in range(len(through))
            },
            compiler_params=pltpu.CompilerParams(vmem_limit_bytes=limit * 2**20),
            cost_estimate=pl.CostEstimate(flops=flops, bytes_accessed=moved, transcendentals=0),
        )(*args, *after, *through)


def doc_at(info, row, position):
    total = jnp.int32(0)
    for k in range(DOCS):
        total += (info[row, k] <= position).astype(jnp.int32)
    return total


def doc_of(info, row, where):
    total = jnp.zeros(where.shape, jnp.int32)
    for k in range(DOCS):
        total += (info[row, k] <= where).astype(jnp.int32)
    return total


def same(a, b):
    return (a == b).astype(F32)


def block_start(info, x=None, y=None, c=None):
    x = info[2, 0] if x is None else x
    y = info[2, 1] if y is None else y
    c = info[2, 2] if c is None else c
    return ((x * 4 + y) * 2 + c) * LANE


def back(place, k):
    return (place - k + 4) % 4


def positions(info, dim):
    shape = (LANE, 1) if dim == 0 else (1, LANE)
    t = lax.broadcasted_iota(jnp.int32, shape, dim)
    slot, inside = t // 32, t % 32
    return block_start(info) + 32 * ((info[2, 3] - slot + 4) % 4) + inside


def row_of(value, row):
    return jnp.concatenate([value[64 * s + 32 * row : 64 * s + 32 * row + 32] for s in range(4)], 0)


def put_row(ref, row, value):
    for s in range(4):
        ref[64 * s + 32 * row : 64 * s + 32 * row + 32, :] = value[32 * s : 32 * s + 32]


def diagonal(g):
    n = g.shape[-1]
    rows = lax.broadcasted_iota(jnp.int32, (n, n), 0)
    cols = lax.broadcasted_iota(jnp.int32, (n, n), 1)
    return jnp.where(rows == cols, jnp.broadcast_to(g.astype(F32), (n, n)), 0.0).astype(BF16)


def column(g):
    return jnp.sum(diagonal(g).astype(F32), 1, keepdims=True)


def early_body(g_ref, q_ref, k_ref, v_ref, wo_ref, o_ref, out_ref):
    d = diagonal(g_ref[...])
    qk = jnp.concatenate([q_ref[...], k_ref[...]], 1)
    o_ref[:, :LANE] = dot(d, qk).astype(BF16)
    o_ref[:, LANE:] = dot(d, v_ref[...]).astype(BF16)
    out_ref[...] = wo_ref[...]


def bulk_body(g_ref, wg_ref, wu_ref, wd_ref, o_ref):
    d = diagonal(g_ref[...])
    units = wg_ref.shape[1]
    groups = -(-units // LANE)
    fill = jnp.zeros((wg_ref.shape[0], groups * LANE - units), BF16)
    gate = jnp.concatenate([dot(d, wg_ref[...]).astype(BF16), fill], 1)
    up = jnp.concatenate([dot(d, wu_ref[...]).astype(BF16), fill], 1)
    for b in range(groups):
        here = slice(b * LANE, (b + 1) * LANE)
        o_ref[:, 2 * b * LANE : (2 * b + 1) * LANE] = gate[:, here]
        o_ref[:, (2 * b + 1) * LANE : (2 * b + 2) * LANE] = up[:, here]
    o_ref[:, 2 * groups * LANE : 3 * groups * LANE] = jnp.concatenate([wd_ref[...], fill], 1)


def turn(info, t, keep_ref, send_ref):
    core = info[2, 2]
    for i in range(t.shape[0] // LANE):
        here = pl.multiple_of(LANE * i + 64 * core, 64)
        there = pl.multiple_of(LANE * i + 64 - 64 * core, 64)
        keep_ref[64 * i : 64 * i + 64, :] = t[pl.ds(here, 64), :].astype(BF16)
        send_ref[64 * i : 64 * i + 64, :] = t[pl.ds(there, 64), :].astype(BF16)


def order_body(axis, info, a, b, c, d, o_ref):
    for k, part in enumerate((a, b, c, d)):
        o_ref[back(info[2, axis], k)] = part[...]


def slot_body(info, value_ref, all_ref, keep_ref, send_ref, t):
    for k in range(4):
        at = pl.multiple_of(32 * back(info[2, 3], k), 32)
        for row in range(2):
            here = slice(64 * k + 32 * row, 64 * k + 32 * row + 32)
            all_ref[here, :] = value_ref[row, pl.ds(at, 32), :]
        t[:, 64 * k : 64 * k + 64] = all_ref[64 * k : 64 * k + 64, :].astype(F32).T
    turn(info, t, keep_ref, send_ref)


def turn_body(info, a, b, c, d, keep_ref, send_ref, t):
    for k, part in enumerate((a, b, c, d)):
        t[:, 64 * k : 64 * k + 64] = part[...].astype(F32).T
    turn(info, t, keep_ref, send_ref)


def slotted(info, value):
    d = value.shape[-1]
    half = out((d // 2, 256), BF16)
    return call(
        "slot", slot_body, [out((256, d), BF16), half, half], info, value, kinds="s", token=True,
        scratch=[pltpu.VMEM((d, 256), F32)],
    )


def picks():
    lane = lax.broadcasted_iota(jnp.int32, (1, FT), 1)
    head = sum((lane >= FW * h).astype(jnp.int32) for h in range(1, HH))
    e = lane - FW * head
    n = FDIM + 1
    s = sum((e >= n * m).astype(jnp.int32) for m in range(1, 9))
    a = e - n * s
    b = a + s
    b = jnp.where(b >= n, b - n, b)
    used = e < 9 * n
    rows = lax.broadcasted_iota(jnp.int32, (HF, FT), 0)

    def matrix(i):
        at = jnp.where(used & (i < FDIM), FDIM * head + i, -1)
        return jnp.where(rows == at, 1.0, 0.0).astype(BF16)

    one_a = jnp.where(used & (a == FDIM), 1.0, 0.0)
    one_b = jnp.where(used & (b == FDIM), 1.0, 0.0)
    plain = jnp.where(a == b, 1.0 / 32, 1.0 / 16)
    weight = jnp.where(one_a + one_b == 2.0, 1.0, jnp.where(one_a + one_b == 1.0, 0.25, plain))
    return matrix(a), matrix(b), one_a, one_b, weight


def factors(u, table):
    pick_a, pick_b, one_a, one_b, _ = table
    return dot(u, pick_a) + one_a, dot(u, pick_b) + one_b


def back_to(dphi, fa, fb, table):
    return dot_nt((dphi * fb).astype(BF16), table[0]) + dot_nt((dphi * fa).astype(BF16), table[1])


def pack_state(state, count, extra=None):
    parts = [
        state[h * FW : (h + 1) * FW, h * LANE : (h + 1) * LANE].astype(BF16) for h in range(HH)
    ]
    high = count.astype(BF16).astype(F32)
    low = count - high
    rows = lax.broadcasted_iota(jnp.int32, (16, LANE), 0)
    tile = jnp.zeros((16, LANE), F32)
    for j in range(FT // LANE):
        tile = jnp.where(rows == j, high[:, j * LANE : (j + 1) * LANE], tile)
        tile = jnp.where(rows == j + 5, low[:, j * LANE : (j + 1) * LANE], tile)
    if extra is not None:
        tile = with_extra(tile, extra)
    return jnp.concatenate([*parts, tile.astype(BF16)], 0)


def with_extra(tile, extra):
    rows = lax.broadcasted_iota(jnp.int32, (16, LANE), 0)
    high = extra.astype(BF16).astype(F32)
    tile = jnp.where(rows == 10, high, tile)
    return jnp.where(rows == 11, extra - high, tile)


def extra_of(packed):
    return packed[FT + 10 : FT + 11].astype(F32) + packed[FT + 11 : FT + 12].astype(F32)


def put_packed(ref, total, extra):
    ref[:FT, :] = total[:FT].astype(BF16)
    ref[FT:, :] = with_extra(total[FT:], extra).astype(BF16)


def unpack_state(packed):
    blocks = []
    for h in range(HH):
        mine = packed[h * FW : (h + 1) * FW]
        zero = jnp.zeros_like(mine)
        blocks.append(jnp.concatenate([mine if g == h else zero for g in range(HH)], 1))
    state = jnp.concatenate(blocks, 0)
    tile = packed[FT:].astype(F32)
    lane = lax.broadcasted_iota(jnp.int32, (1, FT), 1)
    head = sum((lane >= FW * h).astype(jnp.int32) for h in range(1, HH))
    heads = lax.broadcasted_iota(jnp.int32, (8, FT), 0)
    counts = []
    for first in (0, 5):
        line = jnp.concatenate([tile[first + j : first + j + 1] for j in range(5)], 1)
        counts.append(jnp.where(head == heads, jnp.broadcast_to(line, (8, FT)), 0.0).astype(BF16))
    return state, counts[0], counts[1]


def split_rows(info, row, packed, keep_ref, send_ref):
    @pl.when(info[2, 2] == row)
    def _():
        keep_ref[...] = packed

    @pl.when(info[2, 2] != row)
    def _():
        send_ref[...] = packed


def assemble(axis, info, blocks, w_ref, sems):
    core = info[2, 2]
    copies = []
    for k in range(4):
        there = back(info[2, axis], k)
        for i, owner in enumerate((core, 1 - core)):
            target = w_ref.at[there, :, owner] if axis == 0 else w_ref.at[:, there, owner]
            copies.append(pltpu.make_async_copy(blocks[4 * i + k], target, sems.at[len(copies)]))
            copies[-1].start()
    return copies


def assembled(copies, w_ref):
    for copy in copies:
        copy.wait()
    return w_ref[...].reshape(-1, w_ref.shape[-1])


def project_body(info, x_ref, *refs):
    blocks, (p_ref, r_ref, keep_ref, send_ref, w_ref, sems) = refs[:8], refs[8:]
    copies = assemble(1, info, blocks, w_ref, sems)
    x = x_ref[...]
    xf = x.astype(F32)
    r = lax.rsqrt(jnp.mean(xf * xf, -1, keepdims=True) + EPS)
    r_ref[...] = r
    table = picks()
    p = (dot(x, assembled(copies, w_ref)) * r).astype(BF16)
    p_ref[...] = p
    for row in range(2):
        mine = row_of(p, row)
        k, v = mine[:, HF : 2 * HF], mine[:, 2 * HF :]
        tail_doc = doc_at(info, row, block_start(info) + LANE - 1)
        tail = (doc_of(info, row, positions(info, 0)) == tail_doc).astype(F32)
        fa, fb = factors(k, table)
        phi = (fa * fb * tail).astype(BF16)
        count = dot(jnp.ones((8, LANE), BF16), phi)[0:1]
        split_rows(info, row, pack_state(dot_tn(phi, v), count), keep_ref, send_ref)


def chip_body(backward, info, keep_ref, recv_ref, o_ref):
    c = info[2, 2]
    base = block_start(info, c=0)
    keep, recv = keep_ref[...].astype(F32), recv_ref[...].astype(F32)
    is_zero = jnp.where(c == 0, 1.0, 0.0)
    zero = is_zero * keep + (1.0 - is_zero) * recv
    one = is_zero * recv + (1.0 - is_zero) * keep
    if backward:
        total = zero + same(doc_at(info, c, base), doc_at(info, c, base + LANE)) * one
    else:
        last, end = doc_at(info, c, base + LANE - 1), doc_at(info, c, base + 2 * LANE - 1)
        total = one + same(last, end) * zero
    put_packed(o_ref, total, extra_of(keep) + extra_of(recv))


def line_body(backward, info, t0, t1, t2, t3, o_ref):
    c, y = info[2, 2], info[2, 1]
    start = block_start(info, y=0, c=0)
    whole = doc_at(info, c, start if backward else start + 8 * LANE - 1)
    total = jnp.zeros(o_ref.shape, F32)
    extra = jnp.zeros((1, LANE), F32)
    for k, t in enumerate((t0, t1, t2, t3)):
        there = start + back(y, k) * 2 * LANE
        there = there if backward else there + 2 * LANE - 1
        value = t[...].astype(F32)
        total += same(doc_at(info, c, there), whole) * value
        extra += extra_of(value)
    put_packed(o_ref, total, extra)


def enter_body(backward, info, keep, recv, t1, t2, t3, s0, s1, s2, s3, mine_ref, send_ref):
    x, y, c = info[2, 0], info[2, 1], info[2, 2]
    base = block_start(info, c=0)
    here = doc_at(info, c, base + 2 * LANE - 1 if backward else base)
    total = jnp.zeros(keep.shape, F32)
    extra = extra_of(s0)
    for k, (t, s) in enumerate(((t1, s1), (t2, s2), (t3, s3)), 1):
        there_y, there_x = back(y, k), back(x, k)
        at_y = block_start(info, y=there_y, c=0)
        at_x = block_start(info, x=there_x, y=0, c=0)
        if backward:
            use_y = same(doc_at(info, c, at_y), here) * (there_y > y).astype(F32)
            use_x = same(doc_at(info, c, at_x), here) * (there_x > x).astype(F32)
        else:
            use_y = same(doc_at(info, c, at_y + 2 * LANE - 1), here) * (there_y < y).astype(F32)
            use_x = same(doc_at(info, c, at_x + 8 * LANE - 1), here) * (there_x < x).astype(F32)
        total += use_y * t[...].astype(F32) + use_x * s[...].astype(F32)
        extra += extra_of(s)
    is_zero = jnp.where(c == 0, 1.0, 0.0)
    if backward:
        one = is_zero * recv[...].astype(F32) + (1.0 - is_zero) * keep[...].astype(F32)
        last = doc_at(info, c, base + LANE - 1)
        for_zero = same(doc_at(info, c, base + LANE), last) * one + same(here, last) * total
        for_one = total
    else:
        zero = is_zero * keep[...].astype(F32) + (1.0 - is_zero) * recv[...].astype(F32)
        begun = doc_at(info, c, base + LANE)
        for_zero = total
        for_one = same(doc_at(info, c, base + LANE - 1), begun) * zero + same(here, begun) * total
    put_packed(mine_ref, is_zero * for_zero + (1.0 - is_zero) * for_one, extra)
    put_packed(send_ref, is_zero * for_one + (1.0 - is_zero) * for_zero, extra)


def shift(value, axis, k, name):
    n = 2 if axis == "c" else 4
    with jax.named_scope(name):
        return lax.ppermute(value, axis, [(i, (i + k) % n) for i in range(n)])


def around(value, axis, name):
    return [value] + [shift(value, axis, k, name) for k in (1, 2, 3)]


def to_near(value, name):
    with jax.named_scope(name):
        return lax.ppermute(value, "z", [(0, 1), (1, 0), (2, 3), (3, 2)])


def to_far(value, name):
    with jax.named_scope(name):
        return lax.ppermute(value, "z", [(0, 3), (3, 0), (1, 2), (2, 1)])


def ordered(name, info, parts, axis, after=()):
    return call(
        name + "_order", lambda *refs: order_body("xy".index(axis), *refs),
        [out((4, *parts[0].shape), parts[0].dtype)], info, *parts, kinds="s", after=after,
    )


def to_slots(parts, name, axis="z", way=-1):
    return [parts[0]] + [shift(parts[k], axis, way * k, name) for k in (1, 2, 3)]


def chip_state(info, keep, send, backward):
    tag = "back_" if backward else ""
    recv = shift(send, "c", 1, tag + "cores")
    chip, token = call(
        tag + "chip", lambda *refs: chip_body(backward, *refs), [out((SROWS, LANE), BF16)],
        info, keep, recv, kinds="s", token=True,
    )
    return recv, chip, token


def line_and_sum_body(backward, info, t0, t1, t2, t3, far_ref, got_ref, o_ref, sum_ref):
    line_body(backward, info, t0, t1, t2, t3, o_ref)
    far_body(far_ref, got_ref, sum_ref)


def scan_states(info, chip, backward, after, extra=(), through=()):
    tag = "back_" if backward else ""
    body = line_and_sum_body if extra else line_body
    outs = [out((SROWS, LANE), BF16)] + [out(a.shape, a.dtype) for a in extra[:1]]
    t = around(chip, "y", tag + "scan_y")
    line, *more = call(
        tag + "line", lambda *refs: body(backward, *refs), outs,
        info, *t, *extra, kinds="s", after=after, through=through,
    )
    s = around(line, "x", tag + "scan_x")
    return t, line, s, *more


def scan_end(info, keep, recv, t, s, backward, after=()):
    packed, tag = out((SROWS, LANE), BF16), "back_" if backward else ""
    mine, other = call(
        tag + "enter", lambda *refs: enter_body(backward, *refs), [packed, packed],
        info, keep, recv, *t[1:], *s, kinds="s", after=after,
    )
    return mine, shift(other, "c", 1, tag + "given")


def entered(info, row, mine, other):
    return jnp.where(info[2, 2] == row, mine[...], other[...])


def pairs(info, row):
    at_i, at_j = positions(info, 0), positions(info, 1)
    doc_i, doc_j = doc_of(info, row, at_i), doc_of(info, row, at_j)
    return (doc_i == doc_j) & (at_i >= at_j)


def carried(info, row):
    doc_i = doc_of(info, row, positions(info, 0))
    return (doc_i == doc_at(info, row, block_start(info))).astype(F32)


def by_head(q):
    lanes = lax.broadcasted_iota(jnp.int32, q.shape, 1) // FDIM
    return jnp.concatenate([jnp.where(lanes == h, q, jnp.zeros_like(q)) for h in range(HH)], 0)


def columns(parts, fill):
    lanes = lax.broadcasted_iota(jnp.int32, (parts[0].shape[0], 8), 1)
    total = jnp.full((parts[0].shape[0], 8), fill, F32)
    for h, part in enumerate(parts):
        total = jnp.where(lanes == h, part, total)
    return total


def mix_here_body(info, p_ref, num_ref, den_ref, phi_ref):
    table = picks()
    p = p_ref[...]
    for row in range(2):
        line = row_of(p, row)
        q, k, v = line[:, :HF], line[:, HF : 2 * HF], line[:, 2 * HF :]
        ok = pairs(info, row)
        s = dot_nt(by_head(q), k) * 0.25
        here = slice(row * LANE, (row + 1) * LANE)
        dens = []
        for h in range(HH):
            cols = slice(h * LANE, (h + 1) * LANE)
            sh = s[cols]
            kap = jnp.where(ok, 1.0 + sh + 0.5 * sh * sh, 0.0)
            dens.append(jnp.sum(kap, -1, keepdims=True))
            num_ref[here, cols] = dot(kap.astype(BF16), v[:, cols])
        den_ref[here, :] = columns(dens, 1.0)
        fa, fb = factors(q, table)
        phi_ref[here, :] = (fa * fb * (table[4] * carried(info, row))).astype(BF16)


def assemble_body(axis, info, *refs):
    for copy in assemble(axis, info, refs[:8], refs[8], refs[9]):
        copy.wait()


def mix_body(
    info, num_ref, den_ref, phi_ref, mine, other, wo, mixed_ref, all_den_ref, b0, b1, b2, b3
):
    for row in range(2):
        here = slice(row * LANE, (row + 1) * LANE)
        state, high, low = unpack_state(entered(info, row, mine, other))
        phi = phi_ref[here, :]
        num = num_ref[here, :] + dot(phi, state)
        den = den_ref[here, :] + dot_nt(phi, high) + dot_nt(phi, low)
        attn = [num[:, h * LANE : (h + 1) * LANE] / den[:, h : h + 1] for h in range(HH)]
        put_row(mixed_ref, row, jnp.concatenate(attn, 1).astype(BF16))
        all_den_ref[here, :] = den
    branch = dot_nt(mixed_ref[...], wo[...])
    for s, b in enumerate((b0, b1, b2, b3)):
        b[...] = branch[64 * s : 64 * s + 64].astype(BF16)


def unmix_state_body(
    info, den_ref, phi_ref, mixed_ref, m0, m1, m2, m3, wo,
    dnum_ref, dden_ref, keep_ref, send_ref, mk_ref, ms_ref, dm, turn_ref,
):
    turn_body(info, m0, m1, m2, m3, mk_ref, ms_ref, turn_ref)
    for s, m in enumerate((m0, m1, m2, m3)):
        dm[64 * s : 64 * s + 64, :] = m[...]
    lanes = lax.broadcasted_iota(jnp.int32, (256, 8), 1)
    total = jnp.sum(jnp.where(lanes < HH, den_ref[...], 0.0), keepdims=True)
    total = jnp.broadcast_to(total, (1, LANE))
    mixed = mixed_ref[...]
    lane = lax.broadcasted_iota(jnp.int32, (1, FT), 1)
    head = sum((lane >= FW * h).astype(jnp.int32) for h in range(1, HH))
    heads = lax.broadcasted_iota(jnp.int32, (8, FT), 0)
    core = info[2, 2]
    d_attn = dot(dm[...], wo[...])
    for row in range(2):
        here = slice(row * LANE, (row + 1) * LANE)
        da, at, den = row_of(d_attn, row), row_of(mixed, row).astype(F32), den_ref[here, :]
        dnums, ddens = [], []
        for h in range(HH):
            cols = slice(h * LANE, (h + 1) * LANE)
            dnum = da[:, cols] / den[:, h : h + 1]
            ddens.append(-jnp.sum(dnum * at[:, cols], -1, keepdims=True))
            dnums.append(dnum)
        dnum = jnp.concatenate(dnums, 1).astype(BF16)
        dden = columns(ddens, 0.0)
        dnum_ref[here, :] = dnum
        dden_ref[here, :] = dden
        phi = phi_ref[here, :]
        dcount = jnp.where(head == heads, dot_tn(dden.astype(BF16), phi), 0.0)
        extra = jnp.where(core == row, 0.0, 1.0) * total
        packed = pack_state(dot_tn(phi, dnum), jnp.sum(dcount, 0, keepdims=True), extra)
        split_rows(info, row, packed, keep_ref, send_ref)


def unmix_here_body(
    info, p_ref, dnum_ref, dden_ref, mine, other, mk, mr, mixed, mixed_other,
    dp_ref, own_ref, on_ref, back_ref, a_ref, b_ref, full,
):
    ring_body(info, mk, mr, mixed, mixed_other, own_ref, on_ref, back_ref, a_ref, b_ref, full)
    table = picks()
    p = p_ref[...]
    for row in range(2):
        here = slice(row * LANE, (row + 1) * LANE)
        line = row_of(p, row)
        q, k, v = line[:, :HF], line[:, HF : 2 * HF], line[:, 2 * HF :]
        ok = pairs(info, row)
        q4 = by_head(q)
        s = dot_nt(q4, k) * 0.25
        dnum, dden = dnum_ref[here, :], dden_ref[here, :]
        gs, dvs = [], []
        for h in range(HH):
            cols = slice(h * LANE, (h + 1) * LANE)
            sh = s[cols]
            kap = jnp.where(ok, 1.0 + sh + 0.5 * sh * sh, 0.0)
            g = (dot_nt(dnum[:, cols], v[:, cols]) + dden[:, h : h + 1]) * (1.0 + sh) * 0.25
            gs.append(jnp.where(ok, g, 0.0).astype(BF16))
            dvs.append(dot_tn(kap.astype(BF16), dnum[:, cols]))
        g4 = jnp.concatenate(gs, 0)
        dk = dot_tn(g4, q4)
        dq4 = dot(g4, k)
        lanes = lax.broadcasted_iota(jnp.int32, (LANE, HF), 1) // FDIM
        dq = jnp.zeros((LANE, HF), F32)
        for h in range(HH):
            dq += jnp.where(lanes == h, dq4[h * LANE : (h + 1) * LANE], 0.0)
        state, high, low = unpack_state(entered(info, row, mine, other))
        dden_low = dden.astype(BF16)
        dphi = dot_nt(dnum, state) + dot(dden_low, high) + dot(dden_low, low)
        fa, fb = factors(q, table)
        dq += back_to(dphi * (table[4] * carried(info, row)), fa, fb, table)
        put_row(dp_ref, row, jnp.concatenate([dq, dk, *dvs], 1))


def unproject_body(info, p_ref, dp_ref, mine, other, r_ref, *refs):
    blocks, (gp_ref, near_ref, keep_ref, far_ref, low_ref, w_ref, sems) = refs[:8], refs[8:]
    copies = assemble(1, info, blocks, w_ref, sems)
    p, dp = p_ref[...], dp_ref[...]
    table = picks()
    for row in range(2):
        line, dline = row_of(p, row), row_of(dp, row)
        k, v = line[:, HF : 2 * HF], line[:, 2 * HF :]
        tail_doc = doc_at(info, row, block_start(info) + LANE - 1)
        tail = (doc_of(info, row, positions(info, 0)) == tail_doc).astype(F32)
        fa, fb = factors(k, table)
        state, high, low = unpack_state(entered(info, row, mine, other))
        ones = jnp.ones((LANE, 8), BF16)
        dphi = (dot_nt(v, state) + dot(ones, high) + dot(ones, low)) * tail
        dk = dline[:, HF : 2 * HF] + back_to(dphi, fa, fb, table)
        dv = dline[:, 2 * HF :] + dot((fa * fb * tail).astype(BF16), state)
        put_row(low_ref, row, jnp.concatenate([dline[:, :HF], dk, dv], 1).astype(BF16))
    d = low_ref[...]
    gp_ref[...] = (d.astype(F32) * r_ref[...]).astype(BF16)
    e = dot_nt(d, assembled(copies, w_ref)).astype(BF16)
    halve(info, e, slice(0, e.shape[1]), near_ref, keep_ref, far_ref)


def middle_body(x_ref, a, b, c, d, middle_ref, low_ref):
    u = x_ref[:64, :].astype(F32)
    for part in (a, b, c, d):
        u += part[...].astype(F32)
    middle_ref[...] = u
    low_ref[...] = (u * lax.rsqrt(jnp.mean(u * u, -1, keepdims=True) + EPS)).astype(BF16)


def norm_back(base_ref, u_ref, parts, low_ref):
    u, e = u_ref[:64, :].astype(F32), summed(parts)
    r = lax.rsqrt(jnp.mean(u * u, -1, keepdims=True) + EPS)
    slope = jnp.mean(e * u, -1, keepdims=True)
    total = base_ref[:64, :].astype(F32) + r * e - u * (r * r * r * slope)
    low_ref[...] = total.astype(BF16)


def norm_back_body(base_ref, u_ref, a, b, c, d, low_ref):
    norm_back(base_ref, u_ref, (a, b, c, d), low_ref)


def last_body(
    base_ref, x_ref, e_keep, e_got, e_far, middle_ref, keep_ref, got_ref, far_ref, o_ref
):
    norm_back(base_ref, x_ref, (e_keep, e_got.at[:64], e_far), o_ref.at[:64])
    o_ref[64:, :] = (middle_ref[...] + summed((keep_ref, got_ref.at[:64], far_ref))).astype(BF16)


def place_body(info, a, b, c, d, grad_ref, out_ref):
    for k, part in enumerate((a, b, c, d)):
        at = pl.multiple_of(32 * back(info[2, 3], k), 32)
        for row in range(2):
            grad_ref[row, pl.ds(at, 32), :] = part[32 * row : 32 * row + 32, :]
            out_ref[row, pl.ds(at, 32), :] = part[64 + 32 * row : 96 + 32 * row, :]


def rows_in(bulk, first, width, w, sems, parts):
    step = w.shape[0] // parts
    copies = [
        pltpu.make_async_copy(
            bulk.at[pl.ds(step * k, step), pl.ds(first, width)],
            w.at[pl.ds(step * k, step), :],
            sems.at[k],
        )
        for k in range(parts)
    ]
    for copy in copies:
        copy.start()
    return copies


def d_hidden_body(dy_hbm, bulk, o_ref, w, dy_ref, sems, dy_sem):
    units = w.shape[1]
    parts = sems.shape[0]
    step = w.shape[0] // parts
    dy_copy = pltpu.make_async_copy(dy_hbm, dy_ref, dy_sem)
    dy_copy.start()
    copies = rows_in(bulk, 2 * units, units, w, sems, parts)
    dy_copy.wait()
    for k, copy in enumerate(copies):
        copy.wait()
        here = slice(step * k, step * (k + 1))
        part = dot(dy_ref[:, here], w[here, :])
        if k == 0:
            o_ref[...] = part
        else:
            o_ref[...] += part


def ffn_body(
    info, u0, u1, u2, u3, dh_ref, bulk,
    a_ref, keep_ref, e0, e1, e2, e3, u, w, pre, t, sems,
):
    core = info[2, 2]
    pair = 2 * LANE
    groups = w.shape[1] // pair
    hid_at, turn_at = w.shape[1], w.shape[1] + w.shape[1] // 2
    parts = sems.shape[0]
    step = w.shape[0] // parts
    copies = rows_in(bulk, 0, w.shape[1], w, sems, parts)
    for s, part in enumerate((u0, u1, u2, u3)):
        u[64 * s : 64 * s + 64, :] = part[...]
    for k, copy in enumerate(copies):
        copy.wait()
        here = slice(step * k, step * (k + 1))
        part = dot(u[:, here], w[here, :])
        if k == 0:
            pre[...] = part
        else:
            pre[...] += part
    for b in range(groups):
        units = slice(b * LANE, (b + 1) * LANE)
        gate = pre[:, b * pair : b * pair + LANE]
        up = pre[:, b * pair + LANE : (b + 1) * pair]
        d_hidden = dh_ref[:, units]
        sigma = 1.0 / (1.0 + jnp.exp(-gate))
        silu = gate * sigma
        a_ref[:, hid_at + b * LANE : hid_at + (b + 1) * LANE] = (silu * up).astype(BF16)
        d_gate = d_hidden * up * (sigma + silu * (1.0 - sigma))
        a_ref[:, b * pair : b * pair + LANE] = d_gate.astype(BF16)
        a_ref[:, b * pair + LANE : (b + 1) * pair] = (d_hidden * silu).astype(BF16)
    for n in range(w.shape[0] // pair):
        here = slice(n * pair, (n + 1) * pair)
        e = dot_nt(a_ref[:, :hid_at], w[here, :]).astype(BF16)
        for s, ref in enumerate((e0, e1, e2, e3)):
            ref[:, here] = e[64 * s : 64 * s + 64]
        t[...] = u[:, here].astype(F32).T
        for i in range(pair // LANE):
            at = slice(n * LANE + 64 * i, n * LANE + 64 * i + 64)
            mine = pl.ds(pl.multiple_of(LANE * i + 64 * core, 64), 64)
            other = pl.ds(pl.multiple_of(LANE * i + 64 - 64 * core, 64), 64)
            keep_ref[at, :] = t[mine, :].astype(BF16)
            row = n % 2 * LANE + 64 * i
            lanes = slice(turn_at + n // 2 * 256, turn_at + n // 2 * 256 + 256)
            a_ref[row : row + 64, lanes] = t[other, :].astype(BF16)


def halve(info, value, here, near_ref, keep_ref, far_ref):
    even = info[2, 3] % 2 == 0
    one, three = value[64:128], value[192:]
    keep_ref[:, here] = value[:64]
    near_ref[:64, here] = jnp.where(even, three, one)
    near_ref[64:, here] = value[128:192]
    far_ref[:, here] = jnp.where(even, one, three)


def down_body(info, a_ref, bulk, near_ref, keep_ref, far_ref, w, sems):
    units = w.shape[1]
    parts = sems.shape[0]
    step = w.shape[0] // parts
    for k, copy in enumerate(rows_in(bulk, 2 * units, units, w, sems, parts)):
        copy.wait()
        here = slice(step * k, step * (k + 1))
        f = dot_nt(a_ref[:, 2 * units : 3 * units], w[here, :]).astype(BF16)
        halve(info, f, here, near_ref, keep_ref, far_ref)


def far_body(far_ref, got_ref, o_ref):
    o_ref[...] = (far_ref[...].astype(F32) + got_ref[64:, :].astype(F32)).astype(BF16)


def ffn_grad_body(uk, yk, yr, a_own, a_other, o_ref, lhs):
    step = pl.program_id(0)
    rows, units = lhs.shape[0], o_ref.shape[1]

    def product(at):
        both = jnp.concatenate([a_own[:, at : at + units], a_other[:, at : at + units]], 0)
        for m in range(rows // 256):
            here = slice(256 * m, 256 * (m + 1))
            o_ref[here, :] = dot(lhs[here, :], both).astype(BF16)

    @pl.when(step == 0)
    def _():
        lhs[:, :256] = uk[...]
        for m in range(rows // 256):
            at = 3 * units + 256 * m
            lhs[256 * m : 256 * (m + 1), 256:] = a_other[:, at : at + 256]
        product(0)

    @pl.when(step == 1)
    def _():
        product(units)

    @pl.when(step == 2)
    def _():
        lhs[:, :256] = yk[...]
        lhs[:, 256:] = yr[...]
        product(2 * units)


def ffn_grads(uk, yk, yr, a_own, a_other, units):
    rows, tokens = uk.shape
    with jax.named_scope("ffn_grad"):
        return pl.pallas_call(
            ffn_grad_body,
            grid=(3,),
            out_shape=pltpu.HBM((rows, 3 * units), BF16),
            in_specs=[pl.BlockSpec(memory_space=pltpu.VMEM)] * 5,
            out_specs=pl.BlockSpec((rows, units), lambda b: (0, b)),
            scratch_shapes=[pltpu.VMEM((rows, 2 * tokens), BF16)],
            compiler_params=pltpu.CompilerParams(vmem_limit_bytes=20 * 2**20),
            cost_estimate=pl.CostEstimate(
                flops=12 * rows * tokens * units, bytes_accessed=6 * rows * units, transcendentals=0
            ),
        )(uk, yk, yr, a_own, a_other)


def fold_body(info, *refs):
    ins, outs, results = refs[:3], refs[3:6], refs[6:]
    for k, o in enumerate(results):
        there = (info[2, 0] + k) % 4
        sides = [sum(part[there].astype(F32) for part in parts) for parts in (ins, outs)]
        o[...] = jnp.concatenate(sides, 1).astype(BF16)


def ring_body(info, lk, lr, own, other, own_ref, on_ref, back_ref, a_ref, b_ref, full):
    full[...] = (dot(lk[...], own[...]) + dot(lr[...], other[...])).astype(BF16)
    for k, o in ((0, own_ref), (1, on_ref), (3, back_ref), (2, None)):
        there = (info[2, 1] + k) % 4
        for i in range(4):
            rows = full[pl.ds(pl.multiple_of((i * 4 + there) * 64, 64), 64), :]
            if o is not None:
                o[i] = rows
            elif i < 2:
                a_ref[i] = rows
            else:
                b_ref[i - 2] = rows


def ring_add_body(on_ref, back_ref, a_ref, b_ref, on_out, back_out):
    on_out[...] = on_ref[...]
    back_out[...] = back_ref[...]
    on_out[:2] = (on_ref[:2].astype(F32) + a_ref[...].astype(F32)).astype(BF16)
    back_out[2:] = (back_ref[2:].astype(F32) + b_ref[...].astype(F32)).astype(BF16)


def ring_sum(name, info, lk, lr, own, other, after=()):
    n = own.shape[1]
    part, half = out((4, 64, n), BF16), out((2, 64, n), BF16)
    mine, on, before, a, b = call(
        name, ring_body, [part, part, part, half, half], info, lk, lr, own, other, kinds="s",
        scratch=[pltpu.VMEM((lk.shape[0], n), BF16)], flops=4 * lk.shape[0] * lk.shape[1] * n,
    )
    return ring_rest(name, mine, on, before, a, b, after)


def ring_rest(name, mine, on, before, a, b, after=()):
    got_a, got_b = shift(a, "y", 1, name + "_far"), shift(b, "y", -1, name + "_far")
    part = out(on.shape, BF16)
    on, before = call(
        name + "_add", ring_add_body, [part, part], on, before, got_a, got_b, after=after
    )
    return [mine, shift(on, "y", 1, name + "_near"), shift(before, "y", -1, name + "_near")]


def summed(parts):
    return sum(part[...].astype(F32) for part in parts)


def row_sums(value):
    total = jnp.broadcast_to(jnp.sum(value, 1, keepdims=True), (64, LANE))
    wide = jnp.concatenate([total, jnp.zeros((64, LANE), F32)], 0)
    return wide.T[0:1]


def finish_ffn_body(s_ref, wg_ref, wu_ref, g_ref, gate_ref, up_ref, down_ref, gain_ref):
    units = gate_ref.shape[1]
    g = column(g_ref[...])
    groups = s_ref.shape[1] // (3 * LANE)

    def side(k):
        at = [(2 * b + k) * LANE for b in range(groups)]
        return jnp.concatenate([s_ref[:, i : i + LANE] for i in at], 1)[:, :units].astype(F32)

    gate, up = side(0), side(1)
    gain = row_sums(gate * wg_ref[...].astype(F32) + up * wu_ref[...].astype(F32))
    gain_ref[...] = jnp.broadcast_to(gain, gain_ref.shape)
    gate_ref[...] = gate * g
    up_ref[...] = up * g
    down_ref[...] = s_ref[:, 2 * groups * LANE : 2 * groups * LANE + units].astype(F32)


def totals_body(a, b, c, d, one_ref, two_ref, den_ref):
    total = summed((a, b, c, d))
    one_ref[...] = total[0:1, :64]
    two_ref[...] = total[1:2, :64]
    den_ref[...] = total[2:3, :1]


def finish_mix_body(
    s0, s1, s2, s3, wq_ref, wk_ref, wv_ref, g_ref, gain2_ref, den0, den1,
    q_ref, k_ref, v_ref, out_ref, message_ref,
):
    g = column(g_ref[...])
    total = summed((s0, s1, s2, s3))
    cols = total.shape[1] - out_ref.shape[1]
    grads = total[:, :cols]
    out_ref[...] = total[:, cols:]
    w = jnp.concatenate([wq_ref[...], wk_ref[...], wv_ref[...]], 1).astype(F32)
    rows = lax.broadcasted_iota(jnp.int32, (8, LANE), 0)
    den = extra_of(den0) + extra_of(den1)
    message = jnp.where(rows == 0, row_sums(grads * w), 0.0)
    message = jnp.where(rows == 1, gain2_ref[0:1, :], message)
    message_ref[...] = jnp.where(rows == 2, den, message)
    scaled = grads * g
    q_ref[...] = scaled[:, :HF]
    k_ref[...] = scaled[:, HF : 2 * HF]
    v_ref[...] = scaled[:, 2 * HF :]


def on_device(
    tokens,
    doc_lengths,
    norm_gain,
    w_query,
    w_key,
    w_value,
    w_out,
    ffn_gain,
    w_gate,
    w_up,
    w_down,
    out_grad,
):
    x, y, c, z = (lax.axis_index(a) for a in ("x", "y", "c", "z"))
    ends = jnp.cumsum(doc_lengths, -1).astype(jnp.int32)
    places = jnp.stack([x, y, c, z, x, x, x, x]).astype(jnp.int32)
    info = jnp.concatenate([ends, places[None]], 0)
    d = tokens.shape[-1]
    width = w_out.shape[0]
    units = -(-w_gate.shape[1] // LANE) * LANE
    cols = 2 * HF + w_value.shape[1]
    piece = out((64, d), BF16)
    piece_full = out((64, d), F32)
    state = out((SROWS, LANE), BF16)

    early, early_out = call(
        "early", early_body, [out((64, cols), BF16), out((64, width), BF16)],
        norm_gain[None], w_query, w_key, w_value, w_out.T, kinds="ddddd",
    )
    out_ys = around(early_out, "y", "out_y")
    (line,) = ordered("in_x", info, around(early, "x", "in_x"), "x", out_ys[1:3])
    w_in = around(line, "y", "in_y")
    (out_line,) = ordered("out_y", info, out_ys, "y", [line])
    w_mix = around(out_line, "x", "out_x")
    x_all, xk, x_send, x_token = slotted(info, tokens)
    dy_all, yk, y_send, y_token = slotted(info, out_grad)
    xr, yr = shift(x_send, "c", 1, "x_cores"), shift(y_send, "c", 1, "y_cores")
    (bulk_own,) = call(
        "bulk", bulk_body, [out((64, 3 * units), BF16)],
        ffn_gain[None], w_gate, w_up, w_down.T, kinds="dddd", after=[*w_in[1:], *w_mix[1:], x_token, y_token],
    )
    bulk = lax.all_gather(bulk_own, BLK, axis=0, tiled=True)
    w_in += [shift(g, "c", 1, "in_cores") for g in w_in]
    w_mix += [shift(g, "c", 1, "out_cores") for g in w_mix]


    p, r, keep, send = call(
        "project", project_body,
        [out((256, cols), BF16), out((256, 1), F32), state, state],
        info, x_all, *w_in, kinds="sv" + "a" * 8, after=[xr, yr],
        scratch=[pltpu.VMEM((4, 4, 2, 64, cols), BF16), pltpu.SemaphoreType.DMA((8,))],
        flops=2 * 256 * d * cols, limit=20,
    )
    num_here, den_here, phi, here_token = call(
        "mix_here", mix_here_body,
        [out((256, width), F32), out((256, 8), F32), out((256, FT), BF16)],
        info, p, kinds="s", token=True, flops=2 * 256 * d * 64,
    )
    recv, chip, _ = chip_state(info, keep, send, False)
    t, _, s = scan_states(info, chip, False, [here_token])
    w_mix_all, w_token = call(
        "assemble", lambda *refs: assemble_body(0, *refs), [out((4, 4, 2, 64, width), BF16)],
        info, *w_mix, kinds="s" + "a" * 8, scratch=[pltpu.SemaphoreType.DMA((8,))], token=True,
    )
    w_mix_all = w_mix_all.reshape(d, width)
    mine, other = scan_end(info, keep, recv, t, s, False, [w_token])
    mixed, den, *branch = call(
        "mix", mix_body,
        [out((256, width), BF16), out((256, 8), F32)] + [piece] * 4,
        info, num_here, den_here, phi, mine, other, w_mix_all, kinds="s",
        flops=2 * 256 * d * width, limit=16,
    )
    (d_hidden,) = call(
        "d_hidden", d_hidden_body, [out((256, units), F32)], dy_all, bulk, kinds="hh",
        scratch=[
            pltpu.VMEM((d, units), BF16), pltpu.VMEM((256, d), BF16),
            pltpu.SemaphoreType.DMA((4,)), pltpu.SemaphoreType.DMA,
        ],
        flops=2 * 256 * d * units, limit=16,
    )
    middle, u2 = call("middle", middle_body, [piece_full, piece], x_all, *to_slots(branch, "branch_sum"))
    us = around(u2, "z", "u_all")
    mixed_other = shift(mixed, "c", 1, "mixed_cores")
    half = out((d // 2, 256), BF16)
    a_own, uk, *e_parts = call(
        "ffn", ffn_body,
        [out((256, 3 * units + d // 2), BF16), half] + [piece] * 4,
        info, *us, d_hidden, bulk, kinds="svvvvvh", after=[mixed_other],
        scratch=[
            pltpu.VMEM((256, d), BF16), pltpu.VMEM((d, 2 * units), BF16),
            pltpu.VMEM((256, 2 * units), F32), pltpu.VMEM((2 * LANE, 256), F32),
            pltpu.SemaphoreType.DMA((4,)),
        ],
        flops=8 * 256 * d * units, limit=36,
    )
    a_other = shift(a_own, "c", 1, "a_cores")
    ffn_rows = ffn_grads(uk, yk, yr, a_own, a_other, units)
    dm, ffn_rows = call(
        "norm_back", norm_back_body, [piece],
        dy_all, middle, *to_slots(e_parts, "e_sum"), through=[ffn_rows],
    )
    ffn_sum = lax.psum_scatter(ffn_rows, ("x", "y"), scatter_dimension=0, tiled=True)
    f_near, f_keep, f_far, f_token = call(
        "down", down_body, [out((128, d), BF16), piece, piece], info, a_own, bulk, kinds="svh", token=True,
        scratch=[pltpu.VMEM((d, units), BF16), pltpu.SemaphoreType.DMA((8,))],
        flops=2 * 256 * d * units, limit=16,
    )
    dms = around(dm, "z", "dm_all")
    dnum, dden, dkeep, dsend, mk, m_send = call(
        "unmix_state", unmix_state_body,
        [out((256, width), BF16), out((256, 8), F32), state, state, half, half],
        info, den, phi, mixed, *dms, w_mix_all, kinds="s", after=[f_token],
        scratch=[pltpu.VMEM((256, d), BF16), pltpu.VMEM((d, 256), F32)],
        flops=2 * 256 * d * width, limit=20,
    )
    drecv, dchip, dtoken = chip_state(info, dkeep, dsend, True)
    mr = shift(m_send, "c", 1, "m_cores")
    dp, *out_ring, unmix_token = call(
        "unmix_here", unmix_here_body,
        [out((256, cols), F32)] + [out((4, 64, width), BF16)] * 3 + [out((2, 64, width), BF16)] * 2,
        info, p, dnum, dden, mine, other, mk, mr, mixed, mixed_other, kinds="s", after=[dtoken],
        token=True,
        scratch=[pltpu.VMEM((d // 2, width), BF16)], flops=2 * 256 * d * 640,
    )
    f_got = to_near(f_near, "f_near")
    dt, _, ds, f_send = scan_states(info, dchip, True, [unmix_token], (f_far, f_got))
    f_last = to_far(f_send, "f_far")
    out_first = ring_rest("out", *out_ring)
    dmine, dother = scan_end(info, dkeep, drecv, dt, ds, True)

    gp, e_near, e_keep, e_far = call(
        "unproject", unproject_body,
        [out((256, cols), BF16), out((128, d), BF16), piece, piece],
        info, p, dp, dmine, dother, r, *w_in, kinds="svvvvv" + "a" * 8, after=[*out_first[1:]],
        scratch=[
            pltpu.VMEM((256, cols), BF16), pltpu.VMEM((4, 4, 2, 64, cols), BF16),
            pltpu.SemaphoreType.DMA((8,)),
        ],
        flops=2 * 256 * d * cols, limit=16,
    )
    e_got = to_near(e_near, "e_near")
    e_send, e_token = call("e_mid", far_body, [piece], e_far, e_got, token=True)
    in_first = ring_sum("in_grad", info, xk, xr, gp, shift(gp, "c", 1, "gp_cores"), [e_token])
    (last,) = call(
        "last", last_body, [out((128, d), BF16)],
        dm, x_all, e_keep, e_got, to_far(e_send, "e_far"), middle, f_keep, f_got, f_last,
    )
    input_grad, block_out = call(
        "place", place_body, [out(tokens.shape, BF16)] * 2,
        info, *around(last, "z", "last_all"), kinds="s",
    )
    sums = call(
        "fold", fold_body, [out((64, cols + width), BF16)] * 4,
        info, *in_first, *out_first, kinds="s",
    )
    g_gate, g_up, g_down, gain2 = call(
        "finish_ffn", finish_ffn_body,
        [out(w_gate.shape, F32), out(w_up.shape, F32), out(w_down.shape[::-1], F32),
         out((8, LANE), F32)],
        ffn_sum, w_gate, w_up, ffn_gain[None], kinds="dddd",
    )
    g_q, g_k, g_v, g_out, message = call(
        "finish_mix", finish_mix_body,
        [out(w_query.shape, F32), out(w_key.shape, F32), out(w_value.shape, F32),
         out(w_out.shape[::-1], F32), out((8, LANE), F32)],
        *to_slots(sums, "second", "x", 1),
        w_query, w_key, w_value, norm_gain[None], gain2, dmine, dother,
        kinds="vvvvdddd",
    )
    gain_one, gain_two, denom = call(
        "totals", totals_body, [out((1, 64), F32), out((1, 64), F32), out((1, 1), F32)],
        *around(message, "z", "message"),
    )
    seq = 32 * LANE
    denom_mean = denom.reshape(()) / (2 * seq * HEADS * seq)
    return (
        block_out, input_grad, gain_one.reshape(64), g_q, g_k, g_v, g_out.T, gain_two.reshape(64),
        g_gate, g_up, g_down.T, denom_mean,
    )


def solution(mesh):
    finer = Mesh(mesh.devices.reshape(4, 4, 2, mesh.shape["head"]), ("x", "y", "c", "z"))
    placed = (
        P(None, BLK, None),
        P(),
        P(BLK),
        P(BLK, "z"),
        P(BLK, "z"),
        P(BLK, "z"),
        P("z", BLK),
        P(BLK),
        P(BLK, "z"),
        P(BLK, "z"),
        P("z", BLK),
        P(None, BLK, None),
    )
    return jax.shard_map(
        on_device,
        mesh=finer,
        in_specs=placed,
        out_specs=(
            P(None, BLK, None),
            P(None, BLK, None),
            P(BLK),
            P(BLK, "z"),
            P(BLK, "z"),
            P(BLK, "z"),
            P("z", BLK),
            P(BLK),
            P(BLK, "z"),
            P(BLK, "z"),
            P("z", BLK),
            P(),
        ),
        check_vma=False,
    )
```

```python
import math

import jax
import jax.numpy as jnp
from jax import lax
from jax.experimental import pallas as pl
from jax.experimental.pallas import tpu as pltpu
from jax.sharding import Mesh
from jax.sharding import PartitionSpec as P

HEADS = 16
FDIM = 16
EPS = 1e-05
BLK = ("x", "y", "c")
F32 = jnp.float32
BF16 = jnp.bfloat16

HH = 4
HF = HH * FDIM
FW = 160
FT = HH * FW
SROWS = FT + 16
LANE = 128
DOCS = 8


def dot(a, b):
    return jnp.dot(a, b, preferred_element_type=F32)


def dot_nt(a, b):
    return lax.dot_general(a, b, (((1,), (1,)), ((), ())), preferred_element_type=F32)


def dot_tn(a, b):
    return lax.dot_general(a, b, (((0,), (0,)), ((), ())), preferred_element_type=F32)


def out(shape, dtype):
    return jax.ShapeDtypeStruct(tuple(shape), dtype)


SPACES = {"s": pltpu.SMEM, "v": pltpu.VMEM, "h": pltpu.HBM, "d": pltpu.HBM, "a": pl.ANY}


def in_hbm(value):
    return pltpu.with_memory_space_constraint(value, pltpu.HBM)


def call(
    name, body, outs, *args, kinds="", after=(), through=(), scratch=(), flops=0, limit=12, token=False
):
    if token:
        first, outs = len(args) + len(outs), [*outs, out((8, LANE), F32)]
        inside = body

        def body(*refs):
            refs[first][...] = jnp.zeros((8, LANE), F32)
            inside(*refs[:first], *refs[first + 1 :])

    kinds = kinds + "v" * (len(args) - len(kinds))
    n_args, n_extra, n_out = len(args), len(after) + len(through), len(outs)
    staged = [k for k in range(n_args) if kinds[k] == "d"]
    places = [pltpu.VMEM(args[k].shape, args[k].dtype) for k in staged]
    if staged:
        places.append(pltpu.SemaphoreType.DMA((len(staged),)))

    def inner(*refs):
        given, results = list(refs[:n_args]), refs[n_args + n_extra :]
        own = results[n_out + len(through) :]
        held, own = own[: len(places)], own[len(places) :]
        copies = [
            pltpu.make_async_copy(given[k], held[i], held[-1].at[i]) for i, k in enumerate(staged)
        ]
        for copy in copies:
            copy.start()
        for copy in copies:
            copy.wait()
        for i, k in enumerate(staged):
            given[k] = held[i]
        body(*given, *results[:n_out], *own)

    moved = sum(math.prod(a.shape) * a.dtype.itemsize for a in (*args, *outs))
    args = [in_hbm(a) if k in "hd" else a for a, k in zip(args, kinds)]
    through = [in_hbm(a) if a.size > 2**21 else a for a in through]
    with jax.named_scope(name):
        return pl.pallas_call(
            inner,
            out_shape=list(outs) + [out(t.shape, t.dtype) for t in through],
            in_specs=[pl.BlockSpec(memory_space=SPACES[k]) for k in kinds + "a" * n_extra],
            out_specs=[pl.BlockSpec(memory_space=SPACES[k]) for k in "v" * n_out + "a" * len(through)],
            scratch_shapes=[*places, *scratch],
            input_output_aliases={
                n_args + len(after) + k: n_out + k for k in range(len(through))
            },
            compiler_params=pltpu.CompilerParams(vmem_limit_bytes=limit * 2**20),
            cost_estimate=pl.CostEstimate(flops=flops, bytes_accessed=moved, transcendentals=0),
        )(*args, *after, *through)


def doc_at(info, row, position):
    total = jnp.int32(0)
    for k in range(DOCS):
        total += (info[row, k] <= position).astype(jnp.int32)
    return total


def doc_of(info, row, where):
    total = jnp.zeros(where.shape, jnp.int32)
    for k in range(DOCS):
        total += (info[row, k] <= where).astype(jnp.int32)
    return total


def same(a, b):
    return (a == b).astype(F32)


def block_start(info, x=None, y=None, c=None):
    x = info[2, 0] if x is None else x
    y = info[2, 1] if y is None else y
    c = info[2, 2] if c is None else c
    return ((x * 4 + y) * 2 + c) * LANE


def back(place, k):
    return (place - k + 4) % 4


def positions(info, dim):
    shape = (LANE, 1) if dim == 0 else (1, LANE)
    t = lax.broadcasted_iota(jnp.int32, shape, dim)
    slot, inside = t // 32, t % 32
    return block_start(info) + 32 * ((info[2, 3] - slot + 4) % 4) + inside


def row_of(value, row):
    return jnp.concatenate([value[64 * s + 32 * row : 64 * s + 32 * row + 32] for s in range(4)], 0)


def put_row(ref, row, value):
    for s in range(4):
        ref[64 * s + 32 * row : 64 * s + 32 * row + 32, :] = value[32 * s : 32 * s + 32]


def diagonal(g):
    n = g.shape[-1]
    rows = lax.broadcasted_iota(jnp.int32, (n, n), 0)
    cols = lax.broadcasted_iota(jnp.int32, (n, n), 1)
    return jnp.where(rows == cols, jnp.broadcast_to(g.astype(F32), (n, n)), 0.0).astype(BF16)


def column(g):
    return jnp.sum(diagonal(g).astype(F32), 1, keepdims=True)


def early_body(g_ref, q_ref, k_ref, v_ref, wo_ref, o_ref, out_ref):
    d = diagonal(g_ref[...])
    qk = jnp.concatenate([q_ref[...], k_ref[...]], 1)
    o_ref[:, :LANE] = dot(d, qk).astype(BF16)
    o_ref[:, LANE:] = dot(d, v_ref[...]).astype(BF16)
    out_ref[...] = wo_ref[...]


def bulk_body(g_ref, wg_ref, wu_ref, wd_ref, o_ref):
    d = diagonal(g_ref[...])
    units = wg_ref.shape[1]
    groups = -(-units // LANE)
    fill = jnp.zeros((wg_ref.shape[0], groups * LANE - units), BF16)
    gate = jnp.concatenate([dot(d, wg_ref[...]).astype(BF16), fill], 1)
    up = jnp.concatenate([dot(d, wu_ref[...]).astype(BF16), fill], 1)
    for b in range(groups):
        here = slice(b * LANE, (b + 1) * LANE)
        o_ref[:, 2 * b * LANE : (2 * b + 1) * LANE] = gate[:, here]
        o_ref[:, (2 * b + 1) * LANE : (2 * b + 2) * LANE] = up[:, here]
    o_ref[:, 2 * groups * LANE : 3 * groups * LANE] = jnp.concatenate([wd_ref[...], fill], 1)


def turn(info, t, keep_ref, send_ref):
    core = info[2, 2]
    for i in range(t.shape[0] // LANE):
        here = pl.multiple_of(LANE * i + 64 * core, 64)
        there = pl.multiple_of(LANE * i + 64 - 64 * core, 64)
        keep_ref[64 * i : 64 * i + 64, :] = t[pl.ds(here, 64), :].astype(BF16)
        send_ref[64 * i : 64 * i + 64, :] = t[pl.ds(there, 64), :].astype(BF16)


def order_body(axis, info, a, b, c, d, o_ref):
    for k, part in enumerate((a, b, c, d)):
        o_ref[back(info[2, axis], k)] = part[...]


def slot_body(info, value_ref, all_ref, keep_ref, send_ref, t):
    for k in range(4):
        at = pl.multiple_of(32 * back(info[2, 3], k), 32)
        for row in range(2):
            here = slice(64 * k + 32 * row, 64 * k + 32 * row + 32)
            all_ref[here, :] = value_ref[row, pl.ds(at, 32), :]
        t[:, 64 * k : 64 * k + 64] = all_ref[64 * k : 64 * k + 64, :].astype(F32).T
    turn(info, t, keep_ref, send_ref)


def turn_body(info, a, b, c, d, keep_ref, send_ref, t):
    for k, part in enumerate((a, b, c, d)):
        t[:, 64 * k : 64 * k + 64] = part[...].astype(F32).T
    turn(info, t, keep_ref, send_ref)


def slotted(info, value):
    d = value.shape[-1]
    half = out((d // 2, 256), BF16)
    return call(
        "slot", slot_body, [out((256, d), BF16), half, half], info, value, kinds="s", token=True,
        scratch=[pltpu.VMEM((d, 256), F32)],
    )


def picks():
    lane = lax.broadcasted_iota(jnp.int32, (1, FT), 1)
    head = sum((lane >= FW * h).astype(jnp.int32) for h in range(1, HH))
    e = lane - FW * head
    n = FDIM + 1
    s = sum((e >= n * m).astype(jnp.int32) for m in range(1, 9))
    a = e - n * s
    b = a + s
    b = jnp.where(b >= n, b - n, b)
    used = e < 9 * n
    rows = lax.broadcasted_iota(jnp.int32, (HF, FT), 0)

    def matrix(i):
        at = jnp.where(used & (i < FDIM), FDIM * head + i, -1)
        return jnp.where(rows == at, 1.0, 0.0).astype(BF16)

    one_a = jnp.where(used & (a == FDIM), 1.0, 0.0)
    one_b = jnp.where(used & (b == FDIM), 1.0, 0.0)
    plain = jnp.where(a == b, 1.0 / 32, 1.0 / 16)
    weight = jnp.where(one_a + one_b == 2.0, 1.0, jnp.where(one_a + one_b == 1.0, 0.25, plain))
    return matrix(a), matrix(b), one_a, one_b, weight


def factors(u, table):
    pick_a, pick_b, one_a, one_b, _ = table
    return dot(u, pick_a) + one_a, dot(u, pick_b) + one_b


def back_to(dphi, fa, fb, table):
    return dot_nt((dphi * fb).astype(BF16), table[0]) + dot_nt((dphi * fa).astype(BF16), table[1])


def pack_state(state, count, extra=None):
    parts = [
        state[h * FW : (h + 1) * FW, h * LANE : (h + 1) * LANE].astype(BF16) for h in range(HH)
    ]
    high = count.astype(BF16).astype(F32)
    low = count - high
    rows = lax.broadcasted_iota(jnp.int32, (16, LANE), 0)
    tile = jnp.zeros((16, LANE), F32)
    for j in range(FT // LANE):
        tile = jnp.where(rows == j, high[:, j * LANE : (j + 1) * LANE], tile)
        tile = jnp.where(rows == j + 5, low[:, j * LANE : (j + 1) * LANE], tile)
    if extra is not None:
        tile = with_extra(tile, extra)
    return jnp.concatenate([*parts, tile.astype(BF16)], 0)


def with_extra(tile, extra):
    rows = lax.broadcasted_iota(jnp.int32, (16, LANE), 0)
    high = extra.astype(BF16).astype(F32)
    tile = jnp.where(rows == 10, high, tile)
    return jnp.where(rows == 11, extra - high, tile)


def extra_of(packed):
    tile = packed[FT:SROWS].astype(F32)
    return tile[10:11] + tile[11:12]


def put_packed(ref, total, extra):
    ref[:FT, :] = total[:FT].astype(BF16)
    ref[FT:, :] = with_extra(total[FT:], extra).astype(BF16)


def unpack_state(packed):
    blocks = []
    for h in range(HH):
        mine = packed[h * FW : (h + 1) * FW]
        zero = jnp.zeros_like(mine)
        blocks.append(jnp.concatenate([mine if g == h else zero for g in range(HH)], 1))
    state = jnp.concatenate(blocks, 0)
    tile = packed[FT:].astype(F32)
    lane = lax.broadcasted_iota(jnp.int32, (1, FT), 1)
    head = sum((lane >= FW * h).astype(jnp.int32) for h in range(1, HH))
    heads = lax.broadcasted_iota(jnp.int32, (8, FT), 0)
    counts = []
    for first in (0, 5):
        line = jnp.concatenate([tile[first + j : first + j + 1] for j in range(5)], 1)
        counts.append(jnp.where(head == heads, jnp.broadcast_to(line, (8, FT)), 0.0).astype(BF16))
    return state, counts[0], counts[1]


def split_rows(info, row, packed, keep_ref, send_ref):
    @pl.when(info[2, 2] == row)
    def _():
        keep_ref[...] = packed

    @pl.when(info[2, 2] != row)
    def _():
        send_ref[...] = packed


def assemble(axis, info, blocks, w_ref, sems):
    core = info[2, 2]
    copies = []
    for k in range(4):
        there = back(info[2, axis], k)
        for i, owner in enumerate((core, 1 - core)):
            target = w_ref.at[there, :, owner] if axis == 0 else w_ref.at[:, there, owner]
            copies.append(pltpu.make_async_copy(blocks[4 * i + k], target, sems.at[len(copies)]))
            copies[-1].start()
    return copies


def assembled(copies, w_ref):
    for copy in copies:
        copy.wait()
    return w_ref[...].reshape(-1, w_ref.shape[-1])


def project_body(info, x_ref, *refs):
    blocks, (p_ref, r_ref, keep_ref, send_ref, w_ref, sems) = refs[:8], refs[8:]
    copies = assemble(1, info, blocks, w_ref, sems)
    x = x_ref[...]
    xf = x.astype(F32)
    r = lax.rsqrt(jnp.mean(xf * xf, -1, keepdims=True) + EPS)
    r_ref[...] = r
    table = picks()
    p = (dot(x, assembled(copies, w_ref)) * r).astype(BF16)
    p_ref[...] = p
    for row in range(2):
        mine = row_of(p, row)
        k, v = mine[:, HF : 2 * HF], mine[:, 2 * HF :]
        tail_doc = doc_at(info, row, block_start(info) + LANE - 1)
        tail = (doc_of(info, row, positions(info, 0)) == tail_doc).astype(F32)
        fa, fb = factors(k, table)
        phi = (fa * fb * tail).astype(BF16)
        count = dot(jnp.ones((8, LANE), BF16), phi)[0:1]
        split_rows(info, row, pack_state(dot_tn(phi, v), count), keep_ref, send_ref)


def chip_body(backward, info, keep_ref, recv_ref, o_ref):
    c = info[2, 2]
    base = block_start(info, c=0)
    keep, recv = keep_ref[...].astype(F32), recv_ref[...].astype(F32)
    is_zero = jnp.where(c == 0, 1.0, 0.0)
    zero = is_zero * keep + (1.0 - is_zero) * recv
    one = is_zero * recv + (1.0 - is_zero) * keep
    if backward:
        total = zero + same(doc_at(info, c, base), doc_at(info, c, base + LANE)) * one
    else:
        last, end = doc_at(info, c, base + LANE - 1), doc_at(info, c, base + 2 * LANE - 1)
        total = one + same(last, end) * zero
    put_packed(o_ref, total, extra_of(keep) + extra_of(recv))


def line_body(backward, info, t0, t1, t2, t3, o_ref):
    c, y = info[2, 2], info[2, 1]
    start = block_start(info, y=0, c=0)
    whole = doc_at(info, c, start if backward else start + 8 * LANE - 1)
    total = jnp.zeros(o_ref.shape, F32)
    extra = jnp.zeros((1, LANE), F32)
    for k, t in enumerate((t0, t1, t2, t3)):
        there = start + back(y, k) * 2 * LANE
        there = there if backward else there + 2 * LANE - 1
        value = t[...].astype(F32)
        total += same(doc_at(info, c, there), whole) * value
        extra += extra_of(value)
    put_packed(o_ref, total, extra)


def enter_body(backward, info, keep, recv, t1, t2, t3, s0, s1, s2, s3, mine_ref, send_ref):
    x, y, c = info[2, 0], info[2, 1], info[2, 2]
    base = block_start(info, c=0)
    here = doc_at(info, c, base + 2 * LANE - 1 if backward else base)
    total = jnp.zeros(keep.shape, F32)
    extra = extra_of(s0)
    for k, (t, s) in enumerate(((t1, s1), (t2, s2), (t3, s3)), 1):
        there_y, there_x = back(y, k), back(x, k)
        at_y = block_start(info, y=there_y, c=0)
        at_x = block_start(info, x=there_x, y=0, c=0)
        if backward:
            use_y = same(doc_at(info, c, at_y), here) * (there_y > y).astype(F32)
            use_x = same(doc_at(info, c, at_x), here) * (there_x > x).astype(F32)
        else:
            use_y = same(doc_at(info, c, at_y + 2 * LANE - 1), here) * (there_y < y).astype(F32)
            use_x = same(doc_at(info, c, at_x + 8 * LANE - 1), here) * (there_x < x).astype(F32)
        total += use_y * t[...].astype(F32) + use_x * s[...].astype(F32)
        extra += extra_of(s)
    is_zero = jnp.where(c == 0, 1.0, 0.0)
    if backward:
        one = is_zero * recv[...].astype(F32) + (1.0 - is_zero) * keep[...].astype(F32)
        last = doc_at(info, c, base + LANE - 1)
        for_zero = same(doc_at(info, c, base + LANE), last) * one + same(here, last) * total
        for_one = total
    else:
        zero = is_zero * keep[...].astype(F32) + (1.0 - is_zero) * recv[...].astype(F32)
        begun = doc_at(info, c, base + LANE)
        for_zero = total
        for_one = same(doc_at(info, c, base + LANE - 1), begun) * zero + same(here, begun) * total
    put_packed(mine_ref, is_zero * for_zero + (1.0 - is_zero) * for_one, extra)
    put_packed(send_ref, is_zero * for_one + (1.0 - is_zero) * for_zero, extra)


def shift(value, axis, k, name):
    n = 2 if axis == "c" else 4
    with jax.named_scope(name):
        return lax.ppermute(value, axis, [(i, (i + k) % n) for i in range(n)])


def around(value, axis, name):
    return [value] + [shift(value, axis, k, name) for k in (1, 2, 3)]


def to_near(value, name):
    with jax.named_scope(name):
        return lax.ppermute(value, "z", [(0, 1), (1, 0), (2, 3), (3, 2)])


def to_far(value, name):
    with jax.named_scope(name):
        return lax.ppermute(value, "z", [(0, 3), (3, 0), (1, 2), (2, 1)])


def ordered(name, info, parts, axis, after=()):
    return call(
        name + "_order", lambda *refs: order_body("xy".index(axis), *refs),
        [out((4, *parts[0].shape), parts[0].dtype)], info, *parts, kinds="s", after=after,
    )


def to_slots(parts, name, axis="z", way=-1):
    return [parts[0]] + [shift(parts[k], axis, way * k, name) for k in (1, 2, 3)]


def chip_state(info, keep, send, backward):
    tag = "back_" if backward else ""
    recv = shift(send, "c", 1, tag + "cores")
    chip, token = call(
        tag + "chip", lambda *refs: chip_body(backward, *refs), [out((SROWS, LANE), BF16)],
        info, keep, recv, kinds="s", token=True,
    )
    return recv, chip, token


def line_and_sum_body(backward, info, t0, t1, t2, t3, far_ref, got_ref, o_ref, sum_ref):
    line_body(backward, info, t0, t1, t2, t3, o_ref)
    far_body(far_ref, got_ref, sum_ref)


def scan_states(info, chip, backward, after, extra=(), through=()):
    tag = "back_" if backward else ""
    body = line_and_sum_body if extra else line_body
    outs = [out((SROWS, LANE), BF16)] + [out(a.shape, a.dtype) for a in extra[:1]]
    t = around(chip, "y", tag + "scan_y")
    line, *more = call(
        tag + "line", lambda *refs: body(backward, *refs), outs,
        info, *t, *extra, kinds="s", after=after, through=through,
    )
    s = around(line, "x", tag + "scan_x")
    return t, line, s, *more


def scan_end(info, keep, recv, t, s, backward, after=()):
    packed, tag = out((SROWS, LANE), BF16), "back_" if backward else ""
    mine, other = call(
        tag + "enter", lambda *refs: enter_body(backward, *refs), [packed, packed],
        info, keep, recv, *t[1:], *s, kinds="s", after=after,
    )
    return mine, shift(other, "c", 1, tag + "given")


def entered(info, row, mine, other):
    return jnp.where(info[2, 2] == row, mine[...], other[...])


def pairs(info, row):
    at_i, at_j = positions(info, 0), positions(info, 1)
    doc_i, doc_j = doc_of(info, row, at_i), doc_of(info, row, at_j)
    return (doc_i == doc_j) & (at_i >= at_j)


def carried(info, row):
    doc_i = doc_of(info, row, positions(info, 0))
    return (doc_i == doc_at(info, row, block_start(info))).astype(F32)


def by_head(q):
    lanes = lax.broadcasted_iota(jnp.int32, q.shape, 1) // FDIM
    return jnp.concatenate([jnp.where(lanes == h, q, jnp.zeros_like(q)) for h in range(HH)], 0)


def columns(parts, fill):
    lanes = lax.broadcasted_iota(jnp.int32, (parts[0].shape[0], 8), 1)
    total = jnp.full((parts[0].shape[0], 8), fill, F32)
    for h, part in enumerate(parts):
        total = jnp.where(lanes == h, part, total)
    return total


def mix_here_body(info, p_ref, num_ref, den_ref, phi_ref):
    table = picks()
    p = p_ref[...]
    for row in range(2):
        line = row_of(p, row)
        q, k, v = line[:, :HF], line[:, HF : 2 * HF], line[:, 2 * HF :]
        ok = pairs(info, row)
        s = dot_nt(by_head(q), k) * 0.25
        here = slice(row * LANE, (row + 1) * LANE)
        dens = []
        for h in range(HH):
            cols = slice(h * LANE, (h + 1) * LANE)
            sh = s[cols]
            kap = jnp.where(ok, 1.0 + sh + 0.5 * sh * sh, 0.0)
            dens.append(jnp.sum(kap, -1, keepdims=True))
            num_ref[here, cols] = dot(kap.astype(BF16), v[:, cols])
        den_ref[here, :] = columns(dens, 1.0)
        fa, fb = factors(q, table)
        phi_ref[here, :] = (fa * fb * (table[4] * carried(info, row))).astype(BF16)


def assemble_body(axis, info, *refs):
    for copy in assemble(axis, info, refs[:8], refs[8], refs[9]):
        copy.wait()


def mix_body(
    info, num_ref, den_ref, phi_ref, mine, other, wo, mixed_ref, all_den_ref, b0, b1, b2, b3
):
    for row in range(2):
        here = slice(row * LANE, (row + 1) * LANE)
        state, high, low = unpack_state(entered(info, row, mine, other))
        phi = phi_ref[here, :]
        num = num_ref[here, :] + dot(phi, state)
        den = den_ref[here, :] + dot_nt(phi, high) + dot_nt(phi, low)
        attn = [num[:, h * LANE : (h + 1) * LANE] / den[:, h : h + 1] for h in range(HH)]
        put_row(mixed_ref, row, jnp.concatenate(attn, 1).astype(BF16))
        all_den_ref[here, :] = den
    branch = dot_nt(mixed_ref[...], wo[...])
    for s, b in enumerate((b0, b1, b2, b3)):
        b[...] = branch[64 * s : 64 * s + 64].astype(BF16)


def unmix_state_body(
    info, den_ref, phi_ref, mixed_ref, m0, m1, m2, m3, wo,
    dnum_ref, dden_ref, keep_ref, send_ref, mk_ref, ms_ref, dm, turn_ref,
):
    turn_body(info, m0, m1, m2, m3, mk_ref, ms_ref, turn_ref)
    for s, m in enumerate((m0, m1, m2, m3)):
        dm[64 * s : 64 * s + 64, :] = m[...]
    lanes = lax.broadcasted_iota(jnp.int32, (256, 8), 1)
    total = jnp.sum(jnp.where(lanes < HH, den_ref[...], 0.0), keepdims=True)
    total = jnp.broadcast_to(total, (1, LANE))
    mixed = mixed_ref[...]
    lane = lax.broadcasted_iota(jnp.int32, (1, FT), 1)
    head = sum((lane >= FW * h).astype(jnp.int32) for h in range(1, HH))
    heads = lax.broadcasted_iota(jnp.int32, (8, FT), 0)
    core = info[2, 2]
    d_attn = dot(dm[...], wo[...])
    for row in range(2):
        here = slice(row * LANE, (row + 1) * LANE)
        da, at, den = row_of(d_attn, row), row_of(mixed, row).astype(F32), den_ref[here, :]
        dnums, ddens = [], []
        for h in range(HH):
            cols = slice(h * LANE, (h + 1) * LANE)
            dnum = da[:, cols] / den[:, h : h + 1]
            ddens.append(-jnp.sum(dnum * at[:, cols], -1, keepdims=True))
            dnums.append(dnum)
        dnum = jnp.concatenate(dnums, 1).astype(BF16)
        dden = columns(ddens, 0.0)
        dnum_ref[here, :] = dnum
        dden_ref[here, :] = dden
        phi = phi_ref[here, :]
        dcount = jnp.where(head == heads, dot_tn(dden.astype(BF16), phi), 0.0)
        extra = jnp.where(core == row, 0.0, 1.0) * total
        packed = pack_state(dot_tn(phi, dnum), jnp.sum(dcount, 0, keepdims=True), extra)
        split_rows(info, row, packed, keep_ref, send_ref)


def unmix_here_body(
    info, p_ref, dnum_ref, dden_ref, mine, other, mk, mr, mixed, mixed_other,
    dp_ref, own_ref, on_ref, back_ref, a_ref, b_ref, full,
):
    ring_body(info, mk, mr, mixed, mixed_other, own_ref, on_ref, back_ref, a_ref, b_ref, full)
    table = picks()
    p = p_ref[...]
    for row in range(2):
        here = slice(row * LANE, (row + 1) * LANE)
        line = row_of(p, row)
        q, k, v = line[:, :HF], line[:, HF : 2 * HF], line[:, 2 * HF :]
        ok = pairs(info, row)
        q4 = by_head(q)
        s = dot_nt(q4, k) * 0.25
        dnum, dden = dnum_ref[here, :], dden_ref[here, :]
        gs, dvs = [], []
        for h in range(HH):
            cols = slice(h * LANE, (h + 1) * LANE)
            sh = s[cols]
            kap = jnp.where(ok, 1.0 + sh + 0.5 * sh * sh, 0.0)
            g = (dot_nt(dnum[:, cols], v[:, cols]) + dden[:, h : h + 1]) * (1.0 + sh) * 0.25
            gs.append(jnp.where(ok, g, 0.0).astype(BF16))
            dvs.append(dot_tn(kap.astype(BF16), dnum[:, cols]))
        g4 = jnp.concatenate(gs, 0)
        dk = dot_tn(g4, q4)
        dq4 = dot(g4, k)
        lanes = lax.broadcasted_iota(jnp.int32, (LANE, HF), 1) // FDIM
        dq = jnp.zeros((LANE, HF), F32)
        for h in range(HH):
            dq += jnp.where(lanes == h, dq4[h * LANE : (h + 1) * LANE], 0.0)
        state, high, low = unpack_state(entered(info, row, mine, other))
        dden_low = dden.astype(BF16)
        dphi = dot_nt(dnum, state) + dot(dden_low, high) + dot(dden_low, low)
        fa, fb = factors(q, table)
        dq += back_to(dphi * (table[4] * carried(info, row)), fa, fb, table)
        put_row(dp_ref, row, jnp.concatenate([dq, dk, *dvs], 1))


def unproject_body(info, p_ref, dp_ref, mine, other, r_ref, *refs):
    blocks, (gp_ref, near_ref, keep_ref, far_ref, low_ref, w_ref, sems) = refs[:8], refs[8:]
    copies = assemble(1, info, blocks, w_ref, sems)
    p, dp = p_ref[...], dp_ref[...]
    table = picks()
    for row in range(2):
        line, dline = row_of(p, row), row_of(dp, row)
        k, v = line[:, HF : 2 * HF], line[:, 2 * HF :]
        tail_doc = doc_at(info, row, block_start(info) + LANE - 1)
        tail = (doc_of(info, row, positions(info, 0)) == tail_doc).astype(F32)
        fa, fb = factors(k, table)
        state, high, low = unpack_state(entered(info, row, mine, other))
        ones = jnp.ones((LANE, 8), BF16)
        dphi = (dot_nt(v, state) + dot(ones, high) + dot(ones, low)) * tail
        dk = dline[:, HF : 2 * HF] + back_to(dphi, fa, fb, table)
        dv = dline[:, 2 * HF :] + dot((fa * fb * tail).astype(BF16), state)
        put_row(low_ref, row, jnp.concatenate([dline[:, :HF], dk, dv], 1).astype(BF16))
    d = low_ref[...]
    gp_ref[...] = (d.astype(F32) * r_ref[...]).astype(BF16)
    e = dot_nt(d, assembled(copies, w_ref)).astype(BF16)
    halve(info, e, slice(0, e.shape[1]), near_ref, keep_ref, far_ref)


def middle_body(x_ref, a, b, c, d, middle_ref, low_ref):
    u = x_ref[:64, :].astype(F32)
    for part in (a, b, c, d):
        u += part[...].astype(F32)
    middle_ref[...] = u
    low_ref[...] = (u * lax.rsqrt(jnp.mean(u * u, -1, keepdims=True) + EPS)).astype(BF16)


def norm_back(base_ref, u_ref, parts, low_ref):
    u, e = u_ref[:64, :].astype(F32), summed(parts)
    r = lax.rsqrt(jnp.mean(u * u, -1, keepdims=True) + EPS)
    slope = jnp.mean(e * u, -1, keepdims=True)
    total = base_ref[:64, :].astype(F32) + r * e - u * (r * r * r * slope)
    low_ref[...] = total.astype(BF16)


def norm_back_body(base_ref, u_ref, a, b, c, d, low_ref):
    norm_back(base_ref, u_ref, (a, b, c, d), low_ref)


def last_body(
    base_ref, x_ref, e_keep, e_got, e_far, middle_ref, keep_ref, got_ref, far_ref, o_ref
):
    norm_back(base_ref, x_ref, (e_keep, e_got.at[:64], e_far), o_ref.at[:64])
    o_ref[64:, :] = (middle_ref[...] + summed((keep_ref, got_ref.at[:64], far_ref))).astype(BF16)


def place_body(info, a, b, c, d, grad_ref, out_ref):
    for k, part in enumerate((a, b, c, d)):
        at = pl.multiple_of(32 * back(info[2, 3], k), 32)
        for row in range(2):
            grad_ref[row, pl.ds(at, 32), :] = part[32 * row : 32 * row + 32, :]
            out_ref[row, pl.ds(at, 32), :] = part[64 + 32 * row : 96 + 32 * row, :]


def rows_in(bulk, first, width, w, sems, parts):
    step = w.shape[0] // parts
    copies = [
        pltpu.make_async_copy(
            bulk.at[pl.ds(step * k, step), pl.ds(first, width)],
            w.at[pl.ds(step * k, step), :],
            sems.at[k],
        )
        for k in range(parts)
    ]
    for copy in copies:
        copy.start()
    return copies


def d_hidden_body(dy_hbm, bulk, o_ref, w, dy_ref, sems, dy_sem):
    units = w.shape[1]
    parts = sems.shape[0]
    step = w.shape[0] // parts
    dy_copy = pltpu.make_async_copy(dy_hbm, dy_ref, dy_sem)
    dy_copy.start()
    copies = rows_in(bulk, 2 * units, units, w, sems, parts)
    dy_copy.wait()
    for k, copy in enumerate(copies):
        copy.wait()
        here = slice(step * k, step * (k + 1))
        part = dot(dy_ref[:, here], w[here, :])
        if k == 0:
            o_ref[...] = part
        else:
            o_ref[...] += part


def ffn_body(
    info, u0, u1, u2, u3, dh_ref, bulk,
    a_ref, keep_ref, e0, e1, e2, e3, u, w, pre, t, sems,
):
    core = info[2, 2]
    pair = 2 * LANE
    groups = w.shape[1] // pair
    hid_at, turn_at = w.shape[1], w.shape[1] + w.shape[1] // 2
    parts = sems.shape[0]
    step = w.shape[0] // parts
    copies = rows_in(bulk, 0, w.shape[1], w, sems, parts)
    for s, part in enumerate((u0, u1, u2, u3)):
        u[64 * s : 64 * s + 64, :] = part[...]
    for k, copy in enumerate(copies):
        copy.wait()
        here = slice(step * k, step * (k + 1))
        part = dot(u[:, here], w[here, :])
        if k == 0:
            pre[...] = part
        else:
            pre[...] += part
    for b in range(groups):
        units = slice(b * LANE, (b + 1) * LANE)
        gate = pre[:, b * pair : b * pair + LANE]
        up = pre[:, b * pair + LANE : (b + 1) * pair]
        d_hidden = dh_ref[:, units]
        sigma = 1.0 / (1.0 + jnp.exp(-gate))
        silu = gate * sigma
        a_ref[:, hid_at + b * LANE : hid_at + (b + 1) * LANE] = (silu * up).astype(BF16)
        d_gate = d_hidden * up * (sigma + silu * (1.0 - sigma))
        a_ref[:, b * pair : b * pair + LANE] = d_gate.astype(BF16)
        a_ref[:, b * pair + LANE : (b + 1) * pair] = (d_hidden * silu).astype(BF16)
    for n in range(w.shape[0] // pair):
        here = slice(n * pair, (n + 1) * pair)
        e = dot_nt(a_ref[:, :hid_at], w[here, :]).astype(BF16)
        for s, ref in enumerate((e0, e1, e2, e3)):
            ref[:, here] = e[64 * s : 64 * s + 64]
        t[...] = u[:, here].astype(F32).T
        for i in range(pair // LANE):
            at = slice(n * LANE + 64 * i, n * LANE + 64 * i + 64)
            mine = pl.ds(pl.multiple_of(LANE * i + 64 * core, 64), 64)
            other = pl.ds(pl.multiple_of(LANE * i + 64 - 64 * core, 64), 64)
            keep_ref[at, :] = t[mine, :].astype(BF16)
            row = n % 2 * LANE + 64 * i
            lanes = slice(turn_at + n // 2 * 256, turn_at + n // 2 * 256 + 256)
            a_ref[row : row + 64, lanes] = t[other, :].astype(BF16)


def halve(info, value, here, near_ref, keep_ref, far_ref):
    even = info[2, 3] % 2 == 0
    one, three = value[64:128], value[192:]
    keep_ref[:, here] = value[:64]
    near_ref[:64, here] = jnp.where(even, three, one)
    near_ref[64:, here] = value[128:192]
    far_ref[:, here] = jnp.where(even, one, three)


def down_body(info, a_ref, bulk, near_ref, keep_ref, far_ref, w, sems):
    units = w.shape[1]
    parts = sems.shape[0]
    step = w.shape[0] // parts
    for k, copy in enumerate(rows_in(bulk, 2 * units, units, w, sems, parts)):
        copy.wait()
        here = slice(step * k, step * (k + 1))
        f = dot_nt(a_ref[:, 2 * units : 3 * units], w[here, :]).astype(BF16)
        halve(info, f, here, near_ref, keep_ref, far_ref)


def far_body(far_ref, got_ref, o_ref):
    o_ref[...] = (far_ref[...].astype(F32) + got_ref[64:, :].astype(F32)).astype(BF16)


def ffn_grad_body(uk, yk, yr, a_own, a_other, o_ref, lhs):
    step = pl.program_id(0)
    rows, units = lhs.shape[0], o_ref.shape[1]

    def product(at):
        both = jnp.concatenate([a_own[:, at : at + units], a_other[:, at : at + units]], 0)
        for m in range(rows // 256):
            here = slice(256 * m, 256 * (m + 1))
            o_ref[here, :] = dot(lhs[here, :], both).astype(BF16)

    @pl.when(step == 0)
    def _():
        lhs[:, :256] = uk[...]
        for m in range(rows // 256):
            at = 3 * units + 256 * m
            lhs[256 * m : 256 * (m + 1), 256:] = a_other[:, at : at + 256]
        product(0)

    @pl.when(step == 1)
    def _():
        product(units)

    @pl.when(step == 2)
    def _():
        lhs[:, :256] = yk[...]
        lhs[:, 256:] = yr[...]
        product(2 * units)


def ffn_grads(uk, yk, yr, a_own, a_other, units):
    rows, tokens = uk.shape
    with jax.named_scope("ffn_grad"):
        return pl.pallas_call(
            ffn_grad_body,
            grid=(3,),
            out_shape=pltpu.HBM((rows, 3 * units), BF16),
            in_specs=[pl.BlockSpec(memory_space=pltpu.VMEM)] * 5,
            out_specs=pl.BlockSpec((rows, units), lambda b: (0, b)),
            scratch_shapes=[pltpu.VMEM((rows, 2 * tokens), BF16)],
            compiler_params=pltpu.CompilerParams(vmem_limit_bytes=20 * 2**20),
            cost_estimate=pl.CostEstimate(
                flops=12 * rows * tokens * units, bytes_accessed=6 * rows * units, transcendentals=0
            ),
        )(uk, yk, yr, a_own, a_other)


def fold_body(info, *refs):
    ins, outs, results = refs[:3], refs[3:6], refs[6:]
    for k, o in enumerate(results):
        there = (info[2, 0] + k) % 4
        sides = [sum(part[there].astype(F32) for part in parts) for parts in (ins, outs)]
        o[...] = jnp.concatenate(sides, 1).astype(BF16)


def ring_body(info, lk, lr, own, other, own_ref, on_ref, back_ref, a_ref, b_ref, full):
    full[...] = (dot(lk[...], own[...]) + dot(lr[...], other[...])).astype(BF16)
    for k, o in ((0, own_ref), (1, on_ref), (3, back_ref), (2, None)):
        there = (info[2, 1] + k) % 4
        for i in range(4):
            rows = full[pl.ds(pl.multiple_of((i * 4 + there) * 64, 64), 64), :]
            if o is not None:
                o[i] = rows
            elif i < 2:
                a_ref[i] = rows
            else:
                b_ref[i - 2] = rows


def ring_add_body(on_ref, back_ref, a_ref, b_ref, on_out, back_out):
    on_out[...] = on_ref[...]
    back_out[...] = back_ref[...]
    on_out[:2] = (on_ref[:2].astype(F32) + a_ref[...].astype(F32)).astype(BF16)
    back_out[2:] = (back_ref[2:].astype(F32) + b_ref[...].astype(F32)).astype(BF16)


def ring_sum(name, info, lk, lr, own, other, after=()):
    n = own.shape[1]
    part, half = out((4, 64, n), BF16), out((2, 64, n), BF16)
    mine, on, before, a, b = call(
        name, ring_body, [part, part, part, half, half], info, lk, lr, own, other, kinds="s",
        scratch=[pltpu.VMEM((lk.shape[0], n), BF16)], flops=4 * lk.shape[0] * lk.shape[1] * n,
    )
    return ring_rest(name, mine, on, before, a, b, after)


def ring_rest(name, mine, on, before, a, b, after=()):
    got_a, got_b = shift(a, "y", 1, name + "_far"), shift(b, "y", -1, name + "_far")
    part = out(on.shape, BF16)
    on, before = call(
        name + "_add", ring_add_body, [part, part], on, before, got_a, got_b, after=after
    )
    return [mine, shift(on, "y", 1, name + "_near"), shift(before, "y", -1, name + "_near")]


def summed(parts):
    return sum(part[...].astype(F32) for part in parts)


def row_sums(value):
    total = jnp.broadcast_to(jnp.sum(value, 1, keepdims=True), (64, LANE))
    wide = jnp.concatenate([total, jnp.zeros((64, LANE), F32)], 0)
    return wide.T[0:1]


def finish_ffn_body(s_ref, wg_ref, wu_ref, g_ref, gate_ref, up_ref, down_ref, gain_ref):
    units = gate_ref.shape[1]
    g = column(g_ref[...])
    groups = s_ref.shape[1] // (3 * LANE)

    def side(k):
        at = [(2 * b + k) * LANE for b in range(groups)]
        return jnp.concatenate([s_ref[:, i : i + LANE] for i in at], 1)[:, :units].astype(F32)

    gate, up = side(0), side(1)
    gain = row_sums(gate * wg_ref[...].astype(F32) + up * wu_ref[...].astype(F32))
    gain_ref[...] = jnp.broadcast_to(gain, gain_ref.shape)
    gate_ref[...] = gate * g
    up_ref[...] = up * g
    down_ref[...] = s_ref[:, 2 * groups * LANE : 2 * groups * LANE + units].astype(F32)


def totals_body(a, b, c, d, one_ref, two_ref, den_ref):
    total = summed((a, b, c, d))
    one_ref[...] = total[0:1, :64]
    two_ref[...] = total[1:2, :64]
    den_ref[...] = total[2:3, :1]


def finish_mix_body(
    s0, s1, s2, s3, wq_ref, wk_ref, wv_ref, g_ref, gain2_ref, den0, den1,
    q_ref, k_ref, v_ref, out_ref, message_ref,
):
    g = column(g_ref[...])
    total = summed((s0, s1, s2, s3))
    cols = total.shape[1] - out_ref.shape[1]
    grads = total[:, :cols]
    out_ref[...] = total[:, cols:]
    w = jnp.concatenate([wq_ref[...], wk_ref[...], wv_ref[...]], 1).astype(F32)
    rows = lax.broadcasted_iota(jnp.int32, (8, LANE), 0)
    den = extra_of(den0) + extra_of(den1)
    message = jnp.where(rows == 0, row_sums(grads * w), 0.0)
    message = jnp.where(rows == 1, gain2_ref[0:1, :], message)
    message_ref[...] = jnp.where(rows == 2, den, message)
    scaled = grads * g
    q_ref[...] = scaled[:, :HF]
    k_ref[...] = scaled[:, HF : 2 * HF]
    v_ref[...] = scaled[:, 2 * HF :]


def on_device(
    tokens,
    doc_lengths,
    norm_gain,
    w_query,
    w_key,
    w_value,
    w_out,
    ffn_gain,
    w_gate,
    w_up,
    w_down,
    out_grad,
):
    x, y, c, z = (lax.axis_index(a) for a in ("x", "y", "c", "z"))
    ends = jnp.cumsum(doc_lengths, -1).astype(jnp.int32)
    places = jnp.stack([x, y, c, z, x, x, x, x]).astype(jnp.int32)
    info = jnp.concatenate([ends, places[None]], 0)
    d = tokens.shape[-1]
    width = w_out.shape[0]
    units = -(-w_gate.shape[1] // LANE) * LANE
    cols = 2 * HF + w_value.shape[1]
    piece = out((64, d), BF16)
    piece_full = out((64, d), F32)
    state = out((SROWS, LANE), BF16)

    early, early_out = call(
        "early", early_body, [out((64, cols), BF16), out((64, width), BF16)],
        norm_gain[None], w_query, w_key, w_value, w_out.T, kinds="ddddd",
    )
    out_ys = around(early_out, "y", "out_y")
    (line,) = ordered("in_x", info, around(early, "x", "in_x"), "x", out_ys[1:3])
    w_in = around(line, "y", "in_y")
    (out_line,) = ordered("out_y", info, out_ys, "y", [line])
    w_mix = around(out_line, "x", "out_x")
    x_all, xk, x_send, x_token = slotted(info, tokens)
    dy_all, yk, y_send, y_token = slotted(info, out_grad)
    xr, yr = shift(x_send, "c", 1, "x_cores"), shift(y_send, "c", 1, "y_cores")
    (bulk_own,) = call(
        "bulk", bulk_body, [out((64, 3 * units), BF16)],
        ffn_gain[None], w_gate, w_up, w_down.T, kinds="dddd", after=[*w_in[1:], *w_mix[1:], x_token, y_token],
    )
    bulk = lax.all_gather(bulk_own, BLK, axis=0, tiled=True)
    w_in += [shift(g, "c", 1, "in_cores") for g in w_in]
    w_mix += [shift(g, "c", 1, "out_cores") for g in w_mix]


    p, r, keep, send = call(
        "project", project_body,
        [out((256, cols), BF16), out((256, 1), F32), state, state],
        info, x_all, *w_in, kinds="sv" + "a" * 8, after=[xr, yr],
        scratch=[pltpu.VMEM((4, 4, 2, 64, cols), BF16), pltpu.SemaphoreType.DMA((8,))],
        flops=2 * 256 * d * cols, limit=20,
    )
    num_here, den_here, phi, here_token = call(
        "mix_here", mix_here_body,
        [out((256, width), F32), out((256, 8), F32), out((256, FT), BF16)],
        info, p, kinds="s", token=True, flops=2 * 256 * d * 64,
    )
    recv, chip, _ = chip_state(info, keep, send, False)
    t, _, s = scan_states(info, chip, False, [here_token])
    w_mix_all, w_token = call(
        "assemble", lambda *refs: assemble_body(0, *refs), [out((4, 4, 2, 64, width), BF16)],
        info, *w_mix, kinds="s" + "a" * 8, scratch=[pltpu.SemaphoreType.DMA((8,))], token=True,
    )
    w_mix_all = w_mix_all.reshape(d, width)
    mine, other = scan_end(info, keep, recv, t, s, False, [w_token])
    mixed, den, *branch = call(
        "mix", mix_body,
        [out((256, width), BF16), out((256, 8), F32)] + [piece] * 4,
        info, num_here, den_here, phi, mine, other, w_mix_all, kinds="s",
        flops=2 * 256 * d * width, limit=16,
    )
    (d_hidden,) = call(
        "d_hidden", d_hidden_body, [out((256, units), F32)], dy_all, bulk, kinds="hh",
        scratch=[
            pltpu.VMEM((d, units), BF16), pltpu.VMEM((256, d), BF16),
            pltpu.SemaphoreType.DMA((4,)), pltpu.SemaphoreType.DMA,
        ],
        flops=2 * 256 * d * units, limit=16,
    )
    middle, u2 = call("middle", middle_body, [piece_full, piece], x_all, *to_slots(branch, "branch_sum"))
    us = around(u2, "z", "u_all")
    mixed_other = shift(mixed, "c", 1, "mixed_cores")
    half = out((d // 2, 256), BF16)
    a_own, uk, *e_parts = call(
        "ffn", ffn_body,
        [out((256, 3 * units + d // 2), BF16), half] + [piece] * 4,
        info, *us, d_hidden, bulk, kinds="svvvvvh", after=[mixed_other],
        scratch=[
            pltpu.VMEM((256, d), BF16), pltpu.VMEM((d, 2 * units), BF16),
            pltpu.VMEM((256, 2 * units), F32), pltpu.VMEM((2 * LANE, 256), F32),
            pltpu.SemaphoreType.DMA((4,)),
        ],
        flops=8 * 256 * d * units, limit=36,
    )
    a_other = shift(a_own, "c", 1, "a_cores")
    ffn_rows = ffn_grads(uk, yk, yr, a_own, a_other, units)
    dm, ffn_rows = call(
        "norm_back", norm_back_body, [piece],
        dy_all, middle, *to_slots(e_parts, "e_sum"), through=[ffn_rows],
    )
    ffn_sum = lax.psum_scatter(ffn_rows, ("x", "y"), scatter_dimension=0, tiled=True)
    f_near, f_keep, f_far, f_token = call(
        "down", down_body, [out((128, d), BF16), piece, piece], info, a_own, bulk, kinds="svh", token=True,
        scratch=[pltpu.VMEM((d, units), BF16), pltpu.SemaphoreType.DMA((8,))],
        flops=2 * 256 * d * units, limit=16,
    )
    dms = around(dm, "z", "dm_all")
    dnum, dden, dkeep, dsend, mk, m_send = call(
        "unmix_state", unmix_state_body,
        [out((256, width), BF16), out((256, 8), F32), state, state, half, half],
        info, den, phi, mixed, *dms, w_mix_all, kinds="s", after=[f_token],
        scratch=[pltpu.VMEM((256, d), BF16), pltpu.VMEM((d, 256), F32)],
        flops=2 * 256 * d * width, limit=20,
    )
    drecv, dchip, dtoken = chip_state(info, dkeep, dsend, True)
    mr = shift(m_send, "c", 1, "m_cores")
    dp, *out_ring, unmix_token = call(
        "unmix_here", unmix_here_body,
        [out((256, cols), F32)] + [out((4, 64, width), BF16)] * 3 + [out((2, 64, width), BF16)] * 2,
        info, p, dnum, dden, mine, other, mk, mr, mixed, mixed_other, kinds="s", after=[dtoken],
        token=True,
        scratch=[pltpu.VMEM((d // 2, width), BF16)], flops=2 * 256 * d * 640,
    )
    f_got = to_near(f_near, "f_near")
    dt, _, ds, f_send = scan_states(info, dchip, True, [unmix_token], (f_far, f_got))
    f_last = to_far(f_send, "f_far")
    out_first = ring_rest("out", *out_ring)
    dmine, dother = scan_end(info, dkeep, drecv, dt, ds, True)

    gp, e_near, e_keep, e_far = call(
        "unproject", unproject_body,
        [out((256, cols), BF16), out((128, d), BF16), piece, piece],
        info, p, dp, dmine, dother, r, *w_in, kinds="svvvvv" + "a" * 8, after=[*out_first[1:]],
        scratch=[
            pltpu.VMEM((256, cols), BF16), pltpu.VMEM((4, 4, 2, 64, cols), BF16),
            pltpu.SemaphoreType.DMA((8,)),
        ],
        flops=2 * 256 * d * cols, limit=16,
    )
    e_got = to_near(e_near, "e_near")
    e_send, e_token = call("e_mid", far_body, [piece], e_far, e_got, token=True)
    in_first = ring_sum("in_grad", info, xk, xr, gp, shift(gp, "c", 1, "gp_cores"), [e_token])
    (last,) = call(
        "last", last_body, [out((128, d), BF16)],
        dm, x_all, e_keep, e_got, to_far(e_send, "e_far"), middle, f_keep, f_got, f_last,
    )
    input_grad, block_out = call(
        "place", place_body, [out(tokens.shape, BF16)] * 2,
        info, *around(last, "z", "last_all"), kinds="s",
    )
    sums = call(
        "fold", fold_body, [out((64, cols + width), BF16)] * 4,
        info, *in_first, *out_first, kinds="s",
    )
    g_gate, g_up, g_down, gain2 = call(
        "finish_ffn", finish_ffn_body,
        [out(w_gate.shape, F32), out(w_up.shape, F32), out(w_down.shape[::-1], F32),
         out((8, LANE), F32)],
        ffn_sum, w_gate, w_up, ffn_gain[None], kinds="dddd",
    )
    g_q, g_k, g_v, g_out, message = call(
        "finish_mix", finish_mix_body,
        [out(w_query.shape, F32), out(w_key.shape, F32), out(w_value.shape, F32),
         out(w_out.shape[::-1], F32), out((8, LANE), F32)],
        *to_slots(sums, "second", "x", 1),
        w_query, w_key, w_value, norm_gain[None], gain2, dmine, dother,
        kinds="vvvvdddd",
    )
    gain_one, gain_two, denom = call(
        "totals", totals_body, [out((1, 64), F32), out((1, 64), F32), out((1, 1), F32)],
        *around(message, "z", "message"),
    )
    seq = 32 * LANE
    denom_mean = denom.reshape(()) / (2 * seq * HEADS * seq)
    return (
        block_out, input_grad, gain_one.reshape(64), g_q, g_k, g_v, g_out.T, gain_two.reshape(64),
        g_gate, g_up, g_down.T, denom_mean,
    )


def solution(mesh):
    finer = Mesh(mesh.devices.reshape(4, 4, 2, mesh.shape["head"]), ("x", "y", "c", "z"))
    placed = (
        P(None, BLK, None),
        P(),
        P(BLK),
        P(BLK, "z"),
        P(BLK, "z"),
        P(BLK, "z"),
        P("z", BLK),
        P(BLK),
        P(BLK, "z"),
        P(BLK, "z"),
        P("z", BLK),
        P(None, BLK, None),
    )
    return jax.shard_map(
        on_device,
        mesh=finer,
        in_specs=placed,
        out_specs=(
            P(None, BLK, None),
            P(None, BLK, None),
            P(BLK),
            P(BLK, "z"),
            P(BLK, "z"),
            P(BLK, "z"),
            P("z", BLK),
            P(BLK),
            P(BLK, "z"),
            P(BLK, "z"),
            P("z", BLK),
            P(),
        ),
        check_vma=False,
    )
```
